32 devices in a mesh: dp: 4 (over y, x), fsdp: 8 (over z, core).
Axes of the slice: x: 2, y: 2, z: 4, core: 2. Of those that a mesh axis runs over, the one named last changes fastest.
Arguments:
- tokens: bfloat16 [8192, 768], P(('dp', 'fsdp')), may hold values from -6 to 6
- memory: bfloat16 [16384, 768], P(('dp', 'fsdp')), may hold values from -6 to 6
- target_lengths: int32 [32], P(('dp', 'fsdp')), may hold values from 1 to 256, as said below
- memory_lengths: int32 [32], P(('dp', 'fsdp')), may hold values from 128 to 512, as said below
- task_ids: int32 [32], P(('dp', 'fsdp')), may hold values from 0 to 7
- cotangent: bfloat16 [8192, 768], P(('dp', 'fsdp')), may hold values from -6 to 6
- self_qkv: bfloat16 [768, 2304], P('fsdp'), may hold values from -0.21875 to 0.21875
- self_out: bfloat16 [768, 768], P('fsdp'), may hold values from -0.875 to 0.875
- cross_q: bfloat16 [768, 768], P('fsdp'), may hold values from -0.21875 to 0.21875
- cross_kv: bfloat16 [768, 1536], P('fsdp'), may hold values from -0.21875 to 0.21875
- cross_out: bfloat16 [768, 768], P('fsdp'), may hold values from -1.25 to 1.25
- ffn_in: bfloat16 [768, 3072], P('fsdp'), may hold values from -0.21875 to 0.21875
- ffn_out: bfloat16 [3072, 768], P('fsdp'), may hold values from -0.109375 to 0.109375
- task_table: float32 [8, 64], replicated, may hold values from -6 to 6
- hyper_in: float32 [64, 128], replicated, may hold values from -0.75 to 0.75
- hyper_gen: bfloat16 [128, 76032], P(None, 'fsdp'), may hold values from -0.5 to 0.5
Outputs:
- mixed_out: bfloat16 [8192, 768], P(('dp', 'fsdp'))
- token_grad: float32 [8192, 768], P(('dp', 'fsdp'))
- memory_grad: float32 [16384, 768], P(('dp', 'fsdp'))
- grad_self_qkv: float32 [768, 2304], P('fsdp')
- grad_self_out: float32 [768, 768], P('fsdp')
- grad_cross_q: float32 [768, 768], P('fsdp')
- grad_cross_kv: float32 [768, 1536], P('fsdp')
- grad_cross_out: float32 [768, 768], P('fsdp')
- grad_ffn_in: float32 [768, 3072], P('fsdp')
- grad_ffn_out: float32 [3072, 768], P('fsdp')
- grad_task_table: float32 [8, 64], replicated
- grad_hyper_in: float32 [64, 128], replicated
- grad_hyper_gen: float32 [128, 76032], P(None, 'fsdp')
The draws below stay inside these ranges and needn't reach their ends.
Inputs may be any that keep to these rules, and one draw needn't show every extreme that they name: `target_lengths`: sequence s lies in bucket s // 8; bucket b holds lengths from b * 64 + 1 to (b + 1) * 64; some sequence of the last bucket has exactly 256. `memory_lengths`: some sequence has exactly 512.
All inputs are finite; a program needn't handle non-finite values.
Results may differ from the reference program's by a relative error of at most 0.024.
Values may be sent and summed in bfloat16 or wider, within the bound.
No kernel may reach another device: no remote copies, remote signals or barrier semaphores. Data moves between devices by JAX's collectives and lax.ppermute only.
A program may use at most 192 MiB of HBM per device.

```python
import jax
import jax.numpy as jnp
from jax import lax

D = 768
HEADS = 12
HEAD = 64
FF = 3072
ADAPT = 24
EMB = 64
HYPER = 128
TASKS = 8
TOK_DEV = 256
MEM = 512
BUCKETS = 4
SEQS = 32
TOKENS = 8192
MEMS = 16384
GEN = 76032


def draw_target_lengths(key, part):
    key = jax.random.fold_in(key, 7)
    key_values, key_pick = jax.random.split(key)
    positions = jnp.arange(SEQS, dtype=jnp.int32)
    per_bucket = SEQS // BUCKETS
    bucket = positions // per_bucket
    lowest = bucket * TOK_DEV // BUCKETS + 1
    highest = (bucket + 1) * TOK_DEV // BUCKETS
    random_draw = jax.random.randint(key_values, (SEQS,), 0, 1 << 20, dtype=jnp.int32)
    lengths = lowest + random_draw % (highest - lowest + 1)
    chosen = SEQS - per_bucket + jax.random.randint(key_pick, (), 0, per_bucket, dtype=jnp.int32)
    return jnp.where(positions == chosen, TOK_DEV, lengths).astype(jnp.int32)


def draw_memory_lengths(key, part):
    key = jax.random.fold_in(key, 13)
    key_values, key_pick = jax.random.split(key)
    positions = jnp.arange(SEQS, dtype=jnp.int32)
    lengths = jax.random.randint(key_values, (SEQS,), max(MEM // 4, 1), MEM + 1, dtype=jnp.int32)
    chosen = jax.random.randint(key_pick, (), 0, SEQS, dtype=jnp.int32)
    return jnp.where(positions == chosen, MEM, lengths).astype(jnp.int32)


def plant(array, key, smallest, high):
    shape = array.shape
    index_at = [jax.random.randint(jax.random.fold_in(key, axis), (), 0, shape[axis]) for axis in range(len(shape))]
    array = array.at[tuple(index_at)].set(smallest)
    longest = shape.index(max(shape))
    index_at[longest] = (index_at[longest] + 1) % shape[longest]
    return array.at[tuple(index_at)].set(high)


def block_scale(stream_key, extent, cuts, least, high):
    gain = 1.0
    for position, shards_of in cuts:
        heights = jax.random.uniform(jax.random.fold_in(jax.random.fold_in(stream_key, 6), position), (shards_of,), jnp.float32, least / len(cuts), high / len(cuts))
        gain = gain * jnp.repeat(jnp.exp(heights), extent[position] // shards_of).reshape((-1,) + (1,) * (len(extent) - 1 - position))
    return gain


def scatter_about(key, shape, deviation, most, cuts=(), kind=jnp.bfloat16):
    level = block_scale(key, shape, cuts, -0.22, 0.18) if cuts else 1.0
    values = jax.random.normal(key, shape, jnp.float32) * deviation * level
    return jnp.minimum(jnp.maximum(values, -most), most).astype(kind)


def setup_inputs(seed: int = 0) -> dict:
    seeds = jax.random.split(jax.random.key(seed), 17)
    return {
        "tokens": scatter_about(seeds[0], (TOKENS, D), 1.0, 6.0, ((0, 32),)),
        "memory": scatter_about(seeds[1], (MEMS, D), 1.0, 6.0, ((0, 32),)),
        "target_lengths": draw_target_lengths(jax.random.fold_in(seeds[16], 71), 0),
        "memory_lengths": draw_memory_lengths(jax.random.fold_in(seeds[16], 71), 0),
        "task_ids": plant(jax.random.randint(seeds[4], (SEQS,), 0, TASKS), jax.random.fold_in(seeds[4], 1), 0, TASKS - 1).astype(jnp.int32),
        "cotangent": scatter_about(seeds[5], (TOKENS, D), 1.0, 6.0, ((0, 32),)),
        "self_qkv": scatter_about(seeds[6], (D, 3 * D), D ** -0.5, 0.21875, ((0, 8),)),
        "self_out": scatter_about(seeds[7], (D, D), (max(D * 16 // TOK_DEV, 1)) ** -0.5, 0.875, ((0, 8),)),
        "cross_q": scatter_about(seeds[8], (D, D), D ** -0.5, 0.21875, ((0, 8),)),
        "cross_kv": scatter_about(seeds[9], (D, 2 * D), D ** -0.5, 0.21875, ((0, 8),)),
        "cross_out": scatter_about(seeds[10], (D, D), (max(D * 16 // MEM, 1)) ** -0.5, 1.25, ((0, 8),)),
        "ffn_in": scatter_about(seeds[11], (D, FF), D ** -0.5, 0.21875, ((0, 8),)),
        "ffn_out": scatter_about(seeds[12], (FF, D), FF ** -0.5, 0.109375, ((0, 8),)),
        "task_table": scatter_about(seeds[13], (TASKS, EMB), 1.0, 6.0, (), jnp.float32),
        "hyper_in": scatter_about(seeds[14], (EMB, HYPER), EMB ** -0.5, 0.75, (), jnp.float32),
        "hyper_gen": scatter_about(seeds[15], (HYPER, GEN), HYPER ** -0.5, 0.5, ((1, 8),)),
    }


@jax.custom_vjp
def low(v):
    return lax.optimization_barrier(v.astype(jnp.bfloat16)).astype(jnp.float32)

@jax.custom_vjp
def low_back(v):
    return v

def low_keep(v):
    return (low(v), None)

def low_pass(kept, grad):
    return (grad,)

def back_keep(v):
    return (v, None)

def back_low(kept, grad):
    return (low(grad),)
low.defvjp(low_keep, low_pass)
low_back.defvjp(back_keep, back_low)

def matmul(left, right):
    return jnp.dot(left, right, precision=lax.Precision.HIGHEST)

def rms_norm(values, gains):
    return values * lax.rsqrt(lax.optimization_barrier(jnp.mean(values * values, axis=-1, keepdims=True)) + 1e-06) * gains

def attend(queries, keys, values, allowed):
    count = queries.shape[0]
    split_q = queries.reshape(count, HEADS, HEAD)
    split_k = keys.reshape(keys.shape[0], HEADS, HEAD)
    split_v = values.reshape(values.shape[0], HEADS, HEAD)
    scores = jnp.einsum('qhd,khd->hqk', split_q, split_k, precision=lax.Precision.HIGHEST) * HEAD ** (-0.5)
    scores = low_back(jnp.where(allowed[None], scores, -1e+30))
    weights = low(jax.nn.softmax(scores, axis=-1))
    mixed = jnp.einsum('hqk,khd->qhd', weights, split_v, precision=lax.Precision.HIGHEST)
    return mixed.reshape(count, HEADS * HEAD)

def adapter_branch(branch, down, upward):
    inner = low_back(matmul(branch, down) * D ** (-0.5))
    active = low(jax.nn.gelu(inner))
    return branch + low_back(matmul(active, upward) * ADAPT ** (-0.5))

def split_params(generated):
    gain_first = 1.0 + 0.25 * generated[0:D]
    gain_second = 1.0 + 0.25 * generated[D:2 * D]
    gain_third = 1.0 + 0.25 * generated[2 * D:3 * D]
    block = D * ADAPT
    start = 3 * D
    down_first = generated[start:start + block].reshape(D, ADAPT)
    up_first = generated[start + block:start + 2 * block].reshape(ADAPT, D)
    down_second = generated[start + 2 * block:start + 3 * block].reshape(D, ADAPT)
    up_second = generated[start + 3 * block:start + 4 * block].reshape(ADAPT, D)
    return (gain_first, gain_second, gain_third, down_first, up_first, down_second, up_second)

def one_layer(inputs, memory, target_len, memory_len, generated, weights):
    self_qkv, self_out, cross_q, cross_kv, cross_out, ffn_in, ffn_out = weights
    gain_first, gain_second, gain_third, down_first, up_first, down_second, up_second = split_params(generated)
    positions = jnp.arange(TOK_DEV, dtype=jnp.int32)
    valid = positions < target_len
    self_allowed = (positions[None, :] <= positions[:, None]) & (positions[None, :] < target_len)
    slots = jnp.arange(MEM, dtype=jnp.int32)
    memory_allowed = jnp.broadcast_to((slots < memory_len)[None, :], (TOK_DEV, MEM))
    normed = low(rms_norm(inputs, gain_first))
    qkv = low(low_back(matmul(normed, self_qkv)))
    mixed = low(low_back(attend(qkv[:, :D], qkv[:, D:2 * D], qkv[:, 2 * D:], self_allowed)))
    branch = low(low_back(matmul(mixed, self_out)))
    first = inputs + adapter_branch(branch, down_first, up_first)
    normed = low(rms_norm(first, gain_second))
    queries = low(low_back(matmul(normed, cross_q)))
    keyval = low(low_back(matmul(memory, cross_kv)))
    mixed = low(low_back(attend(queries, keyval[:, :D], keyval[:, D:], memory_allowed)))
    second = first + low_back(matmul(mixed, cross_out))
    normed = low(rms_norm(second, gain_third))
    hidden = low(jax.nn.gelu(low_back(matmul(normed, ffn_in))))
    branch = low(low_back(matmul(hidden, ffn_out)))
    result = second + adapter_branch(branch, down_second, up_second)
    return jnp.where(valid[:, None], result, 0.0)

def reference(tokens, memory, target_lengths, memory_lengths, task_ids, cotangent, self_qkv, self_out, cross_q, cross_kv, cross_out, ffn_in, ffn_out, task_table, hyper_in, hyper_gen):
    weights = tuple((w.astype(jnp.float32) for w in (self_qkv, self_out, cross_q, cross_kv, cross_out, ffn_in, ffn_out)))
    token_f = tokens.astype(jnp.float32)
    memory_f = memory.astype(jnp.float32)
    gen_f = hyper_gen.astype(jnp.float32)

    def forward(token_all, memory_all, layer_weights, table, first_layer, generator):
        hidden_all = low(jax.nn.gelu(matmul(table, first_layer)))

        def per_sequence(items):
            inputs, mems, target_len, memory_len, task = items
            select = (jnp.arange(TASKS, dtype=jnp.int32) == task).astype(jnp.float32)
            hidden_row = matmul(select, hidden_all)
            generated = low(low_back(matmul(hidden_row, generator)))
            return one_layer(inputs, mems, target_len, memory_len, generated, layer_weights)
        outputs = lax.map(jax.checkpoint(per_sequence), (token_all.reshape(SEQS, TOK_DEV, D), memory_all.reshape(SEQS, MEM, D), target_lengths, memory_lengths, task_ids))
        return outputs.reshape(SEQS * TOK_DEV, D)
    result, pullback = jax.vjp(forward, token_f, memory_f, weights, task_table, hyper_in, gen_f)
    grads = pullback(cotangent.astype(jnp.float32))
    grad_tokens, grad_memory, grad_weights, grad_table, grad_first, grad_gen = grads
    return (result.astype(jnp.bfloat16), grad_tokens, grad_memory, grad_weights[0], grad_weights[1], grad_weights[2], grad_weights[3], grad_weights[4], grad_weights[5], grad_weights[6], grad_table, grad_first, grad_gen)
```

```python
import functools

import jax
import jax.numpy as jnp
from jax import lax
from jax.experimental import pallas as pl
from jax.experimental.pallas import tpu as pltpu
from jax.sharding import PartitionSpec as P

D = 768
HEADS = 12
HEAD = 64
ADAPT = 24
TASKS = 8
BOTH = ("dp", "fsdp")


def matmul(left, right):
    return jnp.dot(left, right, preferred_element_type=jnp.float32)


def matmul_left_t(left, right):
    return lax.dot_general(
        left, right, (((0,), (0,)), ((), ())), preferred_element_type=jnp.float32
    )


def matmul_right_t(left, right):
    return lax.dot_general(
        left, right, (((1,), (1,)), ((), ())), preferred_element_type=jnp.float32
    )


def rms_norm(values, gains):
    return values * lax.rsqrt(jnp.mean(values * values, axis=-1, keepdims=True) + 1e-06) * gains


def norm_grad(values, gains, upstream):
    return jax.vjp(rms_norm, values, gains)[1](upstream)


def gelu_grad(values, upstream):
    return jax.vjp(jax.nn.gelu, values)[1](upstream)[0]


def split_heads(values):
    return values.reshape(values.shape[0], HEADS, HEAD)


def attend_scores(queries, keys, allowed):
    scores = jnp.einsum(
        "qhd,khd->hqk", split_heads(queries), split_heads(keys), preferred_element_type=jnp.float32
    )
    return jnp.where(allowed[None], scores * HEAD ** (-0.5), -1e30)


def attend_forward(queries, keys, values, allowed):
    scores = attend_scores(queries, keys, allowed)
    top = jnp.max(scores, axis=-1, keepdims=True)
    total = jnp.sum(jnp.exp(scores - top), axis=-1, keepdims=True)
    weights = jnp.exp(scores - top) / total
    mixed = jnp.einsum(
        "hqk,khd->qhd",
        weights.astype(jnp.bfloat16),
        split_heads(values),
        preferred_element_type=jnp.float32,
    )
    return (mixed.reshape(queries.shape[0], D).astype(jnp.bfloat16), top + jnp.log(total))


def attend_backward(queries, keys, values, allowed, log_total, grad_mixed):
    weights = jnp.exp(attend_scores(queries, keys, allowed) - log_total)
    grad_split = split_heads(grad_mixed)
    grad_weights = jnp.einsum(
        "qhd,khd->hqk", grad_split, split_heads(values), preferred_element_type=jnp.float32
    )
    grad_scores = weights * (grad_weights - jnp.sum(grad_weights * weights, axis=-1, keepdims=True))
    grad_low = grad_scores.astype(jnp.bfloat16)
    grad_q = jnp.einsum(
        "hqk,khd->qhd", grad_low, split_heads(keys), preferred_element_type=jnp.float32
    ) * HEAD ** (-0.5)
    grad_k = jnp.einsum(
        "hqk,qhd->khd", grad_low, split_heads(queries), preferred_element_type=jnp.float32
    ) * HEAD ** (-0.5)
    grad_v = jnp.einsum(
        "hqk,qhd->khd", weights.astype(jnp.bfloat16), grad_split, preferred_element_type=jnp.float32
    )
    return (
        grad_q.reshape(queries.shape[0], D),
        grad_k.reshape(keys.shape[0], D),
        grad_v.reshape(keys.shape[0], D),
    )


def adapter_forward(branch, down, upward):
    inner = matmul(branch, down) * D ** (-0.5)
    active = jax.nn.gelu(inner).astype(jnp.bfloat16)
    return (branch.astype(jnp.float32) + matmul(active, upward) * ADAPT ** (-0.5), inner, active)


def adapter_backward(branch, down, upward, inner, active, grad_out):
    grad_low = grad_out.astype(jnp.bfloat16)
    grad_up = matmul_left_t(active, grad_low) * ADAPT ** (-0.5)
    grad_active = matmul_right_t(grad_low, upward) * ADAPT ** (-0.5)
    grad_inner = gelu_grad(inner, grad_active).astype(jnp.bfloat16)
    grad_down = matmul_left_t(branch, grad_inner) * D ** (-0.5)
    grad_branch = grad_out + matmul_right_t(grad_inner, down) * D ** (-0.5)
    return (grad_branch.astype(jnp.bfloat16), grad_down, grad_up)


def split_params(generated):
    values = generated.astype(jnp.float32)
    gains = tuple((1.0 + 0.25 * values[k * D : (k + 1) * D] for k in range(3)))
    block = D * ADAPT
    start = 3 * D
    down_first = generated[start : start + block].reshape(D, ADAPT)
    up_first = generated[start + block : start + 2 * block].reshape(ADAPT, D)
    down_second = generated[start + 2 * block : start + 3 * block].reshape(D, ADAPT)
    up_second = generated[start + 3 * block : start + 4 * block].reshape(ADAPT, D)
    return (gains, down_first, up_first, down_second, up_second)


def moves(step):
    pairs = []
    for y in range(2):
        for x in range(2):
            for z in range(4):
                for c in range(2):
                    ty, tx, tz, tc = step(y, x, z, c)
                    pairs.append((((y * 2 + x) * 4 + z) * 2 + c, ((ty * 2 + tx) * 4 + tz) * 2 + tc))
    return pairs


def swap_x(values):
    return lax.ppermute(values, BOTH, moves(lambda y, x, z, c: (y, 1 - x, z, c)))


def swap_y(values):
    return lax.ppermute(values, BOTH, moves(lambda y, x, z, c: (1 - y, x, z, c)))


def swap_core(values):
    return lax.ppermute(values, BOTH, moves(lambda y, x, z, c: (y, x, z, 1 - c)))


def turn_z(values, by):
    return lax.ppermute(values, BOTH, moves(lambda y, x, z, c: (y, x, (z + by) % 4, c)))


def place_kernel(where, own, other, out, sems):
    q, z, c = where[0], where[1], where[2]
    copies = []
    for r in range(4):
        for k in range(4):
            for side, source in enumerate((own, other)):
                copies.append(
                    pltpu.make_async_copy(
                        source.at[r, k],
                        out.at[q ^ r, (z - k + 4) % 4, c ^ side],
                        sems.at[(r * 4 + k) * 2 + side],
                    )
                )
    for copy in copies:
        copy.start()
    for copy in copies:
        copy.wait()


def place(where, own, other):
    return pl.pallas_call(
        place_kernel,
        out_shape=jax.ShapeDtypeStruct((4, 4, 2) + own.shape[2:], own.dtype),
        grid_spec=pltpu.PrefetchScalarGridSpec(
            num_scalar_prefetch=1,
            grid=(1,),
            in_specs=[pl.BlockSpec(memory_space=pl.ANY)] * 2,
            out_specs=pl.BlockSpec(memory_space=pltpu.VMEM),
            scratch_shapes=[pltpu.SemaphoreType.DMA((32,))],
        ),
        compiler_params=pltpu.CompilerParams(vmem_limit_bytes=24 << 20),
        cost_estimate=pl.CostEstimate(flops=0, bytes_accessed=4 * own.size * own.dtype.itemsize, transcendentals=0),
        name="place",
    )(where, own, other)


def sort_kernel(where, blocks, keep, send, sems):
    q, z, c = where[0], where[1], where[2]
    copies = []
    for r in range(4):
        for k in range(4):
            for side, target in enumerate((keep, send)):
                copies.append(
                    pltpu.make_async_copy(
                        blocks.at[q ^ r, (z + k) % 4, c ^ side],
                        target.at[r, k],
                        sems.at[(r * 4 + k) * 2 + side],
                    )
                )
    for copy in copies:
        copy.start()
    for copy in copies:
        copy.wait()


def sort(where, blocks):
    half = jax.ShapeDtypeStruct((4, 4) + blocks.shape[3:], blocks.dtype)
    return pl.pallas_call(
        sort_kernel,
        out_shape=(half, half),
        grid_spec=pltpu.PrefetchScalarGridSpec(
            num_scalar_prefetch=1,
            grid=(1,),
            in_specs=[pl.BlockSpec(memory_space=pl.ANY)],
            out_specs=[pl.BlockSpec(memory_space=pltpu.VMEM)] * 2,
            scratch_shapes=[pltpu.SemaphoreType.DMA((32,))],
        ),
        compiler_params=pltpu.CompilerParams(vmem_limit_bytes=24 << 20),
        cost_estimate=pl.CostEstimate(flops=0, bytes_accessed=2 * blocks.size * blocks.dtype.itemsize, transcendentals=0),
        name="sort",
    )(where, blocks)


def gather_blocks(where, blocks, x_first):
    own = lax.dynamic_index_in_dim(jnp.stack(blocks), where[0], 0, keepdims=False)
    column = jnp.stack([own] + [turn_z(own, k) for k in (1, 2, 3)])
    if x_first:
        pair = jnp.stack([column, swap_x(column)])
        quad = jnp.concatenate([pair, swap_y(pair)])
    else:
        pair = jnp.stack([column, swap_y(column)])
        quad = jnp.stack([pair, swap_x(pair)], axis=1).reshape((4,) + column.shape)
    whole = place(where, quad, swap_core(quad))
    return whole.reshape(4, D, D)


def low(values):
    return values.astype(jnp.bfloat16)


def add_low(left, right):
    return low(left.astype(jnp.float32) + right.astype(jnp.float32))


def scatter_blocks(where, blocks, x_first):
    keep, send = sort(where, blocks.reshape(4, 4, 2, D // 8, D))
    total = add_low(keep, swap_core(send))
    if x_first:
        kept, sent = (total[0::2], total[1::2])
        total = add_low(kept, swap_x(sent))
        total = add_low(total[0], swap_y(total[1]))
    else:
        kept, sent = (total[:2], total[2:])
        total = add_low(kept, swap_y(sent))
        total = add_low(total[0], swap_x(total[1]))
    parts = [total[0]] + [turn_z(total[k], k) for k in (1, 2, 3)]
    parts = [part.astype(jnp.float32) for part in parts]
    own = low((parts[0] + parts[2]) + (parts[1] + parts[3]))
    pair = jnp.stack([own, swap_x(own)])
    quad = jnp.concatenate([pair, swap_y(pair)])
    return quad


def to_owner(where, quad):
    q = where[0]
    return [lax.dynamic_index_in_dim(quad, q ^ b, 0, keepdims=False).astype(jnp.float32) for b in range(4)]


def fast_transfers(
    task_id, self_qkv, self_out, cross_q, cross_kv, cross_out, ffn_in, ffn_out, hidden_all, hyper_gen
):
    q = lax.axis_index("dp").astype(jnp.int32)
    f = lax.axis_index("fsdp").astype(jnp.int32)
    where = jnp.stack([q, f // 2, f % 2])
    rows = self_qkv.shape[0]
    ids = jnp.stack([task_id, swap_core(task_id)])
    ids_ahead = [ids] + [turn_z(ids, 4 - k) for k in (1, 2, 3)]
    gen_shard = low(matmul(hidden_all, hyper_gen))

    def rows_of(tasks):
        select = low(tasks[:, None] == jnp.arange(TASKS, dtype=jnp.int32)[None, :])
        return low(matmul(select, gen_shard))

    asked = [rows_of(ids_ahead[k]) for k in range(4)]
    got = jnp.stack([asked[0]] + [turn_z(asked[k], k) for k in (1, 2, 3)], axis=1)
    pieces = jnp.concatenate([got[0], swap_core(got[1])])
    slots = jnp.arange(8, dtype=jnp.int32)
    source = ((slots % 2) ^ where[2]) * 4 + (where[1] - slots // 2 + 4) % 4
    unturn = low(source[:, None] == slots[None, :])
    generated = low(matmul(unturn, pieces)).reshape(-1)
    w1 = gather_blocks(
        where, [self_qkv[:, :D], self_qkv[:, D : 2 * D], self_qkv[:, 2 * D :], self_out], True
    )
    w2 = gather_blocks(where, [cross_q, cross_out, cross_kv[:, :D], cross_kv[:, D:]], False)
    w3 = gather_blocks(where, [ffn_in[:, b * D : (b + 1) * D] for b in range(4)], True)
    w4 = gather_blocks(where, [ffn_out[b * rows : (b + 1) * rows] for b in range(4)], False)
    return (where, ids_ahead, generated, w1, w2, w3, w4)


def layer(
    tokens,
    memory,
    target_len,
    memory_len,
    cotangent,
    generated,
    w_q,
    w_k,
    w_v,
    w_sout,
    w_cq,
    w_cout,
    w_ck,
    w_cv,
    w_in,
    w_out,
):
    w_qkv = jnp.concatenate([w_q, w_k, w_v], axis=1)
    w_ckv = jnp.concatenate([w_ck, w_cv], axis=1)
    w_in = jnp.concatenate(w_in, axis=1)
    w_out = jnp.concatenate(w_out, axis=0)
    gains, down_first, up_first, down_second, up_second = split_params(generated)
    token_rows = tokens.shape[0]
    positions = jnp.arange(token_rows, dtype=jnp.int32)
    valid = (positions < target_len)[:, None]
    self_allowed = (positions[None, :] <= positions[:, None]) & (positions[None, :] < target_len)
    slots = jnp.arange(memory.shape[0], dtype=jnp.int32)
    memory_allowed = jnp.broadcast_to((slots < memory_len)[None, :], (token_rows, memory.shape[0]))
    inputs = tokens.astype(jnp.float32)
    normed_self = low(rms_norm(inputs, gains[0]))
    qkv = low(matmul(normed_self, w_qkv))
    mixed_self, log_self = attend_forward(
        qkv[:, :D], qkv[:, D : 2 * D], qkv[:, 2 * D :], self_allowed
    )
    branch_self = low(matmul(mixed_self, w_sout))
    adapted_self, inner_self, active_self = adapter_forward(branch_self, down_first, up_first)
    first = inputs + adapted_self
    normed_cross = low(rms_norm(first, gains[1]))
    cross_queries = low(matmul(normed_cross, w_cq))
    memory_kv = low(matmul(memory, w_ckv))
    mixed_cross, log_cross = attend_forward(
        cross_queries, memory_kv[:, :D], memory_kv[:, D:], memory_allowed
    )
    second = first + matmul(mixed_cross, w_cout)
    normed_ffn = low(rms_norm(second, gains[2]))
    pre_ffn = matmul(normed_ffn, w_in)
    hidden_ffn = low(jax.nn.gelu(pre_ffn))
    branch_ffn = low(matmul(hidden_ffn, w_out))
    adapted_ffn, inner_ffn, active_ffn = adapter_forward(branch_ffn, down_second, up_second)
    result = second + adapted_ffn
    mixed_out = low(jnp.where(valid, result, 0.0))
    grad_result = jnp.where(valid, cotangent.astype(jnp.float32), 0.0)
    grad_branch_ffn, grad_down_second, grad_up_second = adapter_backward(
        branch_ffn, down_second, up_second, inner_ffn, active_ffn, grad_result
    )
    grad_ffn_out = low(matmul_left_t(hidden_ffn, grad_branch_ffn))
    grad_pre = low(gelu_grad(pre_ffn, matmul_right_t(grad_branch_ffn, w_out)))
    grad_ffn_in = low(matmul_left_t(normed_ffn, grad_pre))
    grad_part, grad_gain_third = norm_grad(second, gains[2], matmul_right_t(grad_pre, w_in))
    grad_second = grad_result + grad_part
    grad_cross_branch = low(grad_second)
    grad_cross_out = low(matmul_left_t(mixed_cross, grad_cross_branch))
    grad_mixed_cross = low(matmul_right_t(grad_cross_branch, w_cout))
    grad_q2, grad_k2, grad_v2 = attend_backward(
        cross_queries,
        memory_kv[:, :D],
        memory_kv[:, D:],
        memory_allowed,
        log_cross,
        grad_mixed_cross,
    )
    grad_queries = low(grad_q2)
    grad_memory_kv = low(jnp.concatenate([grad_k2, grad_v2], axis=1))
    grad_cross_q = low(matmul_left_t(normed_cross, grad_queries))
    grad_cross_kv = low(matmul_left_t(memory, grad_memory_kv))
    memory_grad = matmul_right_t(grad_memory_kv, w_ckv)
    grad_part, grad_gain_second = norm_grad(first, gains[1], matmul_right_t(grad_queries, w_cq))
    grad_first = grad_second + grad_part
    grad_branch_self, grad_down_first, grad_up_first = adapter_backward(
        branch_self, down_first, up_first, inner_self, active_self, grad_first
    )
    grad_self_out = low(matmul_left_t(mixed_self, grad_branch_self))
    grad_mixed_self = low(matmul_right_t(grad_branch_self, w_sout))
    grad_q1, grad_k1, grad_v1 = attend_backward(
        qkv[:, :D], qkv[:, D : 2 * D], qkv[:, 2 * D :], self_allowed, log_self, grad_mixed_self
    )
    grad_qkv = low(jnp.concatenate([grad_q1, grad_k1, grad_v1], axis=1))
    grad_self_qkv = low(matmul_left_t(normed_self, grad_qkv))
    grad_part, grad_gain_first = norm_grad(inputs, gains[0], matmul_right_t(grad_qkv, w_qkv))
    token_grad = grad_first + grad_part
    grad_generated = jnp.concatenate(
        [
            0.25 * grad_gain_first,
            0.25 * grad_gain_second,
            0.25 * grad_gain_third,
            grad_down_first.reshape(-1),
            grad_up_first.reshape(-1),
            grad_down_second.reshape(-1),
            grad_up_second.reshape(-1),
        ]
    ).astype(jnp.bfloat16)
    weight_grads = (
        grad_self_qkv,
        grad_self_out,
        grad_cross_q,
        grad_cross_kv,
        grad_cross_out,
        grad_ffn_in,
        grad_ffn_out,
    )
    return (mixed_out, token_grad, memory_grad, weight_grads, grad_generated)


def hyper_tail(task_grad, pre_all, hidden_all, task_table, hyper_in, hyper_gen, sum_owners):
    grad_hyper_gen = jnp.dot(
        hidden_all.astype(jnp.float32).T, task_grad, precision=lax.Precision.HIGHEST
    )
    grad_hidden = jnp.dot(
        task_grad, hyper_gen.astype(jnp.float32).T, precision=lax.Precision.HIGHEST
    )
    grad_pre_all = gelu_grad(pre_all, sum_owners(grad_hidden))
    grad_table = jnp.dot(grad_pre_all, hyper_in.T, precision=lax.Precision.HIGHEST)
    grad_first = jnp.dot(task_table.T, grad_pre_all, precision=lax.Precision.HIGHEST)
    return grad_table, grad_first, grad_hyper_gen


def columns_of(matrix):
    return [matrix[:, b * D : (b + 1) * D] for b in range(matrix.shape[1] // D)]


def rows_of_blocks(matrix):
    return [matrix[b * D : (b + 1) * D] for b in range(matrix.shape[0] // D)]


def shards(
    tokens,
    memory,
    target_lengths,
    memory_lengths,
    task_ids,
    cotangent,
    self_qkv,
    self_out,
    cross_q,
    cross_kv,
    cross_out,
    ffn_in,
    ffn_out,
    task_table,
    hyper_in,
    hyper_gen,
):
    owners = lax.axis_size("fsdp")
    buckets = lax.axis_size("dp")
    staged = owners == 8 and buckets == 4
    pre_all = jnp.dot(task_table, hyper_in, precision=lax.Precision.HIGHEST)
    hidden_all = low(jax.nn.gelu(pre_all))
    if staged:
        where, ids_ahead, generated, w1, w2, w3, w4 = fast_transfers(
            task_ids[0],
            self_qkv,
            self_out,
            cross_q,
            cross_kv,
            cross_out,
            ffn_in,
            ffn_out,
            hidden_all,
            hyper_gen,
        )
        w_in = list(w3)
        w_out = rows_of_blocks(w4.reshape(4, owners, -1, D).swapaxes(0, 1).reshape(-1, D))
        w_q, w_k, w_v, w_sout = w1
        w_cq, w_cout, w_ck, w_cv = w2
    else:
        full = [
            lax.all_gather(w, "fsdp", axis=0, tiled=True)
            for w in (self_qkv, self_out, cross_q, cross_kv, cross_out, ffn_in, ffn_out)
        ]
        w_q, w_k, w_v = columns_of(full[0])
        w_sout, w_cq = full[1], full[2]
        w_ck, w_cv = columns_of(full[3])
        w_cout = full[4]
        w_in, w_out = columns_of(full[5]), rows_of_blocks(full[6])
        select = low(task_ids[:, None] == jnp.arange(TASKS, dtype=jnp.int32)[None, :])
        gen_shard = low(matmul(hidden_all, hyper_gen))
        gen_tasks = lax.all_gather(gen_shard, "fsdp", axis=1, tiled=True)
        generated = low(matmul(select, gen_tasks)[0])
    mixed_out, token_grad, memory_grad, weight_grads, grad_generated = layer(
        tokens,
        memory,
        target_lengths[0],
        memory_lengths[0],
        cotangent,
        generated,
        w_q,
        w_k,
        w_v,
        w_sout,
        w_cq,
        w_cout,
        w_ck,
        w_cv,
        w_in,
        w_out,
    )
    g_qkv, g_sout, g_cq, g_ckv, g_cout, g_in, g_out = weight_grads
    if staged:
        s4 = to_owner(where, scatter_blocks(
            where, g_out.reshape(owners, 4, -1, D).swapaxes(0, 1).reshape(4, D, D), True
        ))
        s3 = to_owner(where, scatter_blocks(where, jnp.stack(columns_of(g_in)), False))
        s2 = to_owner(where, scatter_blocks(where, jnp.stack([g_cq, g_cout] + columns_of(g_ckv)), True))
        s1 = to_owner(where, scatter_blocks(where, jnp.stack(columns_of(g_qkv) + [g_sout]), False))
        summed = (
            jnp.concatenate(s1[:3], axis=1),
            s1[3],
            s2[0],
            jnp.concatenate(s2[2:], axis=1),
            s2[1],
            jnp.concatenate(s3, axis=1),
            jnp.concatenate(s4, axis=0),
        )
        z, c = where[1], where[2]
        pieces = grad_generated.reshape(4, 2, -1)
        mine = lax.dynamic_index_in_dim(pieces, c, 1, keepdims=False)
        theirs = lax.dynamic_index_in_dim(pieces, 1 - c, 1, keepdims=False)
        both = jnp.stack([mine, swap_core(theirs)], axis=1)
        both = [lax.dynamic_index_in_dim(both, (z + k) % 4, 0, keepdims=False) for k in range(4)]
        terms = jnp.concatenate([both[0]] + [turn_z(both[k], k) for k in (1, 2, 3)])
        ids = jnp.concatenate([ids_ahead[(4 - k) % 4] for k in range(4)])
        select = low(jnp.arange(TASKS, dtype=jnp.int32)[:, None] == ids[None, :])
        task_grad = low(matmul(select, terms))
        task_grad = add_low(task_grad, swap_x(task_grad))
        task_grad = task_grad.astype(jnp.float32) + swap_y(task_grad).astype(jnp.float32)

        def sum_owners(part):
            part = part + swap_core(part)
            turned = [part] + [turn_z(part, k) for k in (1, 2, 3)]
            return (turned[0] + turned[2]) + (turned[1] + turned[3])
    else:
        summed = tuple(
            lax.psum(low(lax.psum_scatter(g, "fsdp", scatter_dimension=0, tiled=True)), "dp").astype(
                jnp.float32
            )
            for g in weight_grads
        )
        pieces = grad_generated.reshape(owners, 1, -1)
        select = low(jnp.arange(TASKS, dtype=jnp.int32)[:, None] == task_ids[None, :])
        terms = low(select[None].astype(jnp.float32) * pieces.astype(jnp.float32))
        terms = lax.all_to_all(terms, "fsdp", split_axis=0, concat_axis=0, tiled=True)
        task_grad = low(jnp.sum(terms.astype(jnp.float32), axis=0))
        task_grad = lax.psum(task_grad, "dp").astype(jnp.float32)

        def sum_owners(part):
            return lax.psum(part, "fsdp")

    grad_table, grad_first, grad_hyper_gen = hyper_tail(
        task_grad, pre_all, hidden_all, task_table, hyper_in, hyper_gen, sum_owners
    )
    return (
        mixed_out,
        token_grad,
        memory_grad,
    ) + summed + (
        grad_table,
        grad_first,
        grad_hyper_gen,
    )


def solution(mesh):
    by_both = P(("dp", "fsdp"), None)
    by_rows = P("fsdp", None)
    return jax.shard_map(
        shards,
        mesh=mesh,
        in_specs=(by_both, by_both)
        + (P(("dp", "fsdp")),) * 3
        + (by_both,)
        + (by_rows,) * 7
        + (P(), P(), P(None, "fsdp")),
        out_specs=(by_both,) * 3 + (by_rows,) * 7 + (P(), P(), P(None, "fsdp")),
        check_vma=False,
    )
```

```python
import functools

import jax
import jax.numpy as jnp
from jax import lax
from jax.experimental import pallas as pl
from jax.experimental.pallas import tpu as pltpu
from jax.sharding import PartitionSpec as P

D = 768
HEADS = 12
HEAD = 64
ADAPT = 24
TASKS = 8
BOTH = ("dp", "fsdp")


def matmul(left, right):
    return jnp.dot(left, right, preferred_element_type=jnp.float32)


def matmul_left_t(left, right):
    return lax.dot_general(
        left, right, (((0,), (0,)), ((), ())), preferred_element_type=jnp.float32
    )


def matmul_right_t(left, right):
    return lax.dot_general(
        left, right, (((1,), (1,)), ((), ())), preferred_element_type=jnp.float32
    )


def low(values):
    return values.astype(jnp.bfloat16)


def add_low(left, right):
    return low(left.astype(jnp.float32) + right.astype(jnp.float32))


def rms_factor(values):
    return lax.rsqrt(jnp.mean(values * values, axis=-1, keepdims=True) + 1e-06)


def norm_grad(values, gains, upstream):
    factor = rms_factor(values)
    scaled = upstream * gains
    mean = jnp.mean(values * scaled, axis=-1, keepdims=True)
    part = factor * scaled - values * (factor * factor * factor * mean)
    return part, jnp.sum(upstream * values * factor, axis=0, keepdims=True)


GELU_A = 0.7978845608
GELU_B = 0.044715


def gelu(values):
    inside = GELU_A * (values + GELU_B * values * values * values)
    return 0.5 * values * (1.0 + jnp.tanh(inside))


def gelu_slope(values):
    square = values * values
    curve = jnp.tanh(GELU_A * (values + GELU_B * square * values))
    inner = GELU_A * (1.0 + 3.0 * GELU_B * square)
    return 0.5 * (1.0 + curve) + 0.5 * values * (1.0 - curve * curve) * inner


def group_row(mixed, block, owner, rows):
    return owner * (4 * rows) + block * rows if mixed else block * D + owner * rows


class Group:
    def __init__(self, scalars, refs, scratch, sems, mixed, blocks):
        self.scalars, self.refs, self.scratch, self.sems = scalars, refs, scratch, sems
        self.mixed, self.blocks = mixed, blocks

    def _each(self, act):
        if len(self.refs) == 1:
            act(pltpu.make_async_copy(self.refs[0], self.scratch, self.sems.at[0]))
            return
        q, c = self.scalars[0], self.scalars[2]
        rows = self.refs[0].shape[1]
        for r in range(4):
            block = q ^ r

            def parts(r=r, block=block):
                for side in range(2):
                    for z in range(4):
                        at = pl.multiple_of(group_row(self.mixed, block, z * 2 + (c ^ side), rows), 32)
                        act(
                            pltpu.make_async_copy(
                                self.refs[side * 4 + r].at[z],
                                self.scratch.at[pl.ds(at, rows)],
                                self.sems.at[(r * 4 + z) * 2 + side],
                            )
                        )

            if len(self.blocks) == 4:
                parts()
            else:
                wanted = block == self.blocks[0]
                for other in self.blocks[1:]:
                    wanted = wanted | (block == other)
                pl.when(wanted)(parts)

    def start(self):
        self._each(lambda copy: copy.start())

    def wait(self):
        self._each(lambda copy: copy.wait())

    def block(self, index):
        return self.scratch[index * D : (index + 1) * D, :]


def part_rows(scalars, value, keep, send, at):
    flat = value.T
    rows = flat.shape[0] // 8
    for parity in range(2):
        here = scalars[2] == parity

        @pl.when(here)
        def _():
            for z in range(4):
                piece = flat[(z * 2 + parity) * rows : (z * 2 + parity + 1) * rows]
                keep[at + z * rows : at + (z + 1) * rows, :] = piece

        @pl.when(jnp.logical_not(here))
        def _():
            for z in range(4):
                piece = flat[(z * 2 + parity) * rows : (z * 2 + parity + 1) * rows]
                send[at + z * rows : at + (z + 1) * rows, :] = piece


ONE_WAY = {True: ((True, 0, 4),), False: ((False, 0, 4),)}
BOTH_WAYS = ((True, 0, 2), (False, 2, 4))


class Blocks:
    def __init__(self, scalars, outs, stage, sems, ways):
        self.scalars, self.outs, self.stage, self.sems, self.ways = scalars, outs, stage, sems, ways
        self.sent = []

    def put(self, block, value):
        rows = value.shape[0] // 4
        value = low(value)
        for z in range(4):
            self.stage[block, z] = value[z * rows : (z + 1) * rows]
        r = self.scalars[0] ^ block
        for i, (x_first, z0, z1) in enumerate(self.ways):
            first, second = (r % 2, r // 2) if x_first else (r // 2, r % 2)
            for away in range(2):
                copy = pltpu.make_async_copy(
                    self.stage.at[block, pl.ds(z0, z1 - z0)],
                    self.outs[2 * i + away].at[second],
                    self.sems.at[block * 4 + 2 * i + away],
                )
                pl.when(first == away)(copy.start)
                self.sent.append((first == away, copy))

    def finish(self):
        for here, copy in self.sent:
            pl.when(here)(copy.wait)


def head_lanes(rows, head):
    lane = lax.broadcasted_iota(jnp.int32, (rows, 128), 1)
    return lane < HEAD if head == 0 else lane >= HEAD


def pick_head(values, head):
    return jnp.where(head_lanes(values.shape[0], head), values, jnp.zeros_like(values))


def attend_pairs(q_ref, k_ref, k_at, v_ref, v_at, bias, probs, mixed):
    ready(q_ref, k_ref, v_ref)

    @pl.loop(0, HEADS // 2)
    def _(pair):
        at = pl.multiple_of(pair * 128, 128)
        queries = q_ref[:, pl.ds(at, 128)]
        keys = k_ref[:, pl.ds(pl.multiple_of(k_at + at, 128), 128)]
        values = v_ref[:, pl.ds(pl.multiple_of(v_at + at, 128), 128)].T
        halves = []
        for head in range(2):
            scores = matmul_right_t(pick_head(keys, head), queries) + bias
            top = jnp.max(scores, axis=0, keepdims=True)
            weights = jnp.exp(scores - top)
            weights = low(weights * (1.0 / jnp.sum(weights, axis=0, keepdims=True)))
            probs[pair * 2 + head] = weights
            halves.append(matmul(values[head * HEAD : (head + 1) * HEAD], weights))
        mixed[:, pl.ds(at, 128)] = low(jnp.concatenate(halves, axis=0).T)


def attend_pairs_back(q_ref, k_ref, k_at, v_ref, v_at, probs, grad_mixed, grad_q, grad_k, gk_at, grad_v, gv_at):
    ready(q_ref, k_ref, v_ref, probs)

    @pl.loop(0, HEADS // 2)
    def _(pair):
        at = pl.multiple_of(pair * 128, 128)
        queries = q_ref[:, pl.ds(at, 128)]
        keys = k_ref[:, pl.ds(pl.multiple_of(k_at + at, 128), 128)]
        values = v_ref[:, pl.ds(pl.multiple_of(v_at + at, 128), 128)]
        grads = grad_mixed[:, pl.ds(at, 128)]
        keys_t = keys.T
        halves, part_k, part_v = [], [], []
        for head in range(2):
            weights = probs[pair * 2 + head]
            wide = weights.astype(jnp.float32)
            grad_w = matmul_right_t(pick_head(values, head), grads)
            total = jnp.sum(grad_w * wide, axis=0, keepdims=True)
            grad_s = low(wide * (grad_w - total))
            part_k.append(matmul(grad_s, queries))
            part_v.append(matmul(weights, grads))
            halves.append(matmul(keys_t[head * HEAD : (head + 1) * HEAD], grad_s))
        first = head_lanes(keys.shape[0], 0)
        grad_q[:, pl.ds(at, 128)] = low(jnp.concatenate(halves, axis=0).T * HEAD ** (-0.5))
        grad_k[:, pl.ds(pl.multiple_of(gk_at + at, 128), 128)] = low(jnp.where(first, part_k[0], part_k[1]))
        grad_v[:, pl.ds(pl.multiple_of(gv_at + at, 128), 128)] = low(jnp.where(first, part_v[0], part_v[1]))


def adapter_forward(branch, down, upward):
    inner = matmul(branch, down) * D ** (-0.5)
    active = low(gelu(inner))
    return branch.astype(jnp.float32) + matmul(active, upward) * ADAPT ** (-0.5), inner, active


def adapter_backward(branch, down, upward, inner, active, grad_out):
    grad_low = low(grad_out)
    grad_up = matmul_left_t(active, grad_low) * ADAPT ** (-0.5)
    grad_active = matmul_right_t(grad_low, upward) * ADAPT ** (-0.5)
    grad_inner = low(gelu_slope(inner) * grad_active)
    grad_down = matmul_left_t(branch, grad_inner) * D ** (-0.5)
    grad_branch = low(grad_out + matmul_right_t(grad_inner, down) * D ** (-0.5))
    return grad_branch, grad_down, grad_up


def self_forward_kernel(n, scalars, tokens, gains, down, up, *rest):
    refs, (qkv, probs, branch, inner_out, first_out, normed_cross, *saved, scratch, sems) = rest[:n], rest[n:]
    *halves, normed, mixed = saved
    group = Group(scalars, refs, scratch, sems, False, range(4))
    group.start()
    inputs = tokens[...].astype(jnp.float32)
    normed[...] = low(inputs * rms_factor(inputs) * gains[0:1])
    rows = inputs.shape[0]
    key = lax.broadcasted_iota(jnp.int32, (rows, rows), 0)
    query = lax.broadcasted_iota(jnp.int32, (rows, rows), 1)
    bias = jnp.where((key <= query) & (key < scalars[3]), 0.0, -1e30)
    if halves:
        part_rows(scalars, normed[...], *halves, 0)
    group.wait()
    for b in range(3):
        product = matmul(normed[...], group.block(b))
        qkv[:, b * D : (b + 1) * D] = low(product) * (HEAD ** (-0.5) if b == 0 else 1.0)
    send(qkv)
    attend_pairs(qkv, qkv, D, qkv, 2 * D, bias, probs, mixed)
    send(probs)
    if halves:
        part_rows(scalars, mixed[...], *halves, D // 2)
        send(*halves)
    branch[...] = low(matmul(mixed[...], group.block(3)))
    adapted, inner, _ = adapter_forward(branch[...], down[...], up[...])
    inner_out[...] = inner
    first = inputs + adapted
    first_out[...] = first
    normed_cross[...] = low(first * rms_factor(first) * gains[1:2])


def cross_forward_kernel(n, scalars, normed, first, memory, gains, *rest):
    refs, (queries, memory_kv, probs, second_out, normed_ffn, *saved, scratch, sems) = rest[:n], rest[n:]
    *halves, mixed = saved
    group = Group(scalars, refs, scratch, sems, False, range(4))
    group.start()
    slot = lax.broadcasted_iota(jnp.int32, (memory.shape[0], 1), 0)
    bias = jnp.where(slot < scalars[4], 0.0, -1e30)
    if halves:
        part_rows(scalars, normed[...], *halves, 0)
        half = memory.shape[0] // 2
        for i in range(2):
            part_rows(scalars, memory[i * half : (i + 1) * half, :], *halves, (2 + i) * (D // 2))
    group.wait()
    queries[...] = low(matmul(normed[...], group.block(0))) * HEAD ** (-0.5)
    for b in range(2):
        memory_kv[:, b * D : (b + 1) * D] = low(matmul(memory[...], group.block(2 + b)))
    send(queries, memory_kv)
    attend_pairs(queries, memory_kv, 0, memory_kv, D, bias, probs, mixed)
    send(probs)
    if halves:
        part_rows(scalars, mixed[...], *halves, D // 2)
        send(*halves)
    second = first[...] + matmul(mixed[...], group.block(1))
    second_out[...] = second
    normed_ffn[...] = low(second * rms_factor(second) * gains[2:3])


def ffn_in_kernel(n, scalars, normed, *rest):
    refs, (pre, hidden, *saved, scratch, sems) = rest[:n], rest[n:]
    group = Group(scalars, refs, scratch, sems, False, range(4))
    group.start()
    if saved:
        part_rows(scalars, normed[...], *saved, 0)
    group.wait()
    for b in range(4):
        at = slice(b * D, (b + 1) * D)
        product = matmul(normed[...], group.block(b))
        pre[:, at] = product
        hidden[:, at] = low(gelu(product))
    send(pre, hidden)
    if saved:
        part_rows(scalars, hidden[...], *saved, D // 2)


def ffn_out_kernel(n, scalars, hidden, second, cotangent, down, up, *rest):
    refs, (mixed_out, grad_branch, grad_down, grad_up, scratch, sems) = rest[:n], rest[n:]
    group = Group(scalars, refs, scratch, sems, True, range(4))
    group.start()
    rows = hidden.shape[0]
    valid = lax.broadcasted_iota(jnp.int32, (rows, 1), 0) < scalars[3]
    group.wait()
    branch = low(matmul(hidden[...], scratch[...]))
    adapted, inner, active = adapter_forward(branch, down[...], up[...])
    mixed_out[...] = low(jnp.where(valid, second[...] + adapted, 0.0))
    grad_result = jnp.where(valid, cotangent[...].astype(jnp.float32), 0.0)
    grad_branch[...], grad_down[...], grad_up[...] = adapter_backward(
        branch, down[...], up[...], inner, active, grad_result
    )


def ffn_back_kernel(n, scalars, grad_branch, pre, *rest):
    refs, (grad_pre, scratch, sems) = rest[:n], rest[n:]
    group = Group(scalars, refs, scratch, sems, True, range(4))
    group.start()
    group.wait()
    for b in range(4):
        at = slice(b * D, (b + 1) * D)
        grad_hidden = matmul_right_t(grad_branch[...], group.block(b))
        grad_pre[:, at] = low(gelu_slope(pre[:, at]) * grad_hidden)


def cross_back_kernel(n, scalars, grad_pre, cotangent, second, gains, queries, memory_kv, probs, *rest):
    refs, cross_refs = rest[:n], rest[n : 2 * n]
    (grad_second_out, grad_gain, pack, grad_mixed, scratch, cross_scratch, sems, cross_sems) = rest[2 * n :]
    group = Group(scalars, refs, scratch, sems, False, range(4))
    cross = Group(scalars, cross_refs, cross_scratch, cross_sems, False, (1,))
    group.start()
    cross.start()
    rows = second.shape[0]
    valid = lax.broadcasted_iota(jnp.int32, (rows, 1), 0) < scalars[3]
    grad_result = jnp.where(valid, cotangent[...].astype(jnp.float32), 0.0)
    group.wait()
    upstream = matmul_right_t(grad_pre[:, :D], group.block(0))
    for b in range(1, 4):
        upstream += matmul_right_t(grad_pre[:, b * D : (b + 1) * D], group.block(b))
    part, grad_gain[...] = norm_grad(second[...], gains[2:3], upstream)
    grad_second = grad_result + part
    grad_second_out[...] = grad_second
    grad_cross, grad_q, _ = cross_views(pack, rows)
    grad_cross[...] = low(grad_second)
    cross.wait()
    grad_mixed[...] = low(matmul_right_t(grad_cross[...], cross.block(1)))
    attend_pairs_back(queries, memory_kv, 0, memory_kv, D, probs, grad_mixed, grad_q, pack, 0, pack, D)


def cross_views(pack, rows):
    ready(pack)
    side = pack.at[:, 2 * D :]
    return side.at[:rows], side.at[rows : 2 * rows], pack.at[:, : 2 * D]


def self_back_kernel(n, scalars, cross_pack, grad_second, first, gains, branch, inner, down, up, qkv, probs, *rest):
    refs, cross_refs = rest[:n], rest[n : 2 * n]
    (grad_first_out, grad_gain, grad_down, grad_up, pack, grad_mixed, scratch, cross_scratch, sems, cross_sems) = rest[2 * n :]
    cross = Group(scalars, cross_refs, cross_scratch, cross_sems, False, (0,))
    group = Group(scalars, refs, scratch, sems, False, (3,))
    cross.start()
    group.start()
    _, grad_q, _ = cross_views(cross_pack, first.shape[0])
    cross.wait()
    upstream = matmul_right_t(grad_q[...], cross.block(0))
    part, grad_gain[...] = norm_grad(first[...], gains[1:2], upstream)
    grad_first = grad_second[...] + part
    grad_first_out[...] = grad_first
    active = low(gelu(inner[...]))
    grad_branch, grad_down[...], grad_up[...] = adapter_backward(
        branch[...], down[...], up[...], inner[...], active, grad_first
    )
    pack[:, 3 * D :] = grad_branch
    group.wait()
    grad_mixed[...] = low(matmul_right_t(grad_branch, group.block(3)))
    attend_pairs_back(qkv, qkv, D, qkv, 2 * D, probs, grad_mixed, pack, pack, D, pack, 2 * D)


def rows_product(kept, at, pairs):
    total = None
    for mine, grad in zip(kept, pairs):
        term = matmul(mine[at : at + D // 2, :], grad)
        total = term if total is None else total + term
    return total


def ffn_out_grad_kernel(n, scalars, kept, got, grad, other, *rest):
    *outs, stage, sems = rest
    blocks = Blocks(scalars, outs, stage, sems, ONE_WAY[False])
    rows, half = D // 8, D // 2
    grads = (grad[...], other[...])
    for b in range(4):
        picked = [
            jnp.concatenate([x[(1 + z) * half + b * rows : (1 + z) * half + (b + 1) * rows, :] for z in range(4)])
            for x in (kept, got)
        ]
        blocks.put(b, matmul(picked[0], grads[0]) + matmul(picked[1], grads[1]))
    blocks.finish()


def ffn_in_grad_kernel(n, scalars, kept, got, grad, other, *rest):
    *outs, stage, sems = rest
    blocks = Blocks(scalars, outs, stage, sems, ONE_WAY[True])
    for b in range(4):
        at = slice(b * D, (b + 1) * D)
        blocks.put(b, rows_product((kept, got), 0, (grad[:, at], other[:, at])))
    blocks.finish()


def cross_grads_kernel(n, scalars, kept, got, pack, other, *rest):
    *outs, stage, sems = rest
    blocks = Blocks(scalars, outs, stage, sems, ONE_WAY[True])
    half = D // 2
    rows = kept.shape[1]
    views = [cross_views(p, rows) for p in (pack, other)]
    blocks.put(0, rows_product((kept, got), 0, [v[1][...] for v in views]))
    blocks.put(1, rows_product((kept, got), half, [v[0][...] for v in views]))
    for b in range(2):
        at = slice(b * D, (b + 1) * D)
        value = rows_product((kept, got), 2 * half, [v[2][:rows, at] for v in views])
        value += rows_product((kept, got), 3 * half, [v[2][rows:, at] for v in views])
        blocks.put(2 + b, value)
    blocks.finish()


def self_grads_kernel(n, scalars, kept, got, pack, other, *rest):
    *outs, stage, sems = rest
    blocks = Blocks(scalars, outs, stage, sems, ONE_WAY[False])
    for b in range(4):
        at = slice(b * D, (b + 1) * D)
        part = D // 2 if b == 3 else 0
        blocks.put(b, rows_product((kept, got), part, (pack[:, at], other[:, at])))
    blocks.finish()


def pick_kernel(counts, scalars, *rest):
    inputs, outs = rest[:7], rest[7 : 7 + len(counts)]
    stage, sems, out_sems = rest[7 + len(counts) :]
    rows = inputs[0].shape[0]
    qkv, sout, cq, ckv, cout, f_in, f_out = inputs

    def columns(ref):
        return [ref.at[:, pl.ds(b * D, D)] for b in range(ref.shape[1] // D)]

    groups = {
        1: columns(qkv) + [sout],
        2: [cq, cout] + columns(ckv),
        3: columns(f_in),
        4: [f_out.at[pl.ds(b * rows, rows)] for b in range(4)],
    }
    used = 0
    loads = []
    for group, many in counts:
        for i in range(many):
            for b in range(4):
                copy = pltpu.make_async_copy(groups[group][b], stage.at[used], sems.at[used])
                pl.when(scalars[0] == (b ^ 3 if i else b))(copy.start)
            loads.append(copy)
            used += 1
    sent = []
    used = 0
    for (group, many), out in zip(counts, outs):
        for i in range(many):
            loads[used].wait()
            for z in range(4):
                target = out.at[z, i] if many > 1 else out.at[z]
                copy = pltpu.make_async_copy(stage.at[used], target, out_sems.at[used * 4 + z])
                copy.start()
                sent.append(copy)
            used += 1
    for copy in sent:
        copy.wait()


def pick(scalars, shards, counts):
    rows = shards[0].shape[0]
    total = sum(many for _, many in counts)
    shapes = [((4,) if many == 1 else (4, many)) + (rows, D) for _, many in counts]
    return pl.pallas_call(
        functools.partial(pick_kernel, counts),
        out_shape=[jax.ShapeDtypeStruct(shape, jnp.bfloat16) for shape in shapes],
        in_specs=[pl.BlockSpec(memory_space=pltpu.SMEM)]
        + [pl.BlockSpec(memory_space=pltpu.HBM)] * len(shards),
        out_specs=[pl.BlockSpec(memory_space=pltpu.HBM)] * len(counts),
        scratch_shapes=[
            pltpu.VMEM((total, rows, D), jnp.bfloat16),
            pltpu.SemaphoreType.DMA((total,)),
            pltpu.SemaphoreType.DMA((total * 4,)),
        ],
        compiler_params=pltpu.CompilerParams(vmem_limit_bytes=60 << 20),
        cost_estimate=pl.CostEstimate(flops=2 << 26, bytes_accessed=2 << 16, transcendentals=0),
        name="pick",
    )(scalars, *shards)


def plain_grads_kernel(n, scalars, left, right, out, sems):
    out[...] = low(matmul_left_t(left[...], right[...]))


def memory_back_kernel(n, scalars, pack, *rest):
    refs, (memory_grad, scratch, sems) = rest[:n], rest[n:]
    group = Group(scalars, refs, scratch, sems, False, (2, 3))
    group.start()
    group.wait()
    memory_grad[...] = matmul_right_t(pack[:, :D], group.block(2)) + matmul_right_t(
        pack[:, D : 2 * D], group.block(3)
    )


def token_back_kernel(n, scalars, grad_qkv, tokens, grad_first, gains, *rest):
    refs, (token_grad, grad_gain, scratch, sems) = rest[:n], rest[n:]
    group = Group(scalars, refs, scratch, sems, False, (0, 1, 2))
    group.start()
    group.wait()
    upstream = matmul_right_t(grad_qkv[:, :D], group.block(0))
    for b in range(1, 3):
        upstream += matmul_right_t(grad_qkv[:, b * D : (b + 1) * D], group.block(b))
    part, grad_gain[...] = norm_grad(tokens[...].astype(jnp.float32), gains[0:1], upstream)
    token_grad[...] = grad_first[...] + part


def nbytes(shape, kind):
    total = jnp.dtype(kind).itemsize
    for size in shape:
        total *= size
    return total


class Moved:
    def __init__(self, outer, inner, sem, is_input):
        self.inner, self.pending, self.is_input = inner, is_input, is_input
        pair = (outer, inner) if is_input else (inner, outer)
        self.copy = pltpu.make_async_copy(*pair, sem)
        if is_input:
            self.copy.start()

    def ready(self):
        if self.is_input and self.pending:
            self.copy.wait()
            self.pending = False
        return self.inner

    def send(self):
        if not self.pending:
            self.copy.start()
            self.pending = True

    def finish(self):
        if self.is_input:
            self.ready()
        else:
            self.send()
            self.copy.wait()

    @property
    def shape(self):
        return self.inner.shape

    @property
    def at(self):
        return self.ready().at

    def __getitem__(self, index):
        return self.ready()[index]

    def __setitem__(self, index, value):
        self.inner[index] = value


def send(*arrays):
    for array in arrays:
        if isinstance(array, Moved):
            array.send()


def ready(*arrays):
    for array in arrays:
        if isinstance(array, Moved):
            array.ready()


def tiled(shape):
    return shape[-1] % 128 == 0 and shape[-2] % 16 == 0


def run(kernel, name, micros, scalars, arrays, groups, outs, scratch=(), direct=False):
    n = len(groups[0]) if groups else 0
    outs, scratch = list(outs), list(scratch)
    ins = [(a.shape, a.dtype) for a in arrays]
    flat = [part for group in groups for part in group]
    moved = [pair for pair in (ins if direct else ins + outs) if tiled(pair[0])]
    spaces = scratch + [((4 * D, D), jnp.bfloat16)] * len(groups)
    need = sum(nbytes(*pair) for pair in ins + outs + spaces)

    def body(scalar_ref, *refs):
        refs = list(refs)
        inputs, parts = refs[: len(ins)], refs[len(ins) : len(ins) + len(flat)]
        results = refs[len(ins) + len(flat) :][: len(outs)]
        rest = refs[len(ins) + len(flat) + len(outs) :]
        copies, rest = rest[: len(moved)], rest[len(moved) :]
        if moved:
            sems, rest = rest[0], rest[1:]
        used = 0
        for side, pairs in ((inputs, ins), (results, [] if direct else outs)):
            for i, (shape, _) in enumerate(pairs):
                if tiled(shape):
                    side[i] = Moved(side[i], copies[used], sems.at[used], side is inputs)
                    used += 1
        kernel(n, scalar_ref, *inputs, *parts, *results, *rest)
        for array in inputs + results:
            if isinstance(array, Moved):
                array.finish()

    def spec(shape):
        return pl.BlockSpec(memory_space=pltpu.HBM if tiled(shape) else pltpu.VMEM)

    return pl.pallas_call(
        body,
        out_shape=[jax.ShapeDtypeStruct(shape, kind) for shape, kind in outs],
        in_specs=[pl.BlockSpec(memory_space=pltpu.SMEM)]
        + [spec(shape) for shape, _ in ins]
        + [pl.BlockSpec(memory_space=pltpu.HBM)] * len(flat),
        out_specs=[spec(shape) for shape, _ in outs],
        scratch_shapes=[pltpu.VMEM(shape, kind) for shape, kind in moved]
        + ([pltpu.SemaphoreType.DMA((len(moved),))] if moved else [])
        + [pltpu.VMEM(shape, kind) for shape, kind in spaces]
        + [pltpu.SemaphoreType.DMA((32,)) for _ in (groups or [None])],
        compiler_params=pltpu.CompilerParams(vmem_limit_bytes=60 << 20),
        cost_estimate=pl.CostEstimate(
            flops=int(micros * 1e8), bytes_accessed=int(micros * 1e5), transcendentals=0
        ),
        name=name,
    )(scalars, *arrays, *flat)


def moves(step):
    pairs = []
    for y in range(2):
        for x in range(2):
            for z in range(4):
                for c in range(2):
                    ty, tx, tz, tc = step(y, x, z, c)
                    pairs.append((((y * 2 + x) * 4 + z) * 2 + c, ((ty * 2 + tx) * 4 + tz) * 2 + tc))
    return pairs


def swap_x(values):
    return lax.ppermute(values, BOTH, moves(lambda y, x, z, c: (y, 1 - x, z, c)))


def swap_y(values):
    return lax.ppermute(values, BOTH, moves(lambda y, x, z, c: (1 - y, x, z, c)))


def swap_core(values):
    return lax.ppermute(values, BOTH, moves(lambda y, x, z, c: (y, x, z, 1 - c)))


def turn_z(values, by):
    return lax.ppermute(values, BOTH, moves(lambda y, x, z, c: (y, x, (z + by) % 4, c)))


def after(value, *marks):
    return lax.optimization_barrier((value,) + marks)[0]


LINES = [[z * 2 + c for z in range(4)] for c in range(2)]


def spread_z(values):
    return lax.all_to_all(
        values, "fsdp", split_axis=0, concat_axis=0, tiled=True, axis_index_groups=LINES
    )


def copy_z(value, *marks):
    return spread_z(after(jnp.broadcast_to(value[None], (4,) + value.shape), *marks))


def sum_z(values):
    return jnp.sum(spread_z(values).astype(jnp.float32), axis=0)


class Layer:
    def __init__(self, scalars, tokens, memory, cotangent, staged):
        self.scalars, self.tokens, self.memory, self.cotangent = scalars, tokens, memory, cotangent
        self.staged = staged
        self.t, self.m = tokens.shape[0], memory.shape[0]

    def hold(self, *marks):
        self.scalars = after(self.scalars, *marks)

    def adapters(self, generated):
        block, start = D * ADAPT, 3 * D
        self.gains = 1.0 + 0.25 * generated[:start].astype(jnp.float32).reshape(3, D)
        self.down_1 = generated[start : start + block].reshape(D, ADAPT)
        self.up_1 = generated[start + block : start + 2 * block].reshape(ADAPT, D)
        self.down_2 = generated[start + 2 * block : start + 3 * block].reshape(D, ADAPT)
        self.up_2 = generated[start + 3 * block : start + 4 * block].reshape(ADAPT, D)

    def rows(self, width=D, kind=jnp.bfloat16):
        return ((self.t, width), kind)

    def wide(self, width=D):
        return self.rows(width, jnp.float32)

    def halves(self, count):
        return [((count * (D // 2), self.t), jnp.bfloat16)] * 2

    def self_forward(self, w1):
        local = [self.rows(), self.rows()]
        outs = run(
            self_forward_kernel,
            "self_forward",
            11,
            self.scalars,
            [self.tokens, self.gains, self.down_1, self.up_1],
            [w1],
            [
                self.rows(3 * D),
                ((HEADS, self.t, self.t), jnp.bfloat16),
                self.rows(),
                self.wide(ADAPT),
                self.wide(),
                self.rows(),
            ]
            + (self.halves(2) if self.staged else local),
            scratch=local if self.staged else [],
        )
        self.qkv, self.probs_1, self.branch_1, self.inner_1, self.first, self.normed_2 = outs[:6]
        self.saved_1 = outs[6:]

    def cross_forward(self, w2):
        local = [self.rows()]
        outs = run(
            cross_forward_kernel,
            "cross_forward",
            15,
            self.scalars,
            [self.normed_2, self.first, self.memory, self.gains],
            [w2],
            [
                self.rows(),
                ((self.m, 2 * D), jnp.bfloat16),
                ((HEADS, self.m, self.t), jnp.bfloat16),
                self.wide(),
                self.rows(),
            ]
            + (self.halves(4) if self.staged else local),
            scratch=local if self.staged else [],
        )
        self.queries, self.memory_kv, self.probs_2, self.second, self.normed_3 = outs[:5]
        self.saved_2 = outs[5:]

    def ffn_in(self, w3):
        outs = run(
            ffn_in_kernel,
            "ffn_in",
            6,
            self.scalars,
            [self.normed_3],
            [w3],
            [self.wide(4 * D), self.rows(4 * D)] + (self.halves(5) if self.staged else []),
        )
        self.pre, self.hidden = outs[:2]
        self.saved_3 = outs[2:]

    def adapter_outs(self):
        return [((D, ADAPT), jnp.float32), ((ADAPT, D), jnp.float32)]

    def ffn_out(self, w4):
        self.mixed_out, self.grad_branch, self.grad_down_2, self.grad_up_2 = run(
            ffn_out_kernel,
            "ffn_out",
            8,
            self.scalars,
            [self.hidden, self.second, self.cotangent, self.down_2, self.up_2],
            [w4],
            [self.rows(), self.rows()] + self.adapter_outs(),
        )

    def ffn_back(self, w4):
        (self.grad_pre,) = run(
            ffn_back_kernel,
            "ffn_back",
            8,
            self.scalars,
            [self.grad_branch, self.pre],
            [w4],
            [self.rows(4 * D)],
        )

    def cross_back(self, w3, w2):
        self.grad_second, self.grad_gain_3, self.cross_pack = run(
            cross_back_kernel,
            "cross_back",
            15,
            self.scalars,
            [
                self.grad_pre,
                self.cotangent,
                self.second,
                self.gains,
                self.queries,
                self.memory_kv,
                self.probs_2,
            ],
            [w3, w2],
            [self.wide(), ((1, D), jnp.float32), ((self.m, 3 * D), jnp.bfloat16)],
            scratch=[self.rows()],
        )

    def self_back(self, w1, w2):
        self.grad_first, self.grad_gain_2, self.grad_down_1, self.grad_up_1, self.self_pack = run(
            self_back_kernel,
            "self_back",
            11,
            self.scalars,
            [
                self.cross_pack,
                self.grad_second,
                self.first,
                self.gains,
                self.branch_1,
                self.inner_1,
                self.down_1,
                self.up_1,
                self.qkv,
                self.probs_1,
            ],
            [w1, w2],
            [self.wide(), ((1, D), jnp.float32)] + self.adapter_outs() + [self.rows(4 * D)],
            scratch=[self.rows()],
        )

    def token_back(self, w1):
        self.token_grad, self.grad_gain_1 = run(
            token_back_kernel,
            "token_back",
            5,
            self.scalars,
            [self.self_pack, self.tokens, self.grad_first, self.gains],
            [w1],
            [self.wide(), ((1, D), jnp.float32)],
        )

    def memory_back(self, w2):
        (self.memory_grad,) = run(
            memory_back_kernel,
            "memory_back",
            6,
            self.scalars,
            [self.cross_pack],
            [w2],
            [((self.m, D), jnp.float32)],
        )

    def block_grads(self, kernel, name, ways, kept, got, grad, other):
        stage = ((4, 4, D // 8, D), jnp.bfloat16)
        shapes = [((2, z1 - z0, D // 8, D), jnp.bfloat16) for _, z0, z1 in ways for _ in range(2)]
        outs = run(kernel, name, 5, self.scalars, [kept, got, grad, other], [], shapes, [stage], direct=True)
        return [(way[0], outs[2 * i], outs[2 * i + 1]) for i, way in enumerate(ways)]

    def plain_grads(self, left, right):
        (out,) = run(
            plain_grads_kernel,
            "plain_grads",
            5,
            self.scalars,
            [left, right],
            [],
            [((left.shape[1], right.shape[1]), jnp.bfloat16)],
        )
        return out

    def grad_generated(self):
        return low(
            jnp.concatenate(
                [
                    0.25 * self.grad_gain_1,
                    0.25 * self.grad_gain_2,
                    0.25 * self.grad_gain_3,
                    self.grad_down_1.reshape(ADAPT, D),
                    self.grad_up_1,
                    self.grad_down_2.reshape(ADAPT, D),
                    self.grad_up_2,
                ]
            )
        ).reshape(-1)


def staged_layer(layer, where, task_ids, hidden_all, hyper_gen, shards):
    q, z, c = where[0], where[1], where[2]

    own_1, own_2, own_3, own_4 = pick(where, shards, [(1, 1), (2, 1), (3, 2), (4, 2)])
    column_1 = spread_z(own_1)
    ids = jnp.stack([task_ids, swap_core(task_ids)])
    ids_ahead = [ids] + [turn_z(ids, 4 - k) for k in (1, 2, 3)]
    gen_shard = low(matmul(hidden_all, hyper_gen))
    near_x_1, near_y_1 = swap_x(column_1), swap_y(column_1)

    def rows_of(tasks):
        select = low(tasks[:, 0:1] == jnp.arange(TASKS, dtype=jnp.int32)[None, :])
        return after(low(matmul(select, gen_shard)), column_1)

    asked = [rows_of(tasks) for tasks in ids_ahead]
    turned = [turn_z(asked[k], k) for k in (1, 2, 3)]
    got = jnp.stack([asked[0]] + turned, axis=1)
    pieces = jnp.concatenate([got[0], swap_core(got[1])])
    slots = jnp.arange(8, dtype=jnp.int32)
    source = ((slots % 2) ^ c) * 4 + (z - slots // 2 + 4) % 4
    unturn = low(source[:, None] == slots[None, :])
    layer.adapters(low(matmul(unturn, pieces)).reshape(-1))

    column_2 = spread_z(after(own_2, *turned))
    far_1 = swap_y(near_x_1)
    w1 = [column_1, near_x_1, near_y_1, far_1]
    w1 += [swap_core(after(part, near_x_1)) for part in w1]

    def second_stage(pair, *marks):
        column = after(pair, *marks)[:, 0]
        return [column, swap_x(column), swap_y(column), pair[:, 1]]

    def third_stage(parts, *marks):
        return parts + [swap_core(after(part, *marks)) for part in parts]

    w2 = [column_2, swap_x(column_2), swap_y(column_2)]
    pair_3 = spread_z(after(own_3, column_2))
    layer.hold(column_2)
    layer.self_forward(w1)
    w2.append(swap_x(after(w2[2], layer.normed_2)))
    w2 = third_stage(w2, layer.normed_2)
    got_1 = swap_core(layer.saved_1[1])
    w3 = second_stage(pair_3, layer.normed_2)
    pair_4 = spread_z(after(own_4, w3[0]))
    layer.hold(got_1, w3[0])
    layer.cross_forward(w2)
    got_2 = swap_core(layer.saved_2[1])
    w3 = third_stage(w3, layer.normed_3)
    layer.hold(got_2)
    layer.ffn_in(w3)
    w4 = second_stage(pair_4, layer.hidden)
    got_3 = swap_core(layer.saved_3[1])
    w4 = third_stage(w4, layer.hidden)
    layer.hold(got_3)
    layer.ffn_out(w4)

    def first_way(parts):
        return [(x_first, home, (swap_x if x_first else swap_y)(away)) for x_first, home, away in parts]

    def second_way(parts, *marks):
        sums = []
        for x_first, home, got in parts:
            home = after(home, *marks)
            leaving = add_low(home[1], got[1])
            sums.append((home, got, leaving, (swap_y if x_first else swap_x)(leaving)))
        return sums

    def third_way(sums, *marks):
        rows = []
        for home, first, _, second in sums:
            terms = [part.astype(jnp.float32) for part in (after(home, *marks)[0], first[0], second)]
            rows.append(low(terms[0] + terms[1] + terms[2]))
        return jnp.concatenate(rows) if len(rows) > 1 else rows[0]

    def own_rows(values):
        return jnp.sum(spread_z(values).astype(jnp.float32), axis=0)

    other = swap_core(layer.grad_branch)
    s4 = first_way(
        layer.block_grads(
            ffn_out_grad_kernel,
            "ffn_out_grad",
            ONE_WAY[False],
            layer.saved_3[0],
            got_3,
            layer.grad_branch,
            other,
        )
    )
    layer.hold(s4[0][1])
    layer.ffn_back(w4)
    other_pre = swap_core(layer.grad_pre)
    s3 = first_way(
        layer.block_grads(
            ffn_in_grad_kernel,
            "ffn_in_grad",
            ONE_WAY[True],
            layer.saved_3[0],
            got_3,
            layer.grad_pre,
            other_pre,
        )
    )
    layer.hold(s3[0][1])
    layer.cross_back(w3, w2)
    other = swap_core(layer.cross_pack)
    s4 = second_way(s4, layer.cross_pack)
    layer.hold(s4[0][2])
    layer.self_back(w1, w2)
    other_self = swap_core(layer.self_pack)
    s3 = second_way(s3, layer.self_pack)
    layer.hold(s3[0][2])
    s2 = first_way(
        layer.block_grads(
            cross_grads_kernel,
            "cross_grads",
            ONE_WAY[True],
            layer.saved_2[0],
            got_2,
            layer.cross_pack,
            other,
        )
    )
    sent_4 = spread_z(third_way(s4, s2[0][1]))
    layer.hold(s2[0][1])
    s1 = first_way(
        layer.block_grads(
            self_grads_kernel,
            "self_grads",
            ONE_WAY[False],
            layer.saved_1[0],
            got_1,
            layer.self_pack,
            other_self,
        )
    )
    layer.hold(s1[0][1])
    layer.token_back(w1)
    sent_3 = spread_z(after(third_way(s3, layer.token_grad), sent_4))
    layer.hold(layer.token_grad, sent_4)
    layer.memory_back(w2)
    s2 = second_way(s2, layer.memory_grad)
    own_4 = jnp.sum(after(sent_4, layer.memory_grad).astype(jnp.float32), axis=0)
    own_3 = jnp.sum(sent_3.astype(jnp.float32), axis=0)

    pieces = after(layer.grad_generated(), layer.memory_grad).reshape(8, -1)
    terms = lax.all_to_all(pieces, "fsdp", split_axis=0, concat_axis=0, tiled=True)
    slots = jnp.arange(8, dtype=jnp.int32)
    ids = jnp.concatenate(ids_ahead)[:, 0]
    turn = ((slots // 2 - z + 4) % 4) * 2 + ((slots % 2) ^ c)
    ids = jnp.sum(jnp.where(turn[:, None] == slots[None, :], ids[None, :], 0), axis=1)
    select = low(jnp.arange(TASKS, dtype=jnp.int32)[:, None] == ids[None, :])
    task_grad = low(matmul(select, terms))
    task_grad = add_low(task_grad, swap_x(task_grad))
    task_grad = task_grad.astype(jnp.float32) + swap_y(task_grad).astype(jnp.float32)

    def sum_owners(part):
        got = copy_z(part + swap_core(after(part, last)))
        return (got[0] + got[1]) + (got[2] + got[3])

    def share(owns):
        own = low(jnp.stack(owns))
        pair = jnp.stack([own, swap_x(own)])
        quad = jnp.concatenate([pair, swap_y(pair)])
        return [
            [lax.dynamic_index_in_dim(quad, q ^ b, 0, keepdims=False)[i].astype(jnp.float32) for b in range(4)]
            for i in range(len(owns))
        ]

    s1 = second_way(s1, s2[0][2])
    last = spread_z(jnp.stack([third_way(s2), third_way(s1)], axis=1))
    own_2, own_1 = jnp.sum(last.astype(jnp.float32), axis=0)
    g3, g4 = share([own_3, own_4])
    g2, g1 = share([own_2, own_1])
    summed = (
        jnp.concatenate(g1[:3], axis=1),
        g1[3],
        g2[0],
        jnp.concatenate(g2[2:], axis=1),
        g2[1],
        jnp.concatenate(g3, axis=1),
        jnp.concatenate(g4, axis=0),
    )
    return summed, task_grad, sum_owners


def plain_layer(layer, task_ids, hidden_all, hyper_gen, groups):
    owners = lax.axis_size("fsdp")

    def whole(shard):
        return lax.all_gather(shard, "fsdp", axis=0, tiled=True)

    w1, w2, w3 = ([jnp.concatenate([whole(block) for block in blocks])] for blocks in groups[:3])
    w4 = [whole(jnp.concatenate(groups[3]))]
    select = low(task_ids[:, None] == jnp.arange(TASKS, dtype=jnp.int32)[None, :])
    gen_shard = low(matmul(hidden_all, hyper_gen))
    gen_tasks = lax.all_gather(gen_shard, "fsdp", axis=1, tiled=True)
    layer.adapters(low(matmul(select, gen_tasks)[0]))
    layer.self_forward(w1)
    layer.cross_forward(w2)
    layer.ffn_in(w3)
    layer.ffn_out(w4)
    layer.ffn_back(w4)
    layer.cross_back(w3, w2)
    layer.self_back(w1, w2)
    layer.token_back(w1)
    layer.memory_back(w2)

    def owned(left, right):
        part = low(lax.psum_scatter(layer.plain_grads(left, right), "fsdp", scatter_dimension=0, tiled=True))
        return lax.psum(part, "dp").astype(jnp.float32)

    t = layer.t
    pack = layer.cross_pack
    summed = (
        owned(layer.saved_1[0], layer.self_pack[:, : 3 * D]),
        owned(layer.saved_1[1], layer.self_pack[:, 3 * D :]),
        owned(layer.normed_2, pack[t : 2 * t, 2 * D :]),
        owned(layer.memory, pack[:, : 2 * D]),
        owned(layer.saved_2[0], pack[:t, 2 * D :]),
        owned(layer.normed_3, layer.grad_pre),
        owned(layer.hidden, layer.grad_branch),
    )
    pieces = layer.grad_generated().reshape(owners, 1, -1)
    select = low(jnp.arange(TASKS, dtype=jnp.int32)[:, None] == task_ids[None, :])
    terms = low(select[None].astype(jnp.float32) * pieces.astype(jnp.float32))
    terms = lax.all_to_all(terms, "fsdp", split_axis=0, concat_axis=0, tiled=True)
    task_grad = low(jnp.sum(terms.astype(jnp.float32), axis=0))
    task_grad = lax.psum(task_grad, "dp").astype(jnp.float32)
    return summed, task_grad, lambda part: lax.psum(part, "fsdp")


def hyper_tail(task_grad, pre_all, hidden_all, task_table, hyper_in, hyper_gen, sum_owners):
    grad_hyper_gen = jnp.dot(
        hidden_all.astype(jnp.float32).T, task_grad, precision=lax.Precision.HIGHEST
    )
    grad_hidden = jnp.dot(
        task_grad, hyper_gen.astype(jnp.float32).T, precision=lax.Precision.HIGHEST
    )
    grad_pre_all = gelu_slope(pre_all) * sum_owners(grad_hidden)
    grad_table = jnp.dot(grad_pre_all, hyper_in.T, precision=lax.Precision.HIGHEST)
    grad_first = jnp.dot(task_table.T, grad_pre_all, precision=lax.Precision.HIGHEST)
    return grad_table, grad_first, grad_hyper_gen


def shards(
    tokens,
    memory,
    target_lengths,
    memory_lengths,
    task_ids,
    cotangent,
    self_qkv,
    self_out,
    cross_q,
    cross_kv,
    cross_out,
    ffn_in,
    ffn_out,
    task_table,
    hyper_in,
    hyper_gen,
):
    staged = lax.axis_size("fsdp") == 8 and lax.axis_size("dp") == 4
    pre_all = jnp.dot(task_table, hyper_in, precision=lax.Precision.HIGHEST)
    hidden_all = low(jax.nn.gelu(pre_all))

    def columns(shard):
        return [shard[:, b * D : (b + 1) * D] for b in range(shard.shape[1] // D)]

    q = lax.axis_index("dp").astype(jnp.int32)
    f = lax.axis_index("fsdp").astype(jnp.int32)
    where = jnp.stack([q, f // 2, f % 2])
    scalars = jnp.concatenate([where, target_lengths, memory_lengths])
    layer = Layer(scalars, tokens, memory, cotangent, staged)
    if staged:
        summed, task_grad, sum_owners = staged_layer(
            layer,
            where,
            task_ids,
            hidden_all,
            hyper_gen,
            (self_qkv, self_out, cross_q, cross_kv, cross_out, ffn_in, ffn_out),
        )
    else:
        rows = self_qkv.shape[0]
        groups = (
            columns(self_qkv) + [self_out],
            [cross_q, cross_out] + columns(cross_kv),
            columns(ffn_in),
            [ffn_out[b * rows : (b + 1) * rows] for b in range(4)],
        )
        summed, task_grad, sum_owners = plain_layer(layer, task_ids, hidden_all, hyper_gen, groups)
    grad_table, grad_first, grad_hyper_gen = hyper_tail(
        task_grad, pre_all, hidden_all, task_table, hyper_in, hyper_gen, sum_owners
    )
    return (
        (layer.mixed_out, layer.token_grad, layer.memory_grad)
        + summed
        + (grad_table, grad_first, grad_hyper_gen)
    )


def solution(mesh):
    by_both = P(("dp", "fsdp"), None)
    by_rows = P("fsdp", None)
    return jax.shard_map(
        shards,
        mesh=mesh,
        in_specs=(by_both, by_both)
        + (P(("dp", "fsdp")),) * 3
        + (by_both,)
        + (by_rows,) * 7
        + (P(), P(), P(None, "fsdp")),
        out_specs=(by_both,) * 3 + (by_rows,) * 7 + (P(), P(), P(None, "fsdp")),
        check_vma=False,
    )
```

```python
import functools

import jax
import jax.numpy as jnp
from jax import lax
from jax.experimental import pallas as pl
from jax.experimental.pallas import tpu as pltpu
from jax.sharding import PartitionSpec as P

D = 768
HEADS = 12
HEAD = 64
ADAPT = 24
TASKS = 8
BOTH = ("dp", "fsdp")


def matmul(left, right):
    return jnp.dot(left, right, preferred_element_type=jnp.float32)


def matmul_left_t(left, right):
    return lax.dot_general(
        left, right, (((0,), (0,)), ((), ())), preferred_element_type=jnp.float32
    )


def matmul_right_t(left, right):
    return lax.dot_general(
        left, right, (((1,), (1,)), ((), ())), preferred_element_type=jnp.float32
    )


def low(values):
    return values.astype(jnp.bfloat16)


def add_low(left, right):
    return low(left.astype(jnp.float32) + right.astype(jnp.float32))


def rms_factor(values):
    return lax.rsqrt(jnp.mean(values * values, axis=-1, keepdims=True) + 1e-06)


def norm_grad(values, gains, upstream):
    factor = rms_factor(values)
    scaled = upstream * gains
    mean = jnp.mean(values * scaled, axis=-1, keepdims=True)
    part = factor * scaled - values * (factor * factor * factor * mean)
    return part, jnp.sum(upstream * values * factor, axis=0, keepdims=True)


GELU_A = 0.7978845608
GELU_B = 0.044715


def gelu(values):
    inside = GELU_A * (values + GELU_B * values * values * values)
    return 0.5 * values * (1.0 + jnp.tanh(inside))


def gelu_both(values):
    square = values * values
    curve = jnp.tanh(GELU_A * (values + GELU_B * square * values))
    inner = GELU_A * (1.0 + 3.0 * GELU_B * square)
    half = 0.5 * (1.0 + curve)
    return values * half, half + 0.5 * values * (1.0 - curve * curve) * inner


def gelu_slope(values):
    square = values * values
    curve = jnp.tanh(GELU_A * (values + GELU_B * square * values))
    inner = GELU_A * (1.0 + 3.0 * GELU_B * square)
    return 0.5 * (1.0 + curve) + 0.5 * values * (1.0 - curve * curve) * inner


class Group:
    def __init__(self, scalars, refs, scratch, sems, by_block, blocks=(0, 1, 2, 3)):
        self.scalars, self.refs, self.scratch, self.sems = scalars, refs, scratch, sems
        self.by_block, self.blocks = by_block, blocks
        self.staged = len(refs) > 1
        self.waited = False

    def _each(self, act, part=None):
        if not self.staged:
            act(pltpu.make_async_copy(self.refs[0], self.scratch, self.sems.at[0]))
            return
        q, c = self.scalars[0], self.scalars[2]
        for r in range(4):
            block = q ^ r

            def parts(r=r, block=block):
                for side in range(2):
                    source = self.refs[side * 4 + r]
                    if self.by_block and part in (None, r):
                        target = self.scratch.at[r, :, c ^ side]
                        act(pltpu.make_async_copy(source, target, self.sems.at[r * 2 + side]))
                    if not self.by_block:
                        for half in range(2):
                            if part in (None, half):
                                at = pl.ds(half * 2, 2)
                                act(
                                    pltpu.make_async_copy(
                                        source.at[at],
                                        self.scratch.at[at, c ^ side, block],
                                        self.sems.at[(r * 2 + side) * 2 + half],
                                    )
                                )

            if len(self.blocks) == 4:
                parts()
            else:
                wanted = block == self.blocks[0]
                for other in self.blocks[1:]:
                    wanted = wanted | (block == other)
                pl.when(wanted)(parts)

    def start(self):
        self._each(lambda copy: copy.start())

    def wait(self, part=None):
        if self.staged:
            self._each(lambda copy: copy.wait(), part)
        elif not self.waited:
            self._each(lambda copy: copy.wait())
            self.waited = True

    def wait_block(self, index):
        if not self.staged:
            self.wait()
            return
        r, c = self.scalars[0] ^ index, self.scalars[2]
        for side in range(2):
            target = self.scratch.at[r, :, c ^ side]
            pltpu.make_async_copy(self.refs[0], target, self.sems.at[r * 2 + side]).wait()

    def place(self, r):
        return self.scratch[r].reshape(D, D)

    def which(self, r):
        return self.scalars[0] ^ r if self.staged else r

    def block(self, index):
        return self.scratch[self.scalars[0] ^ index if self.staged else index].reshape(D, D)

    def quarter(self, z):
        return self.scratch[z].reshape(D, D)


def columns_at(block):
    return pl.ds(pl.multiple_of(block * D, D), D)


def part_rows(scalars, value, keep, send, at):
    flat = value.T
    rows = flat.shape[0] // 8
    for parity in range(2):
        here = scalars[2] == parity

        @pl.when(here)
        def _():
            for z in range(4):
                piece = flat[(z * 2 + parity) * rows : (z * 2 + parity + 1) * rows]
                keep[at + z * rows : at + (z + 1) * rows, :] = piece

        @pl.when(jnp.logical_not(here))
        def _():
            for z in range(4):
                piece = flat[(z * 2 + parity) * rows : (z * 2 + parity + 1) * rows]
                send[at + z * rows : at + (z + 1) * rows, :] = piece


class Blocks:
    def __init__(self, scalars, outs, stage, sems):
        self.scalars, self.outs, self.stage, self.sems = scalars, outs, stage, sems
        self.sent = []

    def put(self, block, value):
        rows = value.shape[0] // 4
        value = low(value)
        for z in range(4):
            self.stage[block, z] = value[z * rows : (z + 1) * rows]
        r, c = self.scalars[0] ^ block, self.scalars[2]
        first = jnp.where(c == 0, r % 2, r // 2)
        second = jnp.where(c == 0, r // 2, r % 2)
        for way, out in enumerate(self.outs):
            copy = pltpu.make_async_copy(self.stage.at[block], out.at[second], self.sems.at[block * 2 + way])
            pl.when(first == way)(copy.start)
            self.sent.append((first == way, copy))

    def finish(self):
        for here, copy in self.sent:
            pl.when(here)(copy.wait)


def head_lanes(rows, head):
    lane = lax.broadcasted_iota(jnp.int32, (rows, 128), 1)
    return lane < HEAD if head == 0 else lane >= HEAD


def pick_head(values, head):
    return jnp.where(head_lanes(values.shape[0], head), values, jnp.zeros_like(values))


def attend_pairs(q_ref, k_ref, k_at, v_ref, v_at, bias, probs, mixed):
    ready(q_ref, k_ref, v_ref)

    def scores_of(pair):
        at = pair * 128
        queries = q_ref[:, at : at + 128]
        keys = k_ref[:, k_at + at : k_at + at + 128]
        return [matmul_right_t(pick_head(keys, head), queries) for head in range(2)]

    def weights_of(scores):
        scores = scores + bias
        weights = jnp.exp(scores - jnp.max(scores, axis=0, keepdims=True))
        return low(weights * (1.0 / jnp.sum(weights, axis=0, keepdims=True)))

    def finish(at, values, weights):
        halves = [matmul(values[head * HEAD : (head + 1) * HEAD], weights[head]) for head in range(2)]
        mixed[:, at : at + 128] = low(jnp.concatenate(halves, axis=0).T)

    ahead = scores_of(0)
    for pair in range(HEADS // 2):
        both, ahead = ahead, scores_of(pair + 1) if pair + 1 < HEADS // 2 else None
        at = pair * 128
        values = v_ref[:, v_at + at : v_at + at + 128].T
        weights = [weights_of(scores) for scores in both]
        for head in range(2):
            probs[pair * 2 + head] = weights[head]
        if pair:
            finish(*pending)
        pending = (at, values, weights)
    finish(*pending)


def attend_pairs_back(q_ref, k_ref, k_at, v_ref, v_at, probs, grad_mixed, grad_q, grad_k, gk_at, grad_v, gv_at):
    ready(q_ref, k_ref, v_ref, probs)

    def grad_weights(pair):
        at = pair * 128
        values = v_ref[:, v_at + at : v_at + at + 128]
        grads = grad_mixed[:, at : at + 128]
        return [matmul_right_t(pick_head(values, head), grads) for head in range(2)]

    def finish(at, weights, grad_s):
        queries = q_ref[:, at : at + 128]
        keys = k_ref[:, k_at + at : k_at + at + 128]
        grads = grad_mixed[:, at : at + 128]
        keys_t = keys.T
        part_v = [matmul(weights[head], grads) for head in range(2)]
        part_k = [matmul(grad_s[head], queries) for head in range(2)]
        halves = [matmul(keys_t[head * HEAD : (head + 1) * HEAD], grad_s[head]) for head in range(2)]
        first = head_lanes(keys.shape[0], 0)
        grad_q[:, at : at + 128] = low(jnp.concatenate(halves, axis=0).T * HEAD ** (-0.5))
        grad_k[:, gk_at + at : gk_at + at + 128] = low(jnp.where(first, part_k[0], part_k[1]))
        grad_v[:, gv_at + at : gv_at + at + 128] = low(jnp.where(first, part_v[0], part_v[1]))

    ahead = grad_weights(0)
    for pair in range(HEADS // 2):
        both, ahead = ahead, grad_weights(pair + 1) if pair + 1 < HEADS // 2 else None
        weights = [probs[pair * 2 + head] for head in range(2)]
        grad_s = []
        for head in range(2):
            wide = weights[head].astype(jnp.float32)
            total = jnp.sum(both[head] * wide, axis=0, keepdims=True)
            grad_s.append(low(wide * (both[head] - total)))
        if pair:
            finish(*pending)
        pending = (pair * 128, weights, grad_s)
    finish(*pending)


def adapter_forward(branch, down, upward):
    inner = matmul(branch, down) * D ** (-0.5)
    active = low(gelu(inner))
    return branch.astype(jnp.float32) + matmul(active, upward) * ADAPT ** (-0.5), inner, active


def adapter_backward(branch, down, upward, inner, active, grad_out):
    grad_low = low(grad_out)
    grad_up = matmul_left_t(active, grad_low) * ADAPT ** (-0.5)
    grad_active = matmul_right_t(grad_low, upward) * ADAPT ** (-0.5)
    grad_inner = low(gelu_slope(inner) * grad_active)
    grad_down = matmul_left_t(branch, grad_inner) * D ** (-0.5)
    grad_branch = low(grad_out + matmul_right_t(grad_inner, down) * D ** (-0.5))
    return grad_branch, grad_down, grad_up


def self_forward_kernel(n, scalars, tokens, gains, down, up, *rest):
    refs, (qkv, probs, branch, inner_out, first_out, normed_cross, *saved, scratch, sems) = rest[: n[0]], rest[n[0] :]
    *halves, normed, mixed = saved
    group = Group(scalars, refs, scratch, sems, True)
    fetch(tokens, group)
    inputs = tokens[...].astype(jnp.float32)
    normed[...] = low(inputs * rms_factor(inputs) * gains[0:1])
    rows = inputs.shape[0]
    key = lax.broadcasted_iota(jnp.int32, (rows, rows), 0)
    query = lax.broadcasted_iota(jnp.int32, (rows, rows), 1)
    bias = jnp.where((key <= query) & (key < scalars[3]), 0.0, -1e30)
    if halves:
        part_rows(scalars, normed[...], *halves, 0)
    for b in range(3):
        group.wait_block(b)
        product = matmul(normed[...], group.block(b))
        qkv[:, b * D : (b + 1) * D] = low(product) * (HEAD ** (-0.5) if b == 0 else 1.0)
    send(qkv)
    attend_pairs(qkv, qkv, D, qkv, 2 * D, bias, probs, mixed)
    send(probs)
    group.wait_block(3)
    branch[...] = low(matmul(mixed[...], group.block(3)))
    adapted, inner, _ = adapter_forward(branch[...], down[...], up[...])
    inner_out[...] = inner
    first = inputs + adapted
    first_out[...] = first
    normed_cross[...] = low(first * rms_factor(first) * gains[1:2])
    send(branch, first_out, normed_cross)
    if halves:
        part_rows(scalars, mixed[...], *halves, D // 2)


def cross_forward_kernel(n, scalars, normed, first, memory, gains, *rest):
    refs, (queries, memory_kv, probs, second_out, normed_ffn, *saved, scratch, sems) = rest[: n[0]], rest[n[0] :]
    *halves, mixed = saved
    group = Group(scalars, refs, scratch, sems, True)
    fetch(memory, normed, group, first)
    slot = lax.broadcasted_iota(jnp.int32, (memory.shape[0], 1), 0)
    bias = jnp.where(slot < scalars[4], 0.0, -1e30)
    if halves:
        part_rows(scalars, normed[...], *halves, 0)
        half = memory.shape[0] // 2
        for i in range(2):
            part_rows(scalars, memory[i * half : (i + 1) * half, :], *halves, (2 + i) * (D // 2))
    group.wait()
    queries[...] = low(matmul(normed[...], group.block(0))) * HEAD ** (-0.5)
    for b in range(2):
        memory_kv[:, b * D : (b + 1) * D] = low(matmul(memory[...], group.block(2 + b)))
    send(queries, memory_kv)
    attend_pairs(queries, memory_kv, 0, memory_kv, D, bias, probs, mixed)
    send(probs)
    second = first[...] + matmul(mixed[...], group.block(1))
    second_out[...] = second
    normed_ffn[...] = low(second * rms_factor(second) * gains[2:3])
    send(second_out, normed_ffn)
    if halves:
        part_rows(scalars, mixed[...], *halves, D // 2)


def ffn_in_kernel(n, scalars, normed, *rest):
    refs, (slope, hidden, *halves, scratch, sems) = rest[: n[0]], rest[n[0] :]
    group = Group(scalars, refs, scratch, sems, True)
    fetch(normed, group)
    if halves:
        part_rows(scalars, normed[...], *halves, 0)
    ahead = None
    for b in range(5):
        product = ahead
        if b < 4:
            group.wait_block(b)
            ahead = matmul(normed[...], group.block(b))
        if b:
            at = slice((b - 1) * D, b * D)
            hidden_b, slope_b = gelu_both(product)
            hidden_b = low(hidden_b)
            slope[:, at] = low(slope_b)
            hidden[:, at] = hidden_b
            send_part(b - 1, slope, hidden)
            if halves:
                flat, half = hidden_b.T, D // 2
                to = slice(b * half, (b + 1) * half)
                even = scalars[2] == 0
                halves[0][to, :] = jnp.where(even, flat[:half], flat[half:])
                halves[1][to, :] = jnp.where(even, flat[half:], flat[:half])


def ffn_out_kernel(n, scalars, hidden, second, cotangent, down, up, *rest):
    refs, (mixed_out, grad_branch, grad_down, grad_up, scratch, sems) = rest[: n[0]], rest[n[0] :]
    group = Group(scalars, refs, scratch, sems, False)
    fetch(hidden, group, second, cotangent)
    rows = hidden.shape[0]
    valid = lax.broadcasted_iota(jnp.int32, (rows, 1), 0) < scalars[3]
    product = None
    for z in range(4):
        if z % 2 == 0:
            group.wait(z // 2)
        term = matmul(hidden[:, z * D : (z + 1) * D], group.quarter(z))
        product = term if product is None else product + term
    branch = low(product)
    adapted, inner, active = adapter_forward(branch, down[...], up[...])
    mixed_out[...] = low(jnp.where(valid, second[...] + adapted, 0.0))
    send(mixed_out)
    grad_result = jnp.where(valid, cotangent[...].astype(jnp.float32), 0.0)
    grad_branch[...], grad_down[...], grad_up[...] = adapter_backward(
        branch, down[...], up[...], inner, active, grad_result
    )


def ffn_back_kernel(n, scalars, grad_branch, slope, *rest):
    refs, (grad_pre, scratch, sems) = rest[: n[0]], rest[n[0] :]
    group = Group(scalars, refs, scratch, sems, False)
    fetch(grad_branch, group, slope)
    for z in range(4):
        if z % 2 == 0:
            group.wait(z // 2)
        at = slice(z * D, (z + 1) * D)
        grad_hidden = matmul_right_t(grad_branch[...], group.quarter(z))
        grad_pre[:, at] = low(slope[:, at].astype(jnp.float32) * grad_hidden)


def cross_views(pack, rows):
    side = pack.at[:, 2 * D :]
    return side.at[:rows], side.at[rows : 2 * rows], pack.at[:, : 2 * D]


def cross_back_kernel(n, scalars, grad_pre, cotangent, second, gains, queries, memory_kv, probs, *rest):
    refs, cross_refs = rest[: n[0]], rest[n[0] : n[0] + n[1]]
    (grad_second_out, grad_gain, pack, grad_mixed, scratch, cross_scratch, sems, cross_sems) = rest[n[0] + n[1] :]
    group = Group(scalars, refs, scratch, sems, True)
    cross = Group(scalars, cross_refs, cross_scratch, cross_sems, True, (1,))
    fetch(grad_pre, group, second, cotangent, cross, queries, memory_kv, probs)
    rows = second.shape[0]
    valid = lax.broadcasted_iota(jnp.int32, (rows, 1), 0) < scalars[3]
    upstream = None
    for r in range(4):
        group.wait(r)
        term = matmul_right_t(grad_pre[:, columns_at(group.which(r))], group.place(r))
        upstream = term if upstream is None else upstream + term
    grad_result = jnp.where(valid, cotangent[...].astype(jnp.float32), 0.0)
    part, grad_gain[...] = norm_grad(second[...], gains[2:3], upstream)
    grad_second = grad_result + part
    grad_second_out[...] = grad_second
    send(grad_second_out)
    grad_cross, grad_q, _ = cross_views(pack, rows)
    grad_cross[...] = low(grad_second)
    cross.wait()
    grad_mixed[...] = low(matmul_right_t(grad_cross[...], cross.block(1)))
    attend_pairs_back(queries, memory_kv, 0, memory_kv, D, probs, grad_mixed, grad_q, pack, 0, pack, D)


def self_back_kernel(n, scalars, cross_pack, grad_second, first, gains, branch, inner, down, up, qkv, probs, *rest):
    refs, cross_refs = rest[: n[0]], rest[n[0] : n[0] + n[1]]
    (grad_first_out, grad_gain, grad_down, grad_up, pack, grad_mixed, scratch, cross_scratch, sems, cross_sems) = rest[n[0] + n[1] :]
    cross = Group(scalars, cross_refs, cross_scratch, cross_sems, True, (0,))
    group = Group(scalars, refs, scratch, sems, True, (3,))
    fetch(cross_pack, cross, first, grad_second, branch, group, qkv, probs)
    _, grad_q, _ = cross_views(cross_pack, first.shape[0])
    cross.wait()
    upstream = matmul_right_t(grad_q[...], cross.block(0))
    part, grad_gain[...] = norm_grad(first[...], gains[1:2], upstream)
    grad_first = grad_second[...] + part
    grad_first_out[...] = grad_first
    send(grad_first_out)
    active = low(gelu(inner[...]))
    grad_branch, grad_down[...], grad_up[...] = adapter_backward(
        branch[...], down[...], up[...], inner[...], active, grad_first
    )
    pack[:, 3 * D :] = grad_branch
    group.wait()
    grad_mixed[...] = low(matmul_right_t(grad_branch, group.block(3)))
    attend_pairs_back(qkv, qkv, D, qkv, 2 * D, probs, grad_mixed, pack, pack, D, pack, 2 * D)


def rows_product(kept, at, pairs):
    total = None
    for mine, grad in zip(kept, pairs):
        term = matmul(mine[at : at + D // 2, :], grad)
        total = term if total is None else total + term
    return total


def ffn_out_grad_kernel(n, scalars, kept, got, grad, other, *rest):
    *outs, stage, sems = rest
    fetch(kept, grad, got, other)
    blocks = Blocks(scalars, outs, stage, sems)
    rows, half = D // 8, D // 2
    grads = (grad[...], other[...])
    for b in range(4):
        picked = [
            jnp.concatenate([x[(1 + z) * half + b * rows : (1 + z) * half + (b + 1) * rows, :] for z in range(4)])
            for x in (kept, got)
        ]
        blocks.put(b, matmul(picked[0], grads[0]) + matmul(picked[1], grads[1]))
    blocks.finish()


def ffn_in_grad_kernel(n, scalars, kept, got, grad, other, *rest):
    *outs, stage, sems = rest
    fetch(kept, got, grad, other)
    blocks = Blocks(scalars, outs, stage, sems)
    for b in range(4):
        at = slice(b * D, (b + 1) * D)
        grad.ready(b)
        other.ready(b)
        blocks.put(b, rows_product((kept, got), 0, (grad.inner[:, at], other.inner[:, at])))
    blocks.finish()


def cross_grads_kernel(n, scalars, kept, got, pack, other, *rest):
    *outs, stage, sems = rest
    fetch(kept, got, pack, other)
    blocks = Blocks(scalars, outs, stage, sems)
    half = D // 2
    rows = kept.shape[1]
    views = [cross_views(p.inner, rows) for p in (pack, other)]
    ready_part(0, pack, other)
    blocks.put(0, rows_product((kept, got), 0, [v[1][...] for v in views]))
    blocks.put(1, rows_product((kept, got), half, [v[0][...] for v in views]))
    for b in range(2):
        ready_part(1 + b, pack, other)
        at = slice(b * D, (b + 1) * D)
        value = rows_product((kept, got), 2 * half, [v[2][:rows, at] for v in views])
        value += rows_product((kept, got), 3 * half, [v[2][rows:, at] for v in views])
        blocks.put(2 + b, value)
    blocks.finish()


def self_grads_kernel(n, scalars, kept, got, pack, other, *rest):
    *outs, stage, sems = rest
    fetch(kept, got, pack, other)
    blocks = Blocks(scalars, outs, stage, sems)
    for b in range(4):
        at = slice(b * D, (b + 1) * D)
        part = D // 2 if b == 3 else 0
        ready_part(b, pack, other)
        blocks.put(b, rows_product((kept, got), part, (pack.inner[:, at], other.inner[:, at])))
    blocks.finish()


def plain_grads_kernel(n, scalars, left, right, out, sems):
    fetch(left, right)
    out[...] = low(matmul_left_t(left[...], right[...]))


def pick_kernel(counts, scalars, *rest):
    inputs, outs = rest[:7], rest[7 : 7 + len(counts)]
    stage, sems, out_sems = rest[7 + len(counts) :]
    rows = inputs[0].shape[0]
    qkv, sout, cq, ckv, cout, f_in, f_out = inputs

    def columns(ref):
        return [ref.at[:, pl.ds(b * D, D)] for b in range(ref.shape[1] // D)]

    groups = {
        1: columns(qkv) + [sout],
        2: [cq, cout] + columns(ckv),
        3: columns(f_in),
        4: [f_out.at[pl.ds(b * rows, rows)] for b in range(4)],
    }
    used = 0
    loads = []
    for group, many in counts:
        for i in range(many):
            for b in range(4):
                copy = pltpu.make_async_copy(groups[group][b], stage.at[used], sems.at[used])
                pl.when(scalars[0] == (b ^ 3 if i else b))(copy.start)
            loads.append(copy)
            used += 1
    sent = []
    used = 0
    for (group, many), out in zip(counts, outs):
        for i in range(many):
            loads[used].wait()
            for z in range(4):
                target = out.at[z, i] if many > 1 else out.at[z]
                copy = pltpu.make_async_copy(stage.at[used], target, out_sems.at[used * 4 + z])
                copy.start()
                sent.append(copy)
            used += 1
    for copy in sent:
        copy.wait()


def pick(scalars, shards, counts):
    rows = shards[0].shape[0]
    total = sum(many for _, many in counts)
    shapes = [((4,) if many == 1 else (4, many)) + (rows, D) for _, many in counts]
    return pl.pallas_call(
        functools.partial(pick_kernel, counts),
        out_shape=[jax.ShapeDtypeStruct(shape, jnp.bfloat16) for shape in shapes],
        in_specs=[pl.BlockSpec(memory_space=pltpu.SMEM)]
        + [pl.BlockSpec(memory_space=pltpu.HBM)] * len(shards),
        out_specs=[pl.BlockSpec(memory_space=pltpu.HBM)] * len(counts),
        scratch_shapes=[
            pltpu.VMEM((total, rows, D), jnp.bfloat16),
            pltpu.SemaphoreType.DMA((total,)),
            pltpu.SemaphoreType.DMA((total * 4,)),
        ],
        compiler_params=pltpu.CompilerParams(vmem_limit_bytes=63 << 20),
        cost_estimate=pl.CostEstimate(flops=2 << 26, bytes_accessed=2 << 16, transcendentals=0),
        name="pick",
    )(scalars, *shards)


def plain_grads_kernel(n, scalars, left, right, out, sems):
    out[...] = low(matmul_left_t(left[...], right[...]))


def memory_back_kernel(n, scalars, pack, *rest):
    refs, (memory_grad, scratch, sems) = rest[: n[0]], rest[n[0] :]
    group = Group(scalars, refs, scratch, sems, True, (2, 3))
    fetch(pack, group)
    group.wait_block(2)
    product = matmul_right_t(pack[:, :D], group.block(2))
    group.wait_block(3)
    memory_grad[...] = product + matmul_right_t(pack[:, D : 2 * D], group.block(3))


def token_back_kernel(n, scalars, grad_qkv, tokens, grad_first, gains, *rest):
    refs, (token_grad, grad_gain, scratch, sems) = rest[: n[0]], rest[n[0] :]
    group = Group(scalars, refs, scratch, sems, True, (0, 1, 2))
    fetch(grad_qkv, group, tokens, grad_first)
    group.wait_block(0)
    upstream = matmul_right_t(grad_qkv[:, :D], group.block(0))
    for b in range(1, 3):
        group.wait_block(b)
        upstream += matmul_right_t(grad_qkv[:, b * D : (b + 1) * D], group.block(b))
    part, grad_gain[...] = norm_grad(tokens[...].astype(jnp.float32), gains[0:1], upstream)
    token_grad[...] = grad_first[...] + part


def nbytes(shape, kind):
    total = jnp.dtype(kind).itemsize
    for size in shape:
        total *= size
    return total


class Moved:
    def __init__(self, outer, inner, sems, first, windows, is_input):
        self.inner, self.is_input = inner, is_input
        self.copies, self.flying, self.done = [], set(), set()
        for i, window in enumerate(windows):
            pair = (outer, inner)
            if window is not None:
                at = (pl.ds(window[0], window[1]), pl.ds(window[2], window[3]))
                pair = (outer.at[at], inner.at[at])
            self.copies.append(pltpu.make_async_copy(*(pair if is_input else pair[::-1]), sems.at[first + i]))

    def start(self, part=None):
        for i, copy in enumerate(self.copies):
            if part in (None, i) and i not in self.flying:
                copy.start()
                self.flying.add(i)

    def ready(self, part=None):
        if self.is_input:
            self.start()
            for i, copy in enumerate(self.copies):
                if part in (None, i) and i not in self.done:
                    copy.wait()
                    self.done.add(i)
        return self.inner

    def finish(self):
        self.start()
        for i, copy in enumerate(self.copies):
            if i not in self.done:
                copy.wait()

    @property
    def shape(self):
        return self.inner.shape

    @property
    def at(self):
        return self.ready().at

    def __getitem__(self, index):
        return self.ready()[index]

    def __setitem__(self, index, value):
        self.inner[index] = value


def fetch(*things):
    for thing in things:
        if isinstance(thing, (Moved, Group)):
            thing.start()


def send(*arrays):
    for array in arrays:
        if isinstance(array, Moved):
            array.start()


def send_part(part, *arrays):
    for array in arrays:
        if isinstance(array, Moved):
            array.start(part)


def ready(*arrays):
    for array in arrays:
        if isinstance(array, Moved):
            array.ready()


def ready_part(part, *arrays):
    for array in arrays:
        array.ready(part)


def column_blocks(shape):
    return [(0, shape[0], b * D, D) for b in range(shape[1] // D)]


def tiled(shape):
    return shape[-1] % 128 == 0 and shape[-2] % 16 == 0


def run(kernel, name, micros, scalars, arrays, groups, outs, scratch=(), direct=False, cut=None):
    n = tuple(len(group) for group in groups)
    outs, scratch = list(outs), list(scratch)
    windows = [pair[1] if isinstance(pair, tuple) else [None] for pair in arrays]
    arrays = [pair[0] if isinstance(pair, tuple) else pair for pair in arrays]
    ins = [(a.shape, a.dtype) for a in arrays]
    flat = [part for group in groups for part in group]
    moved = [pair for pair in (ins if direct else ins + outs) if tiled(pair[0])]
    rows = D // 8
    shape = (4, 2, 4, rows, D) if name in ("ffn_out", "ffn_back") else (4, 4, 2, rows, D)
    spaces = scratch + [(shape, jnp.bfloat16)] * len(groups)

    def body(scalar_ref, *refs):
        refs = list(refs)
        inputs, pieces = refs[: len(ins)], refs[len(ins) : len(ins) + len(flat)]
        results = refs[len(ins) + len(flat) :][: len(outs)]
        rest = refs[len(ins) + len(flat) + len(outs) :]
        copies, rest = rest[: len(moved)], rest[len(moved) :]
        if moved:
            sems, rest = rest[0], rest[1:]
        used, first = 0, 0
        for side, pairs in ((inputs, ins), (results, [] if direct else outs)):
            for i, (shape, _) in enumerate(pairs):
                if tiled(shape):
                    parts = windows[i] if side is inputs else (cut or {}).get(i, [None])
                    side[i] = Moved(side[i], copies[used], sems, first, parts, side is inputs)
                    used, first = used + 1, first + len(parts)
        kernel(n, scalar_ref, *inputs, *pieces, *results, *rest)
        for array in inputs + results:
            if isinstance(array, Moved):
                array.finish()

    def spec(shape):
        return pl.BlockSpec(memory_space=pltpu.HBM if tiled(shape) else pltpu.VMEM)

    return pl.pallas_call(
        body,
        out_shape=[jax.ShapeDtypeStruct(shape, kind) for shape, kind in outs],
        in_specs=[pl.BlockSpec(memory_space=pltpu.SMEM)]
        + [spec(shape) for shape, _ in ins]
        + [pl.BlockSpec(memory_space=pltpu.HBM)] * len(flat),
        out_specs=[spec(shape) for shape, _ in outs],
        scratch_shapes=[pltpu.VMEM(shape, kind) for shape, kind in moved]
        + ([pltpu.SemaphoreType.DMA((len(outs) * 4 + sum(map(len, windows)),))] if moved else [])
        + [pltpu.VMEM(shape, kind) for shape, kind in spaces]
        + [pltpu.SemaphoreType.DMA((32,)) for _ in (groups or [None])],
        compiler_params=pltpu.CompilerParams(vmem_limit_bytes=63 << 20),
        cost_estimate=pl.CostEstimate(
            flops=int(micros * 2e8), bytes_accessed=int(micros * 2e5), transcendentals=0
        ),
        name=name,
    )(scalars, *arrays, *flat)


def moves(step):
    pairs = []
    for y in range(2):
        for x in range(2):
            for z in range(4):
                for c in range(2):
                    ty, tx, tz, tc = step(y, x, z, c)
                    pairs.append((((y * 2 + x) * 4 + z) * 2 + c, ((ty * 2 + tx) * 4 + tz) * 2 + tc))
    return pairs


def swap_x(values):
    return lax.ppermute(values, BOTH, moves(lambda y, x, z, c: (y, 1 - x, z, c)))


def swap_y(values):
    return lax.ppermute(values, BOTH, moves(lambda y, x, z, c: (1 - y, x, z, c)))


def swap_core(values):
    return lax.ppermute(values, BOTH, moves(lambda y, x, z, c: (y, x, z, 1 - c)))


def turn_z(values, by):
    return lax.ppermute(values, BOTH, moves(lambda y, x, z, c: (y, x, (z + by) % 4, c)))


def after(value, *marks):
    return lax.optimization_barrier((value,) + marks)[0]


def first_swap(values):
    return lax.ppermute(
        values, BOTH, moves(lambda y, x, z, c: (y, 1 - x, z, c) if c == 0 else (1 - y, x, z, c))
    )


def second_swap(values):
    return lax.ppermute(
        values, BOTH, moves(lambda y, x, z, c: (1 - y, x, z, c) if c == 0 else (y, 1 - x, z, c))
    )


LINES = [[z * 2 + c for z in range(4)] for c in range(2)]


def spread_z(values):
    return lax.all_to_all(
        values, "fsdp", split_axis=0, concat_axis=0, tiled=True, axis_index_groups=LINES
    )


class Layer:
    def __init__(self, scalars, tokens, memory, cotangent, staged):
        self.scalars, self.tokens, self.memory, self.cotangent = scalars, tokens, memory, cotangent
        self.staged = staged
        self.t, self.m = tokens.shape[0], memory.shape[0]

    def hold(self, *marks):
        self.scalars = after(self.scalars, *marks)

    def adapters(self, generated):
        block, start = D * ADAPT, 3 * D
        self.gains = 1.0 + 0.25 * generated[:start].astype(jnp.float32).reshape(3, D)
        self.down_1 = generated[start : start + block].reshape(D, ADAPT)
        self.up_1 = generated[start + block : start + 2 * block].reshape(ADAPT, D)
        self.down_2 = generated[start + 2 * block : start + 3 * block].reshape(D, ADAPT)
        self.up_2 = generated[start + 3 * block : start + 4 * block].reshape(ADAPT, D)

    def rows(self, width=D, kind=jnp.bfloat16):
        return ((self.t, width), kind)

    def wide(self, width=D):
        return self.rows(width, jnp.float32)

    def halves(self, count):
        return [((count * (D // 2), self.t), jnp.bfloat16)] * 2

    def self_forward(self, w1):
        local = [self.rows(), self.rows()]
        outs = run(
            self_forward_kernel,
            "self_forward",
            11,
            self.scalars,
            [self.tokens, self.gains, self.down_1, self.up_1],
            [w1],
            [
                self.rows(3 * D),
                ((HEADS, self.t, self.t), jnp.bfloat16),
                self.rows(),
                self.wide(ADAPT),
                self.wide(),
                self.rows(),
            ]
            + (self.halves(2) if self.staged else local),
            scratch=local if self.staged else [],
        )
        self.qkv, self.probs_1, self.branch_1, self.inner_1, self.first, self.normed_2 = outs[:6]
        self.saved_1 = outs[6:]

    def cross_forward(self, w2):
        local = [self.rows()]
        outs = run(
            cross_forward_kernel,
            "cross_forward",
            15,
            self.scalars,
            [self.normed_2, self.first, self.memory, self.gains],
            [w2],
            [
                self.rows(),
                ((self.m, 2 * D), jnp.bfloat16),
                ((HEADS, self.m, self.t), jnp.bfloat16),
                self.wide(),
                self.rows(),
            ]
            + (self.halves(4) if self.staged else local),
            scratch=local if self.staged else [],
        )
        self.queries, self.memory_kv, self.probs_2, self.second, self.normed_3 = outs[:5]
        self.saved_2 = outs[5:]

    def ffn_in(self, w3):
        outs = run(
            ffn_in_kernel,
            "ffn_in",
            6,
            self.scalars,
            [self.normed_3],
            [w3],
            [self.rows(4 * D), self.rows(4 * D)] + (self.halves(5) if self.staged else []),
            cut={i: column_blocks((self.t, 4 * D)) for i in range(2)},
        )
        self.slope, self.hidden = outs[:2]
        self.saved_3 = outs[2:]

    def adapter_outs(self):
        return [((D, ADAPT), jnp.float32), ((ADAPT, D), jnp.float32)]

    def ffn_out(self, w4):
        self.mixed_out, self.grad_branch, self.grad_down_2, self.grad_up_2 = run(
            ffn_out_kernel,
            "ffn_out",
            8,
            self.scalars,
            [self.hidden, self.second, self.cotangent, self.down_2, self.up_2],
            [w4],
            [self.rows(), self.rows()] + self.adapter_outs(),
        )

    def ffn_back(self, w4):
        (self.grad_pre,) = run(
            ffn_back_kernel,
            "ffn_back",
            8,
            self.scalars,
            [self.grad_branch, self.slope],
            [w4],
            [self.rows(4 * D)],
        )

    def cross_back(self, w3, w2):
        self.grad_second, self.grad_gain_3, self.cross_pack = run(
            cross_back_kernel,
            "cross_back",
            15,
            self.scalars,
            [
                self.grad_pre,
                self.cotangent,
                self.second,
                self.gains,
                self.queries,
                self.memory_kv,
                self.probs_2,
            ],
            [w3, w2],
            [self.wide(), ((1, D), jnp.float32), ((self.m, 3 * D), jnp.bfloat16)],
            scratch=[self.rows()],
        )

    def self_back(self, w1, w2):
        self.grad_first, self.grad_gain_2, self.grad_down_1, self.grad_up_1, self.self_pack = run(
            self_back_kernel,
            "self_back",
            11,
            self.scalars,
            [
                (self.cross_pack, [(self.t, self.t, 2 * D, D)]),
                self.grad_second,
                self.first,
                self.gains,
                self.branch_1,
                self.inner_1,
                self.down_1,
                self.up_1,
                self.qkv,
                self.probs_1,
            ],
            [w1, w2],
            [self.wide(), ((1, D), jnp.float32)] + self.adapter_outs() + [self.rows(4 * D)],
            scratch=[self.rows()],
        )

    def token_back(self, w1):
        self.token_grad, self.grad_gain_1 = run(
            token_back_kernel,
            "token_back",
            5,
            self.scalars,
            [(self.self_pack, [(0, self.t, 0, 3 * D)]), self.tokens, self.grad_first, self.gains],
            [w1],
            [self.wide(), ((1, D), jnp.float32)],
        )

    def memory_back(self, w2):
        (self.memory_grad,) = run(
            memory_back_kernel,
            "memory_back",
            6,
            self.scalars,
            [(self.cross_pack, [(0, self.m, 0, 2 * D)])],
            [w2],
            [((self.m, D), jnp.float32)],
        )

    def block_grads(self, kernel, name, kept, got, grad, other, windows=None, rows=None):
        stage = ((4, 4, D // 8, D), jnp.bfloat16)
        part = ((2, 4, D // 8, D), jnp.bfloat16)
        if rows:
            kept, got = (kept, [rows + (0, self.t)]), (got, [rows + (0, self.t)])
        if windows:
            grad, other = (grad, windows), (other, windows)
        return run(
            kernel, name, 5, self.scalars, [kept, got, grad, other], [], [part, part], [stage], direct=True
        )

    def plain_grads(self, left, right):
        (out,) = run(
            plain_grads_kernel,
            "plain_grads",
            5,
            self.scalars,
            [left, right],
            [],
            [((left.shape[1], right.shape[1]), jnp.bfloat16)],
        )
        return out

    def grad_generated(self):
        return low(
            jnp.concatenate(
                [
                    0.25 * self.grad_gain_1,
                    0.25 * self.grad_gain_2,
                    0.25 * self.grad_gain_3,
                    self.grad_down_1.reshape(ADAPT, D),
                    self.grad_up_1,
                    self.grad_down_2.reshape(ADAPT, D),
                    self.grad_up_2,
                ]
            )
        ).reshape(-1)


def staged_layer(layer, where, task_ids, hidden_all, hyper_gen, shards):
    q, z, c = where[0], where[1], where[2]

    own_1, own_2, own_3, own_4 = pick(where, shards, [(1, 1), (2, 1), (3, 2), (4, 2)])
    column_1 = spread_z(own_1)
    ids = jnp.stack([task_ids, swap_core(task_ids)])
    ids_ahead = [ids] + [turn_z(ids, 4 - k) for k in (1, 2, 3)]
    gen_shard = low(matmul(hidden_all, hyper_gen))
    column_1 = after(column_1, *ids_ahead)
    near_x_1, near_y_1 = swap_x(column_1), swap_y(column_1)

    column_2 = spread_z(after(own_2, column_1))

    def rows_of(tasks):
        select = low(tasks[:, 0:1] == jnp.arange(TASKS, dtype=jnp.int32)[None, :])
        return after(low(matmul(select, gen_shard)), near_x_1, near_y_1, column_2)

    asked = [rows_of(tasks) for tasks in ids_ahead]
    turned = [turn_z(asked[k], k) for k in (1, 2, 3)]
    got = jnp.stack([asked[0]] + turned, axis=1)
    pieces = jnp.concatenate([got[0], swap_core(got[1])])
    slots = jnp.arange(8, dtype=jnp.int32)
    source = ((slots % 2) ^ c) * 4 + (z - slots // 2 + 4) % 4
    unturn = low(source[:, None] == slots[None, :])
    layer.adapters(low(matmul(unturn, pieces)).reshape(-1))

    far_1 = swap_y(near_x_1)
    w1 = [column_1, near_x_1, near_y_1, far_1]
    w1 += [swap_core(after(part, near_x_1)) for part in w1]

    def second_stage(pair, *marks):
        column = after(pair, *marks)[:, 0]
        return [column, swap_x(column), swap_y(column), pair[:, 1]]

    def third_stage(parts, *marks):
        return parts + [swap_core(after(part, *marks)) for part in parts]

    w2 = [column_2, swap_x(column_2), swap_y(column_2)]
    pair_3 = spread_z(after(own_3, *turned))
    layer.hold(column_2)
    layer.self_forward(w1)
    far_2 = swap_x(after(w2[2], layer.normed_2))
    w3 = second_stage(pair_3, layer.normed_2)
    w2 = third_stage(w2 + [far_2], w3[0])
    got_1 = swap_core(layer.saved_1[1])
    pair_4 = spread_z(after(own_4, w3[0]))
    layer.hold(got_1, w3[0])
    layer.cross_forward(w2)
    got_2 = swap_core(layer.saved_2[1])
    w3 = third_stage(w3, layer.normed_3)
    w4 = second_stage(pair_4, layer.normed_3)
    layer.hold(got_2, w4[0])
    layer.ffn_in(w3)
    got_3 = swap_core(layer.saved_3[1])
    w4 = third_stage(w4, layer.hidden)
    layer.hold(got_3)
    layer.ffn_out(w4)

    def first_way(sums, *marks):
        home, away = sums
        return home, first_swap(after(away, *marks))

    def second_way(sums, *marks):
        home, got = sums
        leaving = add_low(after(home, *marks)[1], got[1])
        return home, got, leaving, second_swap(leaving)

    def third_way(sums, *marks):
        home, first, _, second = sums
        terms = [part.astype(jnp.float32) for part in (after(home, *marks)[0], first[0], second)]
        return low(terms[0] + terms[1] + terms[2])

    def grads(kernel, name, kept, got, grad, other):
        windows = column_blocks(grad.shape) if grad.shape[1] > D else None
        if kernel is cross_grads_kernel:
            windows = [windows[2]] + windows[:2]
        half = D // 2
        rows = {ffn_in_grad_kernel: (0, half), ffn_out_grad_kernel: (half, 4 * half)}.get(kernel)
        return layer.block_grads(kernel, name, kept, got, grad, other, windows, rows)

    other = swap_core(layer.grad_branch)
    g4 = grads(
        ffn_out_grad_kernel, "ffn_out_grad", layer.saved_3[0], got_3, layer.grad_branch, other
    )
    s4 = first_way(g4)
    layer.hold(g4[0])
    layer.ffn_back(w4)
    other_pre = swap_core(layer.grad_pre)
    layer.hold(layer.grad_pre)
    g3 = grads(
        ffn_in_grad_kernel, "ffn_in_grad", layer.saved_3[0], got_3, layer.grad_pre, other_pre
    )
    s3 = first_way(g3)
    layer.hold(g3[0])
    layer.cross_back(w3, w2)
    s4 = second_way(s4, layer.cross_pack)
    s3 = second_way(s3, layer.cross_pack)
    other = swap_core(after(layer.cross_pack, s4[2], s3[2]))
    layer.hold(s4[2], s3[2])
    layer.self_back(w1, w2)
    u4 = third_way(s4, layer.self_pack)
    u3 = third_way(s3, layer.self_pack)
    other_self = swap_core(after(layer.self_pack, u4, u3))
    sent_4 = spread_z(after(u4, u3))
    layer.hold(u4, u3)
    g2 = grads(
        cross_grads_kernel, "cross_grads", layer.saved_2[0], got_2, layer.cross_pack, other
    )
    s2 = first_way(g2)
    layer.hold(g2[0])
    g1 = grads(
        self_grads_kernel, "self_grads", layer.saved_1[0], got_1, layer.self_pack, other_self
    )
    s1 = first_way(g1)
    sent_3 = spread_z(after(u3, sent_4))
    layer.hold(g1[0], sent_4)
    layer.token_back(w1)
    s2 = second_way(s2, layer.token_grad)
    layer.hold(s2[2])
    layer.memory_back(w2)
    s1 = second_way(s1, layer.memory_grad)
    u2 = third_way(s2, s1[2])
    sent_2 = spread_z(after(u2, sent_3))
    own_4 = jnp.sum(after(sent_4, s1[2]).astype(jnp.float32), axis=0)
    own_3 = jnp.sum(after(sent_3, s1[2]).astype(jnp.float32), axis=0)

    pieces = after(layer.grad_generated().reshape(4, 2, -1), s2[2])
    mine = lax.dynamic_index_in_dim(pieces, c, 1, keepdims=False)
    theirs = lax.dynamic_index_in_dim(pieces, 1 - c, 1, keepdims=False)
    both = jnp.stack([mine, swap_core(theirs)], axis=1)
    both = lax.dynamic_slice_in_dim(jnp.concatenate([both, both]), z, 4, 0)
    terms = jnp.concatenate([both[0]] + [turn_z(both[k], k) for k in (1, 2, 3)])
    ids = jnp.concatenate([ids_ahead[(4 - k) % 4] for k in range(4)])[:, 0]
    select = low(jnp.arange(TASKS, dtype=jnp.int32)[:, None] == ids[None, :])
    task_grad = low(matmul(select, terms))
    task_grad = add_low(task_grad, swap_x(task_grad))
    task_grad = task_grad.astype(jnp.float32) + swap_y(task_grad).astype(jnp.float32)

    def sum_owners(part):
        part = part + swap_core(part)
        got = [part] + [turn_z(part, k) for k in (1, 2, 3)]
        return (got[0] + got[2]) + (got[1] + got[3])

    def share(owns):
        own = low(jnp.stack(owns))
        pair = jnp.stack([own, first_swap(own)])
        quad = jnp.concatenate([pair, second_swap(pair)])
        slots = [jnp.where(c == 0, q ^ b, ((q ^ b) % 2) * 2 + (q ^ b) // 2) for b in range(4)]
        return [
            [lax.dynamic_index_in_dim(quad, at, 0, keepdims=False)[i].astype(jnp.float32) for at in slots]
            for i in range(len(owns))
        ]

    sent_1 = spread_z(after(third_way(s1), sent_2))
    own_2 = jnp.sum(sent_2.astype(jnp.float32), axis=0)
    own_1 = jnp.sum(sent_1.astype(jnp.float32), axis=0)
    g3, g4 = share([own_3, own_4])
    g2, g1 = share([own_2, own_1])
    summed = (
        jnp.concatenate(g1[:3], axis=1),
        g1[3],
        g2[0],
        jnp.concatenate(g2[2:], axis=1),
        g2[1],
        jnp.concatenate(g3, axis=1),
        jnp.concatenate(g4, axis=0),
    )
    return summed, task_grad, sum_owners


def plain_layer(layer, task_ids, hidden_all, hyper_gen, groups):
    owners = lax.axis_size("fsdp")

    def whole(shard):
        return lax.all_gather(shard, "fsdp", axis=0, tiled=True)

    w1, w2, w3 = (
        [jnp.concatenate([whole(block) for block in blocks]).reshape(4, 4, 2, D // 8, D)] for blocks in groups[:3]
    )
    w4 = [whole(jnp.concatenate(groups[3])).reshape(4, 2, 4, D // 8, D)]
    select = low(task_ids[:, None] == jnp.arange(TASKS, dtype=jnp.int32)[None, :])
    gen_shard = low(matmul(hidden_all, hyper_gen))
    gen_tasks = lax.all_gather(gen_shard, "fsdp", axis=1, tiled=True)
    layer.adapters(low(matmul(select, gen_tasks)[0]))
    layer.self_forward(w1)
    layer.cross_forward(w2)
    layer.ffn_in(w3)
    layer.ffn_out(w4)
    layer.ffn_back(w4)
    layer.cross_back(w3, w2)
    layer.self_back(w1, w2)
    layer.token_back(w1)
    layer.memory_back(w2)

    def owned(left, right):
        part = low(lax.psum_scatter(layer.plain_grads(left, right), "fsdp", scatter_dimension=0, tiled=True))
        return lax.psum(part, "dp").astype(jnp.float32)

    t = layer.t
    pack = layer.cross_pack
    summed = (
        owned(layer.saved_1[0], layer.self_pack[:, : 3 * D]),
        owned(layer.saved_1[1], layer.self_pack[:, 3 * D :]),
        owned(layer.normed_2, pack[t : 2 * t, 2 * D :]),
        owned(layer.memory, pack[:, : 2 * D]),
        owned(layer.saved_2[0], pack[:t, 2 * D :]),
        owned(layer.normed_3, layer.grad_pre),
        owned(layer.hidden, layer.grad_branch),
    )
    pieces = layer.grad_generated().reshape(owners, 1, -1)
    select = low(jnp.arange(TASKS, dtype=jnp.int32)[:, None] == task_ids[None, :])
    terms = low(select[None].astype(jnp.float32) * pieces.astype(jnp.float32))
    terms = lax.all_to_all(terms, "fsdp", split_axis=0, concat_axis=0, tiled=True)
    task_grad = low(jnp.sum(terms.astype(jnp.float32), axis=0))
    task_grad = lax.psum(task_grad, "dp").astype(jnp.float32)
    return summed, task_grad, lambda part: lax.psum(part, "fsdp")


def hyper_tail(task_grad, pre_all, hidden_all, task_table, hyper_in, hyper_gen, sum_owners):
    grad_hyper_gen = jnp.dot(
        hidden_all.astype(jnp.float32).T, task_grad, precision=lax.Precision.HIGHEST
    )
    grad_hidden = jnp.dot(
        task_grad, hyper_gen.astype(jnp.float32).T, precision=lax.Precision.HIGHEST
    )
    grad_pre_all = gelu_slope(pre_all) * sum_owners(grad_hidden)
    grad_table = jnp.dot(grad_pre_all, hyper_in.T, precision=lax.Precision.HIGHEST)
    grad_first = jnp.dot(task_table.T, grad_pre_all, precision=lax.Precision.HIGHEST)
    return grad_table, grad_first, grad_hyper_gen


def shards(
    tokens,
    memory,
    target_lengths,
    memory_lengths,
    task_ids,
    cotangent,
    self_qkv,
    self_out,
    cross_q,
    cross_kv,
    cross_out,
    ffn_in,
    ffn_out,
    task_table,
    hyper_in,
    hyper_gen,
):
    staged = lax.axis_size("fsdp") == 8 and lax.axis_size("dp") == 4
    pre_all = jnp.dot(task_table, hyper_in, precision=lax.Precision.HIGHEST)
    hidden_all = low(jax.nn.gelu(pre_all))

    def columns(shard):
        return [shard[:, b * D : (b + 1) * D] for b in range(shard.shape[1] // D)]

    q = lax.axis_index("dp").astype(jnp.int32)
    f = lax.axis_index("fsdp").astype(jnp.int32)
    where = jnp.stack([q, f // 2, f % 2])
    scalars = jnp.concatenate([where, target_lengths, memory_lengths])
    layer = Layer(scalars, tokens, memory, cotangent, staged)
    if staged:
        summed, task_grad, sum_owners = staged_layer(
            layer,
            where,
            task_ids,
            hidden_all,
            hyper_gen,
            (self_qkv, self_out, cross_q, cross_kv, cross_out, ffn_in, ffn_out),
        )
    else:
        rows = self_qkv.shape[0]
        groups = (
            columns(self_qkv) + [self_out],
            [cross_q, cross_out] + columns(cross_kv),
            columns(ffn_in),
            [ffn_out[b * rows : (b + 1) * rows] for b in range(4)],
        )
        summed, task_grad, sum_owners = plain_layer(layer, task_ids, hidden_all, hyper_gen, groups)
    grad_table, grad_first, grad_hyper_gen = hyper_tail(
        task_grad, pre_all, hidden_all, task_table, hyper_in, hyper_gen, sum_owners
    )
    return (
        (layer.mixed_out, layer.token_grad, layer.memory_grad)
        + summed
        + (grad_table, grad_first, grad_hyper_gen)
    )


def solution(mesh):
    by_both = P(("dp", "fsdp"), None)
    by_rows = P("fsdp", None)
    return jax.shard_map(
        shards,
        mesh=mesh,
        in_specs=(by_both, by_both)
        + (P(("dp", "fsdp")),) * 3
        + (by_both,)
        + (by_rows,) * 7
        + (P(), P(), P(None, "fsdp")),
        out_specs=(by_both,) * 3 + (by_rows,) * 7 + (P(), P(), P(None, "fsdp")),
        check_vma=False,
    )
```

```python
import functools

import jax
import jax.numpy as jnp
from jax import lax
from jax.experimental import pallas as pl
from jax.experimental.pallas import tpu as pltpu
from jax.sharding import PartitionSpec as P

D = 768
HEADS = 12
HEAD = 64
ADAPT = 24
TASKS = 8
BOTH = ("dp", "fsdp")


def matmul(left, right):
    return jnp.dot(left, right, preferred_element_type=jnp.float32)


def matmul_left_t(left, right):
    return lax.dot_general(
        left, right, (((0,), (0,)), ((), ())), preferred_element_type=jnp.float32
    )


def matmul_right_t(left, right):
    return lax.dot_general(
        left, right, (((1,), (1,)), ((), ())), preferred_element_type=jnp.float32
    )


def low(values):
    return values.astype(jnp.bfloat16)


def add_low(left, right):
    return low(left.astype(jnp.float32) + right.astype(jnp.float32))


def rms_factor(values):
    return lax.rsqrt(jnp.mean(values * values, axis=-1, keepdims=True) + 1e-06)


def norm_grad(values, gains, upstream):
    factor = rms_factor(values)
    scaled = upstream * gains
    mean = jnp.mean(values * scaled, axis=-1, keepdims=True)
    part = factor * scaled - values * (factor * factor * factor * mean)
    return part, jnp.sum(upstream * values * factor, axis=0, keepdims=True)


GELU_A = 0.7978845608
GELU_B = 0.044715


def gelu(values):
    inside = GELU_A * (values + GELU_B * values * values * values)
    return 0.5 * values * (1.0 + jnp.tanh(inside))


def gelu_both(values):
    square = values * values
    curve = jnp.tanh(GELU_A * (values + GELU_B * square * values))
    inner = GELU_A * (1.0 + 3.0 * GELU_B * square)
    half = 0.5 * (1.0 + curve)
    return values * half, half + 0.5 * values * (1.0 - curve * curve) * inner


def gelu_slope(values):
    square = values * values
    curve = jnp.tanh(GELU_A * (values + GELU_B * square * values))
    inner = GELU_A * (1.0 + 3.0 * GELU_B * square)
    return 0.5 * (1.0 + curve) + 0.5 * values * (1.0 - curve * curve) * inner


class Group:
    def __init__(self, scalars, refs, scratch, sems, by_block, blocks=(0, 1, 2, 3)):
        self.scalars, self.refs, self.scratch, self.sems = scalars, refs, scratch, sems
        self.by_block, self.blocks = by_block, blocks
        self.staged = len(refs) > 1
        self.waited = False

    def _each(self, act, part=None):
        if not self.staged:
            act(pltpu.make_async_copy(self.refs[0], self.scratch, self.sems.at[0]))
            return
        c = self.scalars[2]
        for place in range(4):
            block = self.which(place)

            def parts(place=place, block=block):
                for side in range(2):
                    source = self.refs[side * 4 + place]
                    if self.by_block and part in (None, place):
                        target = self.scratch.at[place, :, c ^ side]
                        act(pltpu.make_async_copy(source, target, self.sems.at[place * 2 + side]))
                    if not self.by_block:
                        for half in range(2):
                            if part in (None, half):
                                at = pl.ds(half * 2, 2)
                                act(
                                    pltpu.make_async_copy(
                                        source.at[at],
                                        self.scratch.at[at, c ^ side, block],
                                        self.sems.at[(place * 2 + side) * 2 + half],
                                    )
                                )

            if len(self.blocks) == 4:
                parts()
            else:
                wanted = block == self.blocks[0]
                for other in self.blocks[1:]:
                    wanted = wanted | (block == other)
                pl.when(wanted)(parts)

    def start(self):
        self._each(lambda copy: copy.start())

    def wait(self, part=None):
        if self.staged:
            self._each(lambda copy: copy.wait(), part)
        elif not self.waited:
            self._each(lambda copy: copy.wait())
            self.waited = True

    def wait_block(self, index):
        if not self.staged:
            self.wait()
            return
        place, c = self.which(index), self.scalars[2]
        for side in range(2):
            target = self.scratch.at[place, :, c ^ side]
            pltpu.make_async_copy(self.refs[0], target, self.sems.at[place * 2 + side]).wait()

    def place(self, place):
        return self.scratch[place].reshape(D, D)

    def which(self, place):
        return self.scalars[0] ^ place if self.staged else place

    def block(self, index):
        return self.scratch[self.which(index)].reshape(D, D)

    def quarter(self, z):
        return self.scratch[z].reshape(D, D)


def columns_at(block):
    return pl.ds(pl.multiple_of(block * D, D), D)


def part_rows(scalars, value, keep, send, at):
    flat = value.T
    rows = flat.shape[0] // 8
    for parity in range(2):
        here = scalars[2] == parity

        @pl.when(here)
        def _():
            for z in range(4):
                piece = flat[(z * 2 + parity) * rows : (z * 2 + parity + 1) * rows]
                keep[at + z * rows : at + (z + 1) * rows, :] = piece

        @pl.when(jnp.logical_not(here))
        def _():
            for z in range(4):
                piece = flat[(z * 2 + parity) * rows : (z * 2 + parity + 1) * rows]
                send[at + z * rows : at + (z + 1) * rows, :] = piece


class Blocks:
    def __init__(self, scalars, outs, stage, sems):
        self.scalars, self.outs, self.stage, self.sems = scalars, outs, stage, sems
        self.sent = []

    def put(self, block, value):
        rows = value.shape[0] // 4
        value = low(value)
        for z in range(4):
            self.stage[block, z] = value[z * rows : (z + 1) * rows]
        r, c = self.scalars[0] ^ block, self.scalars[2]
        first = jnp.where(c == 0, r % 2, r // 2)
        second = jnp.where(c == 0, r // 2, r % 2)
        for way, out in enumerate(self.outs):
            copy = pltpu.make_async_copy(self.stage.at[block], out.at[second], self.sems.at[block * 2 + way])
            pl.when(first == way)(copy.start)
            self.sent.append((first == way, copy))

    def finish(self):
        for here, copy in self.sent:
            pl.when(here)(copy.wait)


def head_lanes(rows, head):
    lane = lax.broadcasted_iota(jnp.int32, (rows, 128), 1)
    return lane < HEAD if head == 0 else lane >= HEAD


def pick_head(values, head):
    return jnp.where(head_lanes(values.shape[0], head), values, jnp.zeros_like(values))


def pair_at(pair, base=0):
    return pl.ds(pl.multiple_of(base + pair * 128, 128), 128)


def work_on_pairs(first, middle, last, spaces):
    wide, low_spaces = spaces[:2], spaces[2:]
    pairs = HEADS // 2
    first(0, wide[0])

    @pl.loop(0, pairs // 2)
    def _(turn):
        for i in range(2):
            pair = turn * 2 + i
            first(jnp.minimum(pair + 1, pairs - 1), wide[1 - i])
            middle(pair, wide[i], low_spaces[i])
            last(jnp.maximum(pair - 1, 0), low_spaces[1 - i])

    last(pairs - 1, low_spaces[1])


def attend_spaces(keys, queries):
    shape = (2, keys, queries)
    return [(shape, jnp.float32)] * 2 + [(shape, jnp.bfloat16)] * 2


def attend_pairs(q_ref, k_ref, k_at, v_ref, v_at, bias, probs, mixed, spaces):
    ready(q_ref, k_ref, v_ref)
    q_ref, k_ref, v_ref, probs = (inner_of(ref) for ref in (q_ref, k_ref, v_ref, probs))

    def scores_of(pair, wide):
        keys = k_ref[:, pair_at(pair, k_at)]
        for head in range(2):
            wide[head] = matmul_right_t(pick_head(keys, head), q_ref[:, pair_at(pair)])

    def weights_of(pair, wide, space):
        for head in range(2):
            scores = wide[head] + bias
            weights = jnp.exp(scores - jnp.max(scores, axis=0, keepdims=True))
            weights = low(weights * (1.0 / jnp.sum(weights, axis=0, keepdims=True)))
            space[head] = weights
            probs[pair * 2 + head] = weights

    def mix(pair, space):
        values = v_ref[:, pair_at(pair, v_at)].T
        halves = [matmul(values[head * HEAD : (head + 1) * HEAD], space[head]) for head in range(2)]
        mixed[:, pair_at(pair)] = low(jnp.concatenate(halves, axis=0).T)

    work_on_pairs(scores_of, weights_of, mix, spaces)


def attend_pairs_back(
    q_ref, k_ref, k_at, v_ref, v_at, probs, grad_mixed, grad_q, grad_k, gk_at, grad_v, gv_at, spaces
):
    ready(q_ref, k_ref, v_ref, probs)
    q_ref, k_ref, v_ref, probs = (inner_of(ref) for ref in (q_ref, k_ref, v_ref, probs))
    grad_q, grad_k, grad_v = (inner_of(ref) for ref in (grad_q, grad_k, grad_v))

    def grad_weights(pair, wide):
        values = v_ref[:, pair_at(pair, v_at)]
        for head in range(2):
            wide[head] = matmul_right_t(pick_head(values, head), grad_mixed[:, pair_at(pair)])

    def grad_scores(pair, wide, space):
        for head in range(2):
            weights = probs[pair * 2 + head].astype(jnp.float32)
            grads = wide[head]
            total = jnp.sum(grads * weights, axis=0, keepdims=True)
            space[head] = low(weights * (grads - total))

    def products(pair, space):
        queries = q_ref[:, pair_at(pair)]
        keys = k_ref[:, pair_at(pair, k_at)]
        grads = grad_mixed[:, pair_at(pair)]
        keys_t = keys.T
        part_v = [matmul(probs[pair * 2 + head], grads) for head in range(2)]
        part_k = [matmul(space[head], queries) for head in range(2)]
        halves = [matmul(keys_t[head * HEAD : (head + 1) * HEAD], space[head]) for head in range(2)]
        first = head_lanes(keys.shape[0], 0)
        grad_q[:, pair_at(pair)] = low(jnp.concatenate(halves, axis=0).T * HEAD ** (-0.5))
        grad_k[:, pair_at(pair, gk_at)] = low(jnp.where(first, part_k[0], part_k[1]))
        grad_v[:, pair_at(pair, gv_at)] = low(jnp.where(first, part_v[0], part_v[1]))

    work_on_pairs(grad_weights, grad_scores, products, spaces)


def adapter_forward(branch, down, upward):
    inner = matmul(branch, down) * D ** (-0.5)
    active = low(gelu(inner))
    return branch.astype(jnp.float32) + matmul(active, upward) * ADAPT ** (-0.5), inner, active


def adapter_backward(branch, down, upward, inner, active, grad_out):
    grad_low = low(grad_out)
    grad_up = matmul_left_t(active, grad_low) * ADAPT ** (-0.5)
    grad_active = matmul_right_t(grad_low, upward) * ADAPT ** (-0.5)
    grad_inner = low(gelu_slope(inner) * grad_active)
    grad_down = matmul_left_t(branch, grad_inner) * D ** (-0.5)
    grad_branch = low(grad_out + matmul_right_t(grad_inner, down) * D ** (-0.5))
    return grad_branch, grad_down, grad_up


def self_forward_kernel(n, scalars, tokens, gains, down, up, *rest):
    refs, (qkv, probs, branch, inner_out, first_out, normed_cross, *saved, scratch, sems) = rest[: n[0]], rest[n[0] :]
    *halves, normed, mixed = saved[:-4]
    group = Group(scalars, refs, scratch, sems, True)
    fetch(tokens, group)
    inputs = tokens[...].astype(jnp.float32)
    normed[...] = low(inputs * rms_factor(inputs) * gains[0:1])
    rows = inputs.shape[0]
    key = lax.broadcasted_iota(jnp.int32, (rows, rows), 0)
    query = lax.broadcasted_iota(jnp.int32, (rows, rows), 1)
    bias = jnp.where((key <= query) & (key < scalars[3]), 0.0, -1e30)
    if halves:
        part_rows(scalars, normed[...], *halves, 0)
    for b in range(3):
        group.wait_block(b)
        product = matmul(normed[...], group.block(b))
        qkv[:, b * D : (b + 1) * D] = low(product) * (HEAD ** (-0.5) if b == 0 else 1.0)
    send(qkv)
    attend_pairs(qkv, qkv, D, qkv, 2 * D, bias, probs, mixed, saved[-4:])
    send(probs)
    group.wait_block(3)
    branch[...] = low(matmul(mixed[...], group.block(3)))
    adapted, inner, _ = adapter_forward(branch[...], down[...], up[...])
    inner_out[...] = inner
    first = inputs + adapted
    first_out[...] = first
    normed_cross[...] = low(first * rms_factor(first) * gains[1:2])
    send(branch, first_out, normed_cross)
    if halves:
        part_rows(scalars, mixed[...], *halves, D // 2)


def cross_forward_kernel(n, scalars, normed, first, memory, gains, *rest):
    refs, (queries, memory_kv, probs, second_out, normed_ffn, *saved, scratch, sems) = rest[: n[0]], rest[n[0] :]
    *halves, mixed = saved[:-4]
    group = Group(scalars, refs, scratch, sems, True)
    fetch(memory, normed, group, first)
    slot = lax.broadcasted_iota(jnp.int32, (memory.shape[0], 1), 0)
    bias = jnp.where(slot < scalars[4], 0.0, -1e30)
    if halves:
        part_rows(scalars, normed[...], *halves, 0)
        half = memory.shape[0] // 2
        for i in range(2):
            part_rows(scalars, memory[i * half : (i + 1) * half, :], *halves, (2 + i) * (D // 2))
    group.wait()
    queries[...] = low(matmul(normed[...], group.block(0))) * HEAD ** (-0.5)
    for b in range(2):
        memory_kv[:, b * D : (b + 1) * D] = low(matmul(memory[...], group.block(2 + b)))
    send(queries, memory_kv)
    attend_pairs(queries, memory_kv, 0, memory_kv, D, bias, probs, mixed, saved[-4:])
    send(probs)
    second = first[...] + matmul(mixed[...], group.block(1))
    second_out[...] = second
    normed_ffn[...] = low(second * rms_factor(second) * gains[2:3])
    send(second_out, normed_ffn)
    if halves:
        part_rows(scalars, mixed[...], *halves, D // 2)


def ffn_in_kernel(n, scalars, normed, *rest):
    refs, (slope, hidden, *halves, scratch, sems) = rest[: n[0]], rest[n[0] :]
    group = Group(scalars, refs, scratch, sems, True)
    fetch(normed, group)
    if halves:
        part_rows(scalars, normed[...], *halves, 0)
    ahead = None
    for b in range(5):
        product = ahead
        if b < 4:
            group.wait_block(b)
            ahead = matmul(normed[...], group.block(b))
        if b:
            at = slice((b - 1) * D, b * D)
            hidden_b, slope_b = gelu_both(product)
            hidden_b = low(hidden_b)
            slope[:, at] = low(slope_b)
            hidden[:, at] = hidden_b
            send_part(b - 1, slope, hidden)
            if halves:
                flat, half = hidden_b.T, D // 2
                to = slice(b * half, (b + 1) * half)
                even = scalars[2] == 0
                halves[0][to, :] = jnp.where(even, flat[:half], flat[half:])
                halves[1][to, :] = jnp.where(even, flat[half:], flat[:half])


def ffn_out_kernel(n, scalars, hidden, second, cotangent, down, up, *rest):
    refs, (mixed_out, grad_branch, grad_down, grad_up, scratch, sems) = rest[: n[0]], rest[n[0] :]
    group = Group(scalars, refs, scratch, sems, False)
    fetch(hidden, group, second, cotangent)
    rows = hidden.shape[0]
    valid = lax.broadcasted_iota(jnp.int32, (rows, 1), 0) < scalars[3]
    product = None
    for z in range(4):
        if z % 2 == 0:
            group.wait(z // 2)
        term = matmul(hidden[:, z * D : (z + 1) * D], group.quarter(z))
        product = term if product is None else product + term
    branch = low(product)
    adapted, inner, active = adapter_forward(branch, down[...], up[...])
    mixed_out[...] = low(jnp.where(valid, second[...] + adapted, 0.0))
    send(mixed_out)
    grad_result = jnp.where(valid, cotangent[...].astype(jnp.float32), 0.0)
    grad_branch[...], grad_down[...], grad_up[...] = adapter_backward(
        branch, down[...], up[...], inner, active, grad_result
    )


def ffn_back_kernel(n, scalars, grad_branch, slope, *rest):
    refs, (grad_pre, scratch, sems) = rest[: n[0]], rest[n[0] :]
    group = Group(scalars, refs, scratch, sems, False)
    fetch(grad_branch, group, slope)
    for z in range(4):
        if z % 2 == 0:
            group.wait(z // 2)
        at = slice(z * D, (z + 1) * D)
        grad_hidden = matmul_right_t(grad_branch[...], group.quarter(z))
        grad_pre[:, at] = low(slope[:, at].astype(jnp.float32) * grad_hidden)


def cross_views(pack, rows):
    side = pack.at[:, 2 * D :]
    return side.at[:rows], side.at[rows : 2 * rows], pack.at[:, : 2 * D]


def cross_back_kernel(n, scalars, grad_pre, cotangent, second, gains, queries, memory_kv, probs, *rest):
    refs, cross_refs = rest[: n[0]], rest[n[0] : n[0] + n[1]]
    (grad_second_out, grad_gain, pack, grad_mixed, *spaces, scratch, cross_scratch, sems, cross_sems) = rest[n[0] + n[1] :]
    group = Group(scalars, refs, scratch, sems, True)
    cross = Group(scalars, cross_refs, cross_scratch, cross_sems, True, (1,))
    fetch(grad_pre, group)
    rows = second.shape[0]
    valid = lax.broadcasted_iota(jnp.int32, (rows, 1), 0) < scalars[3]
    upstream = None
    for r in range(4):
        group.wait(r)
        if r == 0:
            fetch(second, cotangent, cross)
        if r == 2:
            fetch(queries, memory_kv, probs)
        term = matmul_right_t(grad_pre[:, columns_at(group.which(r))], group.place(r))
        upstream = term if upstream is None else upstream + term
    grad_result = jnp.where(valid, cotangent[...].astype(jnp.float32), 0.0)
    part, grad_gain[...] = norm_grad(second[...], gains[2:3], upstream)
    grad_second = grad_result + part
    grad_second_out[...] = grad_second
    send(grad_second_out)
    grad_cross, grad_q, _ = cross_views(pack, rows)
    grad_cross[...] = low(grad_second)
    cross.wait()
    grad_mixed[...] = low(matmul_right_t(grad_cross[...], cross.block(1)))
    attend_pairs_back(queries, memory_kv, 0, memory_kv, D, probs, grad_mixed, grad_q, pack, 0, pack, D, spaces)


def self_back_kernel(n, scalars, cross_pack, grad_second, first, gains, branch, inner, down, up, qkv, probs, *rest):
    refs, cross_refs = rest[: n[0]], rest[n[0] : n[0] + n[1]]
    (grad_first_out, grad_gain, grad_down, grad_up, pack, grad_mixed, *spaces, scratch, cross_scratch, sems, cross_sems) = rest[n[0] + n[1] :]
    cross = Group(scalars, cross_refs, cross_scratch, cross_sems, True, (0,))
    group = Group(scalars, refs, scratch, sems, True, (3,))
    fetch(cross_pack, cross, first, grad_second, branch, group, qkv, probs)
    _, grad_q, _ = cross_views(cross_pack, first.shape[0])
    cross.wait()
    upstream = matmul_right_t(grad_q[...], cross.block(0))
    part, grad_gain[...] = norm_grad(first[...], gains[1:2], upstream)
    grad_first = grad_second[...] + part
    grad_first_out[...] = grad_first
    send(grad_first_out)
    active = low(gelu(inner[...]))
    grad_branch, grad_down[...], grad_up[...] = adapter_backward(
        branch[...], down[...], up[...], inner[...], active, grad_first
    )
    pack[:, 3 * D :] = grad_branch
    group.wait()
    grad_mixed[...] = low(matmul_right_t(grad_branch, group.block(3)))
    attend_pairs_back(qkv, qkv, D, qkv, 2 * D, probs, grad_mixed, pack, pack, D, pack, 2 * D, spaces)


def rows_product(kept, at, pairs):
    total = None
    for mine, grad in zip(kept, pairs):
        term = matmul(mine[at : at + D // 2, :], grad)
        total = term if total is None else total + term
    return total


def ffn_out_grad_kernel(n, scalars, kept, got, grad, other, *rest):
    *outs, stage, sems = rest
    fetch(kept, grad, got, other)
    blocks = Blocks(scalars, outs, stage, sems)
    rows, half = D // 8, D // 2
    grads = (grad[...], other[...])
    for b in range(4):
        picked = [
            jnp.concatenate([x[(1 + z) * half + b * rows : (1 + z) * half + (b + 1) * rows, :] for z in range(4)])
            for x in (kept, got)
        ]
        blocks.put(b, matmul(picked[0], grads[0]) + matmul(picked[1], grads[1]))
    blocks.finish()


def ffn_in_grad_kernel(n, scalars, kept, got, grad, other, *rest):
    *outs, stage, sems = rest
    fetch(kept, got, grad, other)
    blocks = Blocks(scalars, outs, stage, sems)
    for b in range(4):
        at = slice(b * D, (b + 1) * D)
        grad.ready(b)
        other.ready(b)
        blocks.put(b, rows_product((kept, got), 0, (grad.inner[:, at], other.inner[:, at])))
    blocks.finish()


def cross_grads_kernel(n, scalars, kept, got, pack, other, *rest):
    *outs, stage, sems = rest
    fetch(kept, got, pack, other)
    blocks = Blocks(scalars, outs, stage, sems)
    half = D // 2
    rows = kept.shape[1]
    views = [cross_views(p.inner, rows) for p in (pack, other)]
    ready_part(0, pack, other)
    blocks.put(0, rows_product((kept, got), 0, [v[1][...] for v in views]))
    blocks.put(1, rows_product((kept, got), half, [v[0][...] for v in views]))
    for b in range(2):
        ready_part(1 + b, pack, other)
        at = slice(b * D, (b + 1) * D)
        value = rows_product((kept, got), 2 * half, [v[2][:rows, at] for v in views])
        value += rows_product((kept, got), 3 * half, [v[2][rows:, at] for v in views])
        blocks.put(2 + b, value)
    blocks.finish()


def self_grads_kernel(n, scalars, kept, got, pack, other, *rest):
    *outs, stage, sems = rest
    fetch(kept, got, pack, other)
    blocks = Blocks(scalars, outs, stage, sems)
    for b in range(4):
        at = slice(b * D, (b + 1) * D)
        part = D // 2 if b == 3 else 0
        ready_part(b, pack, other)
        blocks.put(b, rows_product((kept, got), part, (pack.inner[:, at], other.inner[:, at])))
    blocks.finish()


def combine_kernel(slots, scalars, *rest):
    count = sum(len(terms) for terms in slots)
    refs, (out, stage, out_stage, sems, out_sems) = rest[:count], rest[count:]
    copies = []
    for terms in slots:
        for index in terms:
            at = len(copies)
            source = refs[at] if index is None else refs[at].at[index]
            copies.append(pltpu.make_async_copy(source, stage.at[at], sems.at[at]))
    for copy in copies:
        copy.start()
    sent, at = [], 0
    for i, terms in enumerate(slots):
        total = None
        for _ in terms:
            copies[at].wait()
            term = stage[at].astype(jnp.float32)
            total = term if total is None else total + term
            at += 1
        out_stage[i] = low(total)
        target = out if len(slots) == 1 else out.at[:, i]
        sent.append(pltpu.make_async_copy(out_stage.at[i], target, out_sems.at[i]))
        sent[-1].start()
    for copy in sent:
        copy.wait()


def combine(name, scalars, slots):
    slots = [[term if isinstance(term, tuple) else (term, None) for term in terms] for terms in slots]
    flat = [term for terms in slots for term in terms]
    part = flat[0][0].shape[-2:]
    shape = (4,) + ((len(slots),) if len(slots) > 1 else ()) + part
    return pl.pallas_call(
        functools.partial(combine_kernel, [[index for _, index in terms] for terms in slots]),
        out_shape=jax.ShapeDtypeStruct(shape, jnp.bfloat16),
        in_specs=[pl.BlockSpec(memory_space=pltpu.SMEM)]
        + [pl.BlockSpec(memory_space=pltpu.HBM)] * len(flat),
        out_specs=pl.BlockSpec(memory_space=pltpu.HBM),
        scratch_shapes=[
            pltpu.VMEM((len(flat), 4) + part, jnp.bfloat16),
            pltpu.VMEM((len(slots), 4) + part, jnp.bfloat16),
            pltpu.SemaphoreType.DMA((len(flat),)),
            pltpu.SemaphoreType.DMA((len(slots),)),
        ],
        compiler_params=pltpu.CompilerParams(vmem_limit_bytes=63 << 20),
        cost_estimate=pl.CostEstimate(flops=1 << 28, bytes_accessed=1 << 18, transcendentals=0),
        name=name,
    )(scalars, *[array for array, _ in flat])


def plain_grads_kernel(n, scalars, left, right, out, sems):
    fetch(left, right)
    out[...] = low(matmul_left_t(left[...], right[...]))


def pick_kernel(counts, scalars, *rest):
    inputs, outs = rest[:7], rest[7 : 7 + len(counts)]
    stage, sems, out_sems = rest[7 + len(counts) :]
    rows = inputs[0].shape[0]
    qkv, sout, cq, ckv, cout, f_in, f_out = inputs

    def columns(ref):
        return [ref.at[:, pl.ds(b * D, D)] for b in range(ref.shape[1] // D)]

    groups = {
        1: columns(qkv) + [sout],
        2: [cq, cout] + columns(ckv),
        3: columns(f_in),
        4: [f_out.at[pl.ds(b * rows, rows)] for b in range(4)],
    }
    used = 0
    loads = []
    for group, many in counts:
        for i in range(many):
            for b in range(4):
                copy = pltpu.make_async_copy(groups[group][b], stage.at[used], sems.at[used])
                pl.when(scalars[0] == (b ^ 3 if i else b))(copy.start)
            loads.append(copy)
            used += 1
    sent = []
    used = 0
    for (group, many), out in zip(counts, outs):
        for i in range(many):
            loads[used].wait()
            for z in range(4):
                target = out.at[z, i] if many > 1 else out.at[z]
                copy = pltpu.make_async_copy(stage.at[used], target, out_sems.at[used * 4 + z])
                copy.start()
                sent.append(copy)
            used += 1
    for copy in sent:
        copy.wait()


def pick(scalars, shards, counts):
    rows = shards[0].shape[0]
    total = sum(many for _, many in counts)
    shapes = [((4,) if many == 1 else (4, many)) + (rows, D) for _, many in counts]
    return pl.pallas_call(
        functools.partial(pick_kernel, counts),
        out_shape=[jax.ShapeDtypeStruct(shape, jnp.bfloat16) for shape in shapes],
        in_specs=[pl.BlockSpec(memory_space=pltpu.SMEM)]
        + [pl.BlockSpec(memory_space=pltpu.HBM)] * len(shards),
        out_specs=[pl.BlockSpec(memory_space=pltpu.HBM)] * len(counts),
        scratch_shapes=[
            pltpu.VMEM((total, rows, D), jnp.bfloat16),
            pltpu.SemaphoreType.DMA((total,)),
            pltpu.SemaphoreType.DMA((total * 4,)),
        ],
        compiler_params=pltpu.CompilerParams(vmem_limit_bytes=63 << 20),
        cost_estimate=pl.CostEstimate(flops=2 << 26, bytes_accessed=2 << 16, transcendentals=0),
        name="pick",
    )(scalars, *shards)


def plain_grads_kernel(n, scalars, left, right, out, sems):
    out[...] = low(matmul_left_t(left[...], right[...]))


def memory_back_kernel(n, scalars, pack, *rest):
    refs, (memory_grad, scratch, sems) = rest[: n[0]], rest[n[0] :]
    group = Group(scalars, refs, scratch, sems, True, (2, 3))
    fetch(pack, group)
    group.wait_block(2)
    product = matmul_right_t(pack[:, :D], group.block(2))
    group.wait_block(3)
    memory_grad[...] = product + matmul_right_t(pack[:, D : 2 * D], group.block(3))


def token_back_kernel(n, scalars, grad_qkv, tokens, grad_first, gains, *rest):
    refs, (token_grad, grad_gain, scratch, sems) = rest[: n[0]], rest[n[0] :]
    group = Group(scalars, refs, scratch, sems, True, (0, 1, 2))
    fetch(grad_qkv, group, tokens, grad_first)
    group.wait_block(0)
    upstream = matmul_right_t(grad_qkv[:, :D], group.block(0))
    for b in range(1, 3):
        group.wait_block(b)
        upstream += matmul_right_t(grad_qkv[:, b * D : (b + 1) * D], group.block(b))
    part, grad_gain[...] = norm_grad(tokens[...].astype(jnp.float32), gains[0:1], upstream)
    token_grad[...] = grad_first[...] + part


def nbytes(shape, kind):
    total = jnp.dtype(kind).itemsize
    for size in shape:
        total *= size
    return total


class Moved:
    def __init__(self, outer, inner, sems, first, windows, is_input):
        self.inner, self.is_input = inner, is_input
        self.copies, self.flying, self.done = [], set(), set()
        for i, window in enumerate(windows):
            pair = (outer, inner)
            if window is not None:
                at = (pl.ds(window[0], window[1]), pl.ds(window[2], window[3]))
                pair = (outer.at[at], inner.at[at])
            self.copies.append(pltpu.make_async_copy(*(pair if is_input else pair[::-1]), sems.at[first + i]))

    def start(self, part=None):
        for i, copy in enumerate(self.copies):
            if part in (None, i) and i not in self.flying:
                copy.start()
                self.flying.add(i)

    def ready(self, part=None):
        if self.is_input:
            self.start()
            for i, copy in enumerate(self.copies):
                if part in (None, i) and i not in self.done:
                    copy.wait()
                    self.done.add(i)
        return self.inner

    def finish(self):
        self.start()
        for i, copy in enumerate(self.copies):
            if i not in self.done:
                copy.wait()

    @property
    def shape(self):
        return self.inner.shape

    @property
    def at(self):
        return self.ready().at

    def __getitem__(self, index):
        return self.ready()[index]

    def __setitem__(self, index, value):
        self.inner[index] = value


def fetch(*things):
    for thing in things:
        if isinstance(thing, (Moved, Group)):
            thing.start()


def send(*arrays):
    for array in arrays:
        if isinstance(array, Moved):
            array.start()


def send_part(part, *arrays):
    for array in arrays:
        if isinstance(array, Moved):
            array.start(part)


def inner_of(array):
    return array.inner if isinstance(array, Moved) else array


def ready(*arrays):
    for array in arrays:
        if isinstance(array, Moved):
            array.ready()


def ready_part(part, *arrays):
    for array in arrays:
        array.ready(part)


def column_blocks(shape):
    return [(0, shape[0], b * D, D) for b in range(shape[1] // D)]


def tiled(shape):
    return shape[-1] % 128 == 0 and shape[-2] % 16 == 0


def run(kernel, name, micros, scalars, arrays, groups, outs, scratch=(), direct=False, cut=None):
    n = tuple(len(group) for group in groups)
    outs, scratch = list(outs), list(scratch)
    windows = [pair[1] if isinstance(pair, tuple) else [None] for pair in arrays]
    arrays = [pair[0] if isinstance(pair, tuple) else pair for pair in arrays]
    ins = [(a.shape, a.dtype) for a in arrays]
    flat = [part for group in groups for part in group]
    moved = [pair for pair in (ins if direct else ins + outs) if tiled(pair[0])]
    rows = D // 8
    shape = (4, 2, 4, rows, D) if name in ("ffn_out", "ffn_back") else (4, 4, 2, rows, D)
    spaces = scratch + [(shape, jnp.bfloat16)] * len(groups)

    def body(scalar_ref, *refs):
        refs = list(refs)
        inputs, pieces = refs[: len(ins)], refs[len(ins) : len(ins) + len(flat)]
        results = refs[len(ins) + len(flat) :][: len(outs)]
        rest = refs[len(ins) + len(flat) + len(outs) :]
        copies, rest = rest[: len(moved)], rest[len(moved) :]
        if moved:
            sems, rest = rest[0], rest[1:]
        used, first = 0, 0
        for side, pairs in ((inputs, ins), (results, [] if direct else outs)):
            for i, (shape, _) in enumerate(pairs):
                if tiled(shape):
                    parts = windows[i] if side is inputs else (cut or {}).get(i, [None])
                    side[i] = Moved(side[i], copies[used], sems, first, parts, side is inputs)
                    used, first = used + 1, first + len(parts)
        kernel(n, scalar_ref, *inputs, *pieces, *results, *rest)
        for array in inputs + results:
            if isinstance(array, Moved):
                array.finish()

    def spec(shape):
        return pl.BlockSpec(memory_space=pltpu.HBM if tiled(shape) else pltpu.VMEM)

    return pl.pallas_call(
        body,
        out_shape=[jax.ShapeDtypeStruct(shape, kind) for shape, kind in outs],
        in_specs=[pl.BlockSpec(memory_space=pltpu.SMEM)]
        + [spec(shape) for shape, _ in ins]
        + [pl.BlockSpec(memory_space=pltpu.HBM)] * len(flat),
        out_specs=[spec(shape) for shape, _ in outs],
        scratch_shapes=[pltpu.VMEM(shape, kind) for shape, kind in moved]
        + ([pltpu.SemaphoreType.DMA((len(outs) * 4 + sum(map(len, windows)),))] if moved else [])
        + [pltpu.VMEM(shape, kind) for shape, kind in spaces]
        + [pltpu.SemaphoreType.DMA((32,)) for _ in (groups or [None])],
        compiler_params=pltpu.CompilerParams(vmem_limit_bytes=63 << 20),
        cost_estimate=pl.CostEstimate(
            flops=int(micros * 2e8), bytes_accessed=int(micros * 2e5), transcendentals=0
        ),
        name=name,
    )(scalars, *arrays, *flat)


def moves(step):
    pairs = []
    for y in range(2):
        for x in range(2):
            for z in range(4):
                for c in range(2):
                    ty, tx, tz, tc = step(y, x, z, c)
                    pairs.append((((y * 2 + x) * 4 + z) * 2 + c, ((ty * 2 + tx) * 4 + tz) * 2 + tc))
    return pairs


def swap_x(values):
    return lax.ppermute(values, BOTH, moves(lambda y, x, z, c: (y, 1 - x, z, c)))


def swap_y(values):
    return lax.ppermute(values, BOTH, moves(lambda y, x, z, c: (1 - y, x, z, c)))


def swap_core(values):
    return lax.ppermute(values, BOTH, moves(lambda y, x, z, c: (y, x, z, 1 - c)))


def turn_z(values, by):
    return lax.ppermute(values, BOTH, moves(lambda y, x, z, c: (y, x, (z + by) % 4, c)))


def after(value, *marks):
    return lax.optimization_barrier((value,) + marks)[0]


def first_swap(values):
    return lax.ppermute(
        values, BOTH, moves(lambda y, x, z, c: (y, 1 - x, z, c) if c == 0 else (1 - y, x, z, c))
    )


def second_swap(values):
    return lax.ppermute(
        values, BOTH, moves(lambda y, x, z, c: (1 - y, x, z, c) if c == 0 else (y, 1 - x, z, c))
    )


LINES = [[z * 2 + c for z in range(4)] for c in range(2)]


def spread_z(values):
    return lax.all_to_all(
        values, "fsdp", split_axis=0, concat_axis=0, tiled=True, axis_index_groups=LINES
    )


class Layer:
    def __init__(self, scalars, tokens, memory, cotangent, staged):
        self.scalars, self.tokens, self.memory, self.cotangent = scalars, tokens, memory, cotangent
        self.staged = staged
        self.t, self.m = tokens.shape[0], memory.shape[0]

    def hold(self, *marks):
        self.scalars = after(self.scalars, *marks)

    def adapters(self, generated):
        block, start = D * ADAPT, 3 * D
        self.gains = 1.0 + 0.25 * generated[:start].astype(jnp.float32).reshape(3, D)
        self.down_1 = generated[start : start + block].reshape(D, ADAPT)
        self.up_1 = generated[start + block : start + 2 * block].reshape(ADAPT, D)
        self.down_2 = generated[start + 2 * block : start + 3 * block].reshape(D, ADAPT)
        self.up_2 = generated[start + 3 * block : start + 4 * block].reshape(ADAPT, D)

    def rows(self, width=D, kind=jnp.bfloat16):
        return ((self.t, width), kind)

    def wide(self, width=D):
        return self.rows(width, jnp.float32)

    def halves(self, count):
        return [((count * (D // 2), self.t), jnp.bfloat16)] * 2

    def self_forward(self, w1):
        local = [self.rows(), self.rows()]
        outs = run(
            self_forward_kernel,
            "self_forward",
            11,
            self.scalars,
            [self.tokens, self.gains, self.down_1, self.up_1],
            [w1],
            [
                self.rows(3 * D),
                ((HEADS, self.t, self.t), jnp.bfloat16),
                self.rows(),
                self.wide(ADAPT),
                self.wide(),
                self.rows(),
            ]
            + (self.halves(2) if self.staged else local),
            scratch=(local if self.staged else []) + attend_spaces(self.t, self.t),
        )
        self.qkv, self.probs_1, self.branch_1, self.inner_1, self.first, self.normed_2 = outs[:6]
        self.saved_1 = outs[6:]

    def cross_forward(self, w2):
        local = [self.rows()]
        outs = run(
            cross_forward_kernel,
            "cross_forward",
            15,
            self.scalars,
            [self.normed_2, self.first, self.memory, self.gains],
            [w2],
            [
                self.rows(),
                ((self.m, 2 * D), jnp.bfloat16),
                ((HEADS, self.m, self.t), jnp.bfloat16),
                self.wide(),
                self.rows(),
            ]
            + (self.halves(4) if self.staged else local),
            scratch=(local if self.staged else []) + attend_spaces(self.m, self.t),
        )
        self.queries, self.memory_kv, self.probs_2, self.second, self.normed_3 = outs[:5]
        self.saved_2 = outs[5:]

    def ffn_in(self, w3):
        outs = run(
            ffn_in_kernel,
            "ffn_in",
            6,
            self.scalars,
            [self.normed_3],
            [w3],
            [self.rows(4 * D), self.rows(4 * D)] + (self.halves(5) if self.staged else []),
            cut={i: column_blocks((self.t, 4 * D)) for i in range(2)},
        )
        self.slope, self.hidden = outs[:2]
        self.saved_3 = outs[2:]

    def adapter_outs(self):
        return [((D, ADAPT), jnp.float32), ((ADAPT, D), jnp.float32)]

    def ffn_out(self, w4):
        self.mixed_out, self.grad_branch, self.grad_down_2, self.grad_up_2 = run(
            ffn_out_kernel,
            "ffn_out",
            8,
            self.scalars,
            [self.hidden, self.second, self.cotangent, self.down_2, self.up_2],
            [w4],
            [self.rows(), self.rows()] + self.adapter_outs(),
        )

    def ffn_back(self, w4):
        (self.grad_pre,) = run(
            ffn_back_kernel,
            "ffn_back",
            8,
            self.scalars,
            [self.grad_branch, self.slope],
            [w4],
            [self.rows(4 * D)],
        )

    def cross_back(self, w3, w2):
        self.grad_second, self.grad_gain_3, self.cross_pack = run(
            cross_back_kernel,
            "cross_back",
            15,
            self.scalars,
            [
                self.grad_pre,
                self.cotangent,
                self.second,
                self.gains,
                self.queries,
                self.memory_kv,
                self.probs_2,
            ],
            [w3, w2],
            [self.wide(), ((1, D), jnp.float32), ((self.m, 3 * D), jnp.bfloat16)],
            scratch=[self.rows()] + attend_spaces(self.m, self.t),
        )

    def self_back(self, w1, w2):
        self.grad_first, self.grad_gain_2, self.grad_down_1, self.grad_up_1, self.self_pack = run(
            self_back_kernel,
            "self_back",
            0.5,
            self.scalars,
            [
                (self.cross_pack, [(self.t, self.t, 2 * D, D)]),
                self.grad_second,
                self.first,
                self.gains,
                self.branch_1,
                self.inner_1,
                self.down_1,
                self.up_1,
                self.qkv,
                self.probs_1,
            ],
            [w1, w2],
            [self.wide(), ((1, D), jnp.float32)] + self.adapter_outs() + [self.rows(4 * D)],
            scratch=[self.rows()] + attend_spaces(self.t, self.t),
        )

    def token_back(self, w1):
        self.token_grad, self.grad_gain_1 = run(
            token_back_kernel,
            "token_back",
            5,
            self.scalars,
            [(self.self_pack, [(0, self.t, 0, 3 * D)]), self.tokens, self.grad_first, self.gains],
            [w1],
            [self.wide(), ((1, D), jnp.float32)],
        )

    def memory_back(self, w2):
        (self.memory_grad,) = run(
            memory_back_kernel,
            "memory_back",
            0.3,
            self.scalars,
            [(self.cross_pack, [(0, self.m, 0, 2 * D)])],
            [w2],
            [((self.m, D), jnp.float32)],
        )

    def block_grads(self, kernel, name, kept, got, grad, other, windows=None, rows=None):
        stage = ((4, 4, D // 8, D), jnp.bfloat16)
        part = ((2, 4, D // 8, D), jnp.bfloat16)
        if rows:
            kept, got = (kept, [rows + (0, self.t)]), (got, [rows + (0, self.t)])
        if windows:
            grad, other = (grad, windows), (other, windows)
        return run(
            kernel, name, 5, self.scalars, [kept, got, grad, other], [], [part, part], [stage], direct=True
        )

    def plain_grads(self, left, right):
        (out,) = run(
            plain_grads_kernel,
            "plain_grads",
            5,
            self.scalars,
            [left, right],
            [],
            [((left.shape[1], right.shape[1]), jnp.bfloat16)],
        )
        return out

    def grad_generated(self):
        return low(
            jnp.concatenate(
                [
                    0.25 * self.grad_gain_1,
                    0.25 * self.grad_gain_2,
                    0.25 * self.grad_gain_3,
                    self.grad_down_1.reshape(ADAPT, D),
                    self.grad_up_1,
                    self.grad_down_2.reshape(ADAPT, D),
                    self.grad_up_2,
                ]
            )
        ).reshape(-1)


def staged_layer(layer, where, task_ids, hidden_all, hyper_gen, shards):
    q, z, c = where[0], where[1], where[2]

    own_1, own_2, own_3, own_4 = pick(where, shards, [(1, 1), (2, 1), (3, 2), (4, 2)])
    column_1 = spread_z(own_1)
    ids = jnp.stack([task_ids, swap_core(task_ids)])
    ids_ahead = [ids] + [turn_z(ids, 4 - k) for k in (1, 2, 3)]
    gen_shard = low(matmul(hidden_all, hyper_gen))
    column_1 = after(column_1, *ids_ahead)
    near_x_1, near_y_1 = swap_x(column_1), swap_y(column_1)

    column_2 = spread_z(after(own_2, column_1))

    def pick_near(near_x, near_y, *marks):
        return jnp.where(c == 0, after(near_x, *marks), after(near_y, *marks))

    leaving_1 = pick_near(near_x_1, near_y_1)
    far_1 = second_swap(leaving_1)

    def rows_of(tasks):
        select = low(tasks[:, 0:1] == jnp.arange(TASKS, dtype=jnp.int32)[None, :])
        return after(low(matmul(select, gen_shard)), near_x_1, near_y_1, leaving_1, column_2)

    asked = [rows_of(tasks) for tasks in ids_ahead]
    turned = [turn_z(asked[k], k) for k in (1, 2, 3)]
    got = jnp.stack([asked[0]] + turned, axis=1)
    pieces = jnp.concatenate([got[0], swap_core(got[1])])
    slots = jnp.arange(8, dtype=jnp.int32)
    source = ((slots % 2) ^ c) * 4 + (z - slots // 2 + 4) % 4
    unturn = low(source[:, None] == slots[None, :])
    layer.adapters(low(matmul(unturn, pieces)).reshape(-1))

    w1 = [column_1, near_x_1, near_y_1, far_1]
    w1 += [swap_core(after(part, near_x_1)) for part in w1]

    def split(pair, *marks):
        return after(pair, *marks)[:, 0], pair[:, 1]

    def with_other(parts, *marks):
        return parts + [swap_core(after(part, *marks)) for part in parts]

    near_2 = [swap_x(column_2), swap_y(column_2)]
    pair_3 = spread_z(after(own_3, *turned))
    layer.hold(column_2)
    layer.self_forward(w1)
    leaving_2 = pick_near(*near_2, layer.normed_2)
    far_2 = second_swap(leaving_2)
    got_1 = swap_core(after(layer.saved_1[1], leaving_2))
    column_3, far_3 = split(pair_3, leaving_2)
    w2 = [column_2] + near_2 + [far_2]
    w2 += [swap_core(after(part, leaving_2)) for part in w2[:3]] + [swap_core(after(far_2, column_3))]
    near_3 = [swap_x(column_3), swap_y(column_3)]
    pair_4 = spread_z(after(own_4, column_3))
    layer.hold(got_1, column_3)
    layer.cross_forward(w2)
    layer.hold(layer.normed_3)
    w3 = with_other([column_3] + near_3 + [far_3], layer.normed_3, *near_3)
    got_2 = swap_core(after(layer.saved_2[1], *near_3))
    column_4, far_4 = split(pair_4, *near_3)
    layer.hold(got_2, column_4)
    layer.ffn_in(w3)
    near_4 = [swap_x(column_4), swap_y(column_4)]
    got_3 = swap_core(layer.saved_3[1])
    w4 = with_other([column_4] + near_4 + [far_4], layer.hidden)
    layer.hold(got_3)
    layer.ffn_out(w4)

    def first_way(sums, *marks):
        home, away = sums
        return home, first_swap(after(away, *marks))

    def leaving(*sums):
        return combine("leaving", layer.scalars, [[(home, 1), (got, 1)] for home, got in sums])

    def staying(*sums):
        return combine("staying", layer.scalars, [[(home, 0), (got, 0), part] for home, got, part in sums])

    def grads(kernel, name, kept, got, grad, other):
        windows = column_blocks(grad.shape) if grad.shape[1] > D else None
        if kernel is cross_grads_kernel:
            windows = [windows[2]] + windows[:2]
        half = D // 2
        rows = {ffn_in_grad_kernel: (0, half), ffn_out_grad_kernel: (half, 4 * half)}.get(kernel)
        return layer.block_grads(kernel, name, kept, got, grad, other, windows, rows)

    other = swap_core(layer.grad_branch)
    layer.ffn_back(w4)
    other_pre = swap_core(layer.grad_pre)
    layer.cross_back(w3, w2)
    layer.hold(layer.cross_pack)
    g4 = grads(
        ffn_out_grad_kernel, "ffn_out_grad", layer.saved_3[0], got_3, layer.grad_branch, other
    )
    s4 = first_way(g4)
    other = swap_core(after(layer.cross_pack, g4[0]))
    layer.hold(g4[0])
    g3 = grads(
        ffn_in_grad_kernel, "ffn_in_grad", layer.saved_3[0], got_3, layer.grad_pre, other_pre
    )
    s3 = first_way(g3)
    layer.hold(g3[0])
    layer.self_back(w1, w2)
    layer.hold(layer.self_pack)
    t43 = leaving(s4, s3)
    q43 = second_swap(t43)
    other_self = swap_core(after(layer.self_pack, t43))
    layer.hold(t43)
    g2 = grads(
        cross_grads_kernel, "cross_grads", layer.saved_2[0], got_2, layer.cross_pack, other
    )
    s2 = first_way(g2)
    layer.hold(g2[0])
    g1 = grads(
        self_grads_kernel, "self_grads", layer.saved_1[0], got_1, layer.self_pack, other_self
    )
    s1 = first_way(g1)
    layer.hold(g1[0])
    u43 = staying(s4 + ((q43, (slice(None), 0)),), s3 + ((q43, (slice(None), 1)),))
    sent_43 = spread_z(u43)
    layer.hold(u43)
    layer.token_back(w1)
    layer.hold(layer.token_grad)
    t2 = leaving(s2)
    q2 = second_swap(t2)
    layer.hold(t2)
    layer.memory_back(w2)
    layer.hold(layer.memory_grad)
    t1 = leaving(s1)
    q1 = second_swap(t1)
    layer.hold(t1, sent_43)
    own_4, own_3 = jnp.sum(after(sent_43, t1).astype(jnp.float32), axis=0)
    u21 = staying(s2 + (q2,), s1 + (q1,))
    sent_21 = spread_z(u21)

    pieces = after(layer.grad_generated().reshape(4, 2, -1), u21)
    mine = lax.dynamic_index_in_dim(pieces, c, 1, keepdims=False)
    theirs = lax.dynamic_index_in_dim(pieces, 1 - c, 1, keepdims=False)
    both = jnp.stack([mine, swap_core(theirs)], axis=1)
    both = lax.dynamic_slice_in_dim(jnp.concatenate([both, both]), z, 4, 0)
    terms = jnp.concatenate([both[0]] + [turn_z(both[k], k) for k in (1, 2, 3)])
    ids = jnp.concatenate([ids_ahead[(4 - k) % 4] for k in range(4)])[:, 0]
    select = low(jnp.arange(TASKS, dtype=jnp.int32)[:, None] == ids[None, :])
    task_grad = low(matmul(select, terms))
    task_grad = add_low(task_grad, swap_x(task_grad))
    task_grad = task_grad.astype(jnp.float32) + swap_y(task_grad).astype(jnp.float32)

    def sum_owners(part):
        part = part + swap_core(part)
        got = [part] + [turn_z(part, k) for k in (1, 2, 3)]
        return (got[0] + got[2]) + (got[1] + got[3])

    def share(owns):
        own = low(jnp.stack(owns))
        pair = jnp.stack([own, first_swap(own)])
        quad = jnp.concatenate([pair, second_swap(pair)])
        slots = [jnp.where(c == 0, q ^ b, ((q ^ b) % 2) * 2 + (q ^ b) // 2) for b in range(4)]
        return [
            [lax.dynamic_index_in_dim(quad, at, 0, keepdims=False)[i].astype(jnp.float32) for at in slots]
            for i in range(len(owns))
        ]

    own_2, own_1 = jnp.sum(sent_21.astype(jnp.float32), axis=0)
    g3, g4 = share([own_3, own_4])
    g2, g1 = share([own_2, own_1])
    summed = (
        jnp.concatenate(g1[:3], axis=1),
        g1[3],
        g2[0],
        jnp.concatenate(g2[2:], axis=1),
        g2[1],
        jnp.concatenate(g3, axis=1),
        jnp.concatenate(g4, axis=0),
    )
    return summed, task_grad, sum_owners


def plain_layer(layer, task_ids, hidden_all, hyper_gen, groups):
    owners = lax.axis_size("fsdp")

    def whole(shard):
        return lax.all_gather(shard, "fsdp", axis=0, tiled=True)

    w1, w2, w3 = (
        [jnp.concatenate([whole(block) for block in blocks]).reshape(4, 4, 2, D // 8, D)] for blocks in groups[:3]
    )
    w4 = [whole(jnp.concatenate(groups[3])).reshape(4, 2, 4, D // 8, D)]
    select = low(task_ids[:, None] == jnp.arange(TASKS, dtype=jnp.int32)[None, :])
    gen_shard = low(matmul(hidden_all, hyper_gen))
    gen_tasks = lax.all_gather(gen_shard, "fsdp", axis=1, tiled=True)
    layer.adapters(low(matmul(select, gen_tasks)[0]))
    layer.self_forward(w1)
    layer.cross_forward(w2)
    layer.ffn_in(w3)
    layer.ffn_out(w4)
    layer.ffn_back(w4)
    layer.cross_back(w3, w2)
    layer.self_back(w1, w2)
    layer.token_back(w1)
    layer.memory_back(w2)

    def owned(left, right):
        part = low(lax.psum_scatter(layer.plain_grads(left, right), "fsdp", scatter_dimension=0, tiled=True))
        return lax.psum(part, "dp").astype(jnp.float32)

    t = layer.t
    pack = layer.cross_pack
    summed = (
        owned(layer.saved_1[0], layer.self_pack[:, : 3 * D]),
        owned(layer.saved_1[1], layer.self_pack[:, 3 * D :]),
        owned(layer.normed_2, pack[t : 2 * t, 2 * D :]),
        owned(layer.memory, pack[:, : 2 * D]),
        owned(layer.saved_2[0], pack[:t, 2 * D :]),
        owned(layer.normed_3, layer.grad_pre),
        owned(layer.hidden, layer.grad_branch),
    )
    pieces = layer.grad_generated().reshape(owners, 1, -1)
    select = low(jnp.arange(TASKS, dtype=jnp.int32)[:, None] == task_ids[None, :])
    terms = low(select[None].astype(jnp.float32) * pieces.astype(jnp.float32))
    terms = lax.all_to_all(terms, "fsdp", split_axis=0, concat_axis=0, tiled=True)
    task_grad = low(jnp.sum(terms.astype(jnp.float32), axis=0))
    task_grad = lax.psum(task_grad, "dp").astype(jnp.float32)
    return summed, task_grad, lambda part: lax.psum(part, "fsdp")


def hyper_tail(task_grad, pre_all, hidden_all, task_table, hyper_in, hyper_gen, sum_owners):
    grad_hyper_gen = jnp.dot(
        hidden_all.astype(jnp.float32).T, task_grad, precision=lax.Precision.HIGHEST
    )
    grad_hidden = jnp.dot(
        task_grad, hyper_gen.astype(jnp.float32).T, precision=lax.Precision.HIGHEST
    )
    grad_pre_all = gelu_slope(pre_all) * sum_owners(grad_hidden)
    grad_table = jnp.dot(grad_pre_all, hyper_in.T, precision=lax.Precision.HIGHEST)
    grad_first = jnp.dot(task_table.T, grad_pre_all, precision=lax.Precision.HIGHEST)
    return grad_table, grad_first, grad_hyper_gen


def shards(
    tokens,
    memory,
    target_lengths,
    memory_lengths,
    task_ids,
    cotangent,
    self_qkv,
    self_out,
    cross_q,
    cross_kv,
    cross_out,
    ffn_in,
    ffn_out,
    task_table,
    hyper_in,
    hyper_gen,
):
    staged = lax.axis_size("fsdp") == 8 and lax.axis_size("dp") == 4
    pre_all = jnp.dot(task_table, hyper_in, precision=lax.Precision.HIGHEST)
    hidden_all = low(jax.nn.gelu(pre_all))

    def columns(shard):
        return [shard[:, b * D : (b + 1) * D] for b in range(shard.shape[1] // D)]

    q = lax.axis_index("dp").astype(jnp.int32)
    f = lax.axis_index("fsdp").astype(jnp.int32)
    where = jnp.stack([q, f // 2, f % 2])
    scalars = jnp.concatenate([where, target_lengths, memory_lengths])
    layer = Layer(scalars, tokens, memory, cotangent, staged)
    if staged:
        summed, task_grad, sum_owners = staged_layer(
            layer,
            where,
            task_ids,
            hidden_all,
            hyper_gen,
            (self_qkv, self_out, cross_q, cross_kv, cross_out, ffn_in, ffn_out),
        )
    else:
        rows = self_qkv.shape[0]
        groups = (
            columns(self_qkv) + [self_out],
            [cross_q, cross_out] + columns(cross_kv),
            columns(ffn_in),
            [ffn_out[b * rows : (b + 1) * rows] for b in range(4)],
        )
        summed, task_grad, sum_owners = plain_layer(layer, task_ids, hidden_all, hyper_gen, groups)
    grad_table, grad_first, grad_hyper_gen = hyper_tail(
        task_grad, pre_all, hidden_all, task_table, hyper_in, hyper_gen, sum_owners
    )
    return (
        (layer.mixed_out, layer.token_grad, layer.memory_grad)
        + summed
        + (grad_table, grad_first, grad_hyper_gen)
    )


def solution(mesh):
    by_both = P(("dp", "fsdp"), None)
    by_rows = P("fsdp", None)
    return jax.shard_map(
        shards,
        mesh=mesh,
        in_specs=(by_both, by_both)
        + (P(("dp", "fsdp")),) * 3
        + (by_both,)
        + (by_rows,) * 7
        + (P(), P(), P(None, "fsdp")),
        out_specs=(by_both,) * 3 + (by_rows,) * 7 + (P(), P(), P(None, "fsdp")),
        check_vma=False,
    )
```

```python
import functools

import jax
import jax.numpy as jnp
from jax import lax
from jax.experimental import pallas as pl
from jax.experimental.pallas import tpu as pltpu
from jax.sharding import PartitionSpec as P

D = 768
HEADS = 12
HEAD = 64
ADAPT = 24
TASKS = 8
BOTH = ("dp", "fsdp")


def matmul(left, right):
    return jnp.dot(left, right, preferred_element_type=jnp.float32)


def matmul_left_t(left, right):
    return lax.dot_general(
        left, right, (((0,), (0,)), ((), ())), preferred_element_type=jnp.float32
    )


def matmul_right_t(left, right):
    return lax.dot_general(
        left, right, (((1,), (1,)), ((), ())), preferred_element_type=jnp.float32
    )


def low(values):
    return values.astype(jnp.bfloat16)


def add_low(left, right):
    return low(left.astype(jnp.float32) + right.astype(jnp.float32))


def rms_factor(values):
    return lax.rsqrt(jnp.mean(values * values, axis=-1, keepdims=True) + 1e-06)


def norm_grad(values, gains, upstream):
    factor = rms_factor(values)
    scaled = upstream * gains
    mean = jnp.mean(values * scaled, axis=-1, keepdims=True)
    part = factor * scaled - values * (factor * factor * factor * mean)
    return part, jnp.sum(upstream * values * factor, axis=0, keepdims=True)


GELU_A = 0.7978845608
GELU_B = 0.044715


def gelu(values):
    inside = GELU_A * (values + GELU_B * values * values * values)
    return 0.5 * values * (1.0 + jnp.tanh(inside))


def gelu_both(values):
    square = values * values
    curve = jnp.tanh(GELU_A * (values + GELU_B * square * values))
    inner = GELU_A * (1.0 + 3.0 * GELU_B * square)
    half = 0.5 * (1.0 + curve)
    return values * half, half + 0.5 * values * (1.0 - curve * curve) * inner


def gelu_slope(values):
    square = values * values
    curve = jnp.tanh(GELU_A * (values + GELU_B * square * values))
    inner = GELU_A * (1.0 + 3.0 * GELU_B * square)
    return 0.5 * (1.0 + curve) + 0.5 * values * (1.0 - curve * curve) * inner


class Group:
    def __init__(self, scalars, refs, scratch, sems, by_block, blocks=(0, 1, 2, 3)):
        self.scalars, self.refs, self.scratch, self.sems = scalars, refs, scratch, sems
        self.by_block, self.blocks = by_block, blocks
        self.staged = len(refs) > 1
        self.waited = False

    def _each(self, act, part=None):
        if not self.staged:
            act(pltpu.make_async_copy(self.refs[0], self.scratch, self.sems.at[0]))
            return
        c = self.scalars[2]
        for place in range(4):
            block = self.which(place)

            def parts(place=place, block=block):
                for side in range(2):
                    source = self.refs[side * 4 + place]
                    if self.by_block and part in (None, place):
                        target = self.scratch.at[place, :, c ^ side]
                        act(pltpu.make_async_copy(source, target, self.sems.at[place * 2 + side]))
                    if not self.by_block:
                        for half in range(2):
                            if part in (None, half):
                                at = pl.ds(half * 2, 2)
                                act(
                                    pltpu.make_async_copy(
                                        source.at[at],
                                        self.scratch.at[at, c ^ side, block],
                                        self.sems.at[(place * 2 + side) * 2 + half],
                                    )
                                )

            if len(self.blocks) == 4:
                parts()
            else:
                wanted = block == self.blocks[0]
                for other in self.blocks[1:]:
                    wanted = wanted | (block == other)
                pl.when(wanted)(parts)

    def start(self):
        self._each(lambda copy: copy.start())

    def wait(self, part=None):
        if self.staged:
            self._each(lambda copy: copy.wait(), part)
        elif not self.waited:
            self._each(lambda copy: copy.wait())
            self.waited = True

    def wait_block(self, index):
        if not self.staged:
            self.wait()
            return
        place, c = self.which(index), self.scalars[2]
        for side in range(2):
            target = self.scratch.at[place, :, c ^ side]
            pltpu.make_async_copy(self.refs[0], target, self.sems.at[place * 2 + side]).wait()

    def place(self, place):
        return self.scratch[place].reshape(D, D)

    def which(self, place):
        return self.scalars[0] ^ place if self.staged else place

    def block(self, index):
        return self.scratch[self.which(index)].reshape(D, D)

    def quarter(self, z):
        return self.scratch[z].reshape(D, D)


def columns_at(block):
    return pl.ds(pl.multiple_of(block * D, D), D)


def part_rows(scalars, value, keep, send, at):
    flat = value.T
    rows = flat.shape[0] // 8
    for parity in range(2):
        here = scalars[2] == parity

        @pl.when(here)
        def _():
            for z in range(4):
                piece = flat[(z * 2 + parity) * rows : (z * 2 + parity + 1) * rows]
                keep[at + z * rows : at + (z + 1) * rows, :] = piece

        @pl.when(jnp.logical_not(here))
        def _():
            for z in range(4):
                piece = flat[(z * 2 + parity) * rows : (z * 2 + parity + 1) * rows]
                send[at + z * rows : at + (z + 1) * rows, :] = piece


class Blocks:
    def __init__(self, scalars, outs, stage, sems):
        self.scalars, self.outs, self.stage, self.sems = scalars, outs, stage, sems
        self.sent = []

    def put(self, block, value):
        rows = value.shape[0] // 4
        value = low(value)
        for z in range(4):
            self.stage[block, z] = value[z * rows : (z + 1) * rows]
        r, c = self.scalars[0] ^ block, self.scalars[2]
        first = jnp.where(c == 0, r % 2, r // 2)
        second = jnp.where(c == 0, r // 2, r % 2)
        for way, out in enumerate(self.outs):
            copy = pltpu.make_async_copy(self.stage.at[block], out.at[second], self.sems.at[block * 2 + way])
            pl.when(first == way)(copy.start)
            self.sent.append((first == way, copy))

    def finish(self):
        for here, copy in self.sent:
            pl.when(here)(copy.wait)


def head_lanes(rows, head):
    lane = lax.broadcasted_iota(jnp.int32, (rows, 128), 1)
    return lane < HEAD if head == 0 else lane >= HEAD


def pick_head(values, head):
    return jnp.where(head_lanes(values.shape[0], head), values, jnp.zeros_like(values))


def pair_at(pair, base=0):
    return pl.ds(pl.multiple_of(base + pair * 128, 128), 128)


def work_on_pairs(first, middle, last, spaces):
    wide, low_spaces = spaces[:2], spaces[2:]
    pairs = HEADS // 2
    first(0, wide[0])

    @pl.loop(0, pairs // 2)
    def _(turn):
        for i in range(2):
            pair = turn * 2 + i
            first(jnp.minimum(pair + 1, pairs - 1), wide[1 - i])
            middle(pair, wide[i], low_spaces[i])
            last(jnp.maximum(pair - 1, 0), low_spaces[1 - i])

    last(pairs - 1, low_spaces[1])


def attend_spaces(keys, queries):
    shape = (2, keys, queries)
    return [(shape, jnp.float32)] * 2 + [(shape, jnp.bfloat16)] * 2


def attend_pairs(q_ref, k_ref, k_at, v_ref, v_at, bias, probs, mixed, spaces):
    ready(q_ref, k_ref, v_ref)
    q_ref, k_ref, v_ref, probs = (inner_of(ref) for ref in (q_ref, k_ref, v_ref, probs))

    def scores_of(pair, wide):
        keys = k_ref[:, pair_at(pair, k_at)]
        for head in range(2):
            wide[head] = matmul_right_t(pick_head(keys, head), q_ref[:, pair_at(pair)])

    def weights_of(pair, wide, space):
        for head in range(2):
            scores = wide[head] + bias
            weights = jnp.exp(scores - jnp.max(scores, axis=0, keepdims=True))
            weights = low(weights * (1.0 / jnp.sum(weights, axis=0, keepdims=True)))
            space[head] = weights
            probs[pair * 2 + head] = weights

    def mix(pair, space):
        values = v_ref[:, pair_at(pair, v_at)].T
        halves = [matmul(values[head * HEAD : (head + 1) * HEAD], space[head]) for head in range(2)]
        mixed[:, pair_at(pair)] = low(jnp.concatenate(halves, axis=0).T)

    work_on_pairs(scores_of, weights_of, mix, spaces)


def attend_pairs_back(
    q_ref, k_ref, k_at, v_ref, v_at, probs, grad_mixed, grad_q, grad_k, gk_at, grad_v, gv_at, spaces
):
    ready(q_ref, k_ref, v_ref, probs)
    q_ref, k_ref, v_ref, probs = (inner_of(ref) for ref in (q_ref, k_ref, v_ref, probs))
    grad_q, grad_k, grad_v = (inner_of(ref) for ref in (grad_q, grad_k, grad_v))

    def grad_weights(pair, wide):
        values = v_ref[:, pair_at(pair, v_at)]
        for head in range(2):
            wide[head] = matmul_right_t(pick_head(values, head), grad_mixed[:, pair_at(pair)])

    def grad_scores(pair, wide, space):
        for head in range(2):
            weights = probs[pair * 2 + head].astype(jnp.float32)
            grads = wide[head]
            total = jnp.sum(grads * weights, axis=0, keepdims=True)
            space[head] = low(weights * (grads - total))

    def products(pair, space):
        queries = q_ref[:, pair_at(pair)]
        keys = k_ref[:, pair_at(pair, k_at)]
        grads = grad_mixed[:, pair_at(pair)]
        keys_t = keys.T
        part_v = [matmul(probs[pair * 2 + head], grads) for head in range(2)]
        part_k = [matmul(space[head], queries) for head in range(2)]
        halves = [matmul(keys_t[head * HEAD : (head + 1) * HEAD], space[head]) for head in range(2)]
        first = head_lanes(keys.shape[0], 0)
        grad_q[:, pair_at(pair)] = low(jnp.concatenate(halves, axis=0).T * HEAD ** (-0.5))
        grad_k[:, pair_at(pair, gk_at)] = low(jnp.where(first, part_k[0], part_k[1]))
        grad_v[:, pair_at(pair, gv_at)] = low(jnp.where(first, part_v[0], part_v[1]))

    work_on_pairs(grad_weights, grad_scores, products, spaces)


def adapter_forward(branch, down, upward):
    inner = matmul(branch, down) * D ** (-0.5)
    active = low(gelu(inner))
    return branch.astype(jnp.float32) + matmul(active, upward) * ADAPT ** (-0.5), inner, active


def adapter_backward(branch, down, upward, inner, active, grad_out):
    grad_low = low(grad_out)
    grad_up = matmul_left_t(active, grad_low) * ADAPT ** (-0.5)
    grad_active = matmul_right_t(grad_low, upward) * ADAPT ** (-0.5)
    grad_inner = low(gelu_slope(inner) * grad_active)
    grad_down = matmul_left_t(branch, grad_inner) * D ** (-0.5)
    grad_branch = low(grad_out + matmul_right_t(grad_inner, down) * D ** (-0.5))
    return grad_branch, grad_down, grad_up


def self_forward_kernel(n, scalars, tokens, gains, down, up, *rest):
    refs, (qkv, probs, branch, inner_out, first_out, normed_cross, *saved, scratch, sems) = rest[: n[0]], rest[n[0] :]
    *halves, normed, mixed = saved[:-4]
    group = Group(scalars, refs, scratch, sems, True)
    fetch(tokens, group)
    inputs = tokens[...].astype(jnp.float32)
    normed[...] = low(inputs * rms_factor(inputs) * gains[0:1])
    rows = inputs.shape[0]
    key = lax.broadcasted_iota(jnp.int32, (rows, rows), 0)
    query = lax.broadcasted_iota(jnp.int32, (rows, rows), 1)
    bias = jnp.where((key <= query) & (key < scalars[3]), 0.0, -1e30)
    if halves:
        part_rows(scalars, normed[...], *halves, 0)
    for b in range(3):
        group.wait_block(b)
        product = matmul(normed[...], group.block(b))
        qkv[:, b * D : (b + 1) * D] = low(product) * (HEAD ** (-0.5) if b == 0 else 1.0)
    send(qkv)
    attend_pairs(qkv, qkv, D, qkv, 2 * D, bias, probs, mixed, saved[-4:])
    send(probs)
    group.wait_block(3)
    branch[...] = low(matmul(mixed[...], group.block(3)))
    adapted, inner, _ = adapter_forward(branch[...], down[...], up[...])
    inner_out[...] = inner
    first = inputs + adapted
    first_out[...] = first
    normed_cross[...] = low(first * rms_factor(first) * gains[1:2])
    send(branch, first_out, normed_cross)
    if halves:
        part_rows(scalars, mixed[...], *halves, D // 2)


def cross_forward_kernel(n, scalars, normed, first, memory, gains, *rest):
    refs, (queries, memory_kv, probs, second_out, normed_ffn, *saved, scratch, sems) = rest[: n[0]], rest[n[0] :]
    *halves, mixed = saved[:-4]
    group = Group(scalars, refs, scratch, sems, True)
    fetch(memory, normed, group, first)
    slot = lax.broadcasted_iota(jnp.int32, (memory.shape[0], 1), 0)
    bias = jnp.where(slot < scalars[4], 0.0, -1e30)
    if halves:
        part_rows(scalars, normed[...], *halves, 0)
        half = memory.shape[0] // 2
        for i in range(2):
            part_rows(scalars, memory[i * half : (i + 1) * half, :], *halves, (2 + i) * (D // 2))
    group.wait()
    queries[...] = low(matmul(normed[...], group.block(0))) * HEAD ** (-0.5)
    for b in range(2):
        memory_kv[:, b * D : (b + 1) * D] = low(matmul(memory[...], group.block(2 + b)))
    send(queries, memory_kv)
    attend_pairs(queries, memory_kv, 0, memory_kv, D, bias, probs, mixed, saved[-4:])
    send(probs)
    second = first[...] + matmul(mixed[...], group.block(1))
    second_out[...] = second
    normed_ffn[...] = low(second * rms_factor(second) * gains[2:3])
    send(second_out, normed_ffn)
    if halves:
        part_rows(scalars, mixed[...], *halves, D // 2)


def ffn_in_kernel(n, scalars, normed, *rest):
    refs, (slope, hidden, *halves, scratch, sems) = rest[: n[0]], rest[n[0] :]
    group = Group(scalars, refs, scratch, sems, True)
    fetch(normed, group)
    if halves:
        part_rows(scalars, normed[...], *halves, 0)
    ahead = None
    for b in range(5):
        product = ahead
        if b < 4:
            group.wait_block(b)
            ahead = matmul(normed[...], group.block(b))
        if b:
            at = slice((b - 1) * D, b * D)
            hidden_b, slope_b = gelu_both(product)
            hidden_b = low(hidden_b)
            slope[:, at] = low(slope_b)
            hidden[:, at] = hidden_b
            send_part(b - 1, slope, hidden)
            if halves:
                flat, half = hidden_b.T, D // 2
                to = slice(b * half, (b + 1) * half)
                even = scalars[2] == 0
                halves[0][to, :] = jnp.where(even, flat[:half], flat[half:])
                halves[1][to, :] = jnp.where(even, flat[half:], flat[:half])


def ffn_out_kernel(n, scalars, hidden, second, cotangent, down, up, *rest):
    refs, (mixed_out, grad_branch, grad_down, grad_up, scratch, sems) = rest[: n[0]], rest[n[0] :]
    group = Group(scalars, refs, scratch, sems, False)
    fetch(hidden, group, second, cotangent)
    rows = hidden.shape[0]
    valid = lax.broadcasted_iota(jnp.int32, (rows, 1), 0) < scalars[3]
    product = None
    for z in range(4):
        if z % 2 == 0:
            group.wait(z // 2)
        term = matmul(hidden[:, z * D : (z + 1) * D], group.quarter(z))
        product = term if product is None else product + term
    branch = low(product)
    adapted, inner, active = adapter_forward(branch, down[...], up[...])
    mixed_out[...] = low(jnp.where(valid, second[...] + adapted, 0.0))
    send(mixed_out)
    grad_result = jnp.where(valid, cotangent[...].astype(jnp.float32), 0.0)
    grad_branch[...], grad_down[...], grad_up[...] = adapter_backward(
        branch, down[...], up[...], inner, active, grad_result
    )


def ffn_back_kernel(n, scalars, grad_branch, slope, *rest):
    refs, (grad_pre, scratch, sems) = rest[: n[0]], rest[n[0] :]
    group = Group(scalars, refs, scratch, sems, False)
    fetch(grad_branch, group, slope)
    for z in range(4):
        if z % 2 == 0:
            group.wait(z // 2)
        at = slice(z * D, (z + 1) * D)
        grad_hidden = matmul_right_t(grad_branch[...], group.quarter(z))
        grad_pre[:, at] = low(slope[:, at].astype(jnp.float32) * grad_hidden)


def cross_views(pack, rows):
    side = pack.at[:, 2 * D :]
    return side.at[:rows], side.at[rows : 2 * rows], pack.at[:, : 2 * D]


def cross_back_kernel(n, scalars, grad_pre, cotangent, second, gains, queries, memory_kv, probs, *rest):
    refs, cross_refs = rest[: n[0]], rest[n[0] : n[0] + n[1]]
    (grad_second_out, grad_gain, pack, grad_mixed, *spaces, scratch, cross_scratch, sems, cross_sems) = rest[n[0] + n[1] :]
    group = Group(scalars, refs, scratch, sems, True)
    cross = Group(scalars, cross_refs, cross_scratch, cross_sems, True, (1,))
    fetch(grad_pre, group)
    rows = second.shape[0]
    valid = lax.broadcasted_iota(jnp.int32, (rows, 1), 0) < scalars[3]
    upstream = None
    for r in range(4):
        group.wait(r)
        if r == 0:
            fetch(second, cotangent, cross)
        if r == 2:
            fetch(queries, memory_kv, probs)
        term = matmul_right_t(grad_pre[:, columns_at(group.which(r))], group.place(r))
        upstream = term if upstream is None else upstream + term
    grad_result = jnp.where(valid, cotangent[...].astype(jnp.float32), 0.0)
    part, grad_gain[...] = norm_grad(second[...], gains[2:3], upstream)
    grad_second = grad_result + part
    grad_second_out[...] = grad_second
    send(grad_second_out)
    grad_cross, grad_q, _ = cross_views(pack, rows)
    grad_cross[...] = low(grad_second)
    cross.wait()
    grad_mixed[...] = low(matmul_right_t(grad_cross[...], cross.block(1)))
    attend_pairs_back(queries, memory_kv, 0, memory_kv, D, probs, grad_mixed, grad_q, pack, 0, pack, D, spaces)


def self_back_kernel(n, scalars, cross_pack, grad_second, first, gains, branch, inner, down, up, qkv, probs, *rest):
    refs, cross_refs = rest[: n[0]], rest[n[0] : n[0] + n[1]]
    (grad_first_out, grad_gain, grad_down, grad_up, pack, grad_mixed, *spaces, scratch, cross_scratch, sems, cross_sems) = rest[n[0] + n[1] :]
    cross = Group(scalars, cross_refs, cross_scratch, cross_sems, True, (0,))
    group = Group(scalars, refs, scratch, sems, True, (3,))
    fetch(cross_pack, cross, first, grad_second, branch, group, qkv, probs)
    _, grad_q, _ = cross_views(cross_pack, first.shape[0])
    cross.wait()
    upstream = matmul_right_t(grad_q[...], cross.block(0))
    part, grad_gain[...] = norm_grad(first[...], gains[1:2], upstream)
    grad_first = grad_second[...] + part
    grad_first_out[...] = grad_first
    send(grad_first_out)
    active = low(gelu(inner[...]))
    grad_branch, grad_down[...], grad_up[...] = adapter_backward(
        branch[...], down[...], up[...], inner[...], active, grad_first
    )
    pack[:, 3 * D :] = grad_branch
    group.wait()
    grad_mixed[...] = low(matmul_right_t(grad_branch, group.block(3)))
    attend_pairs_back(qkv, qkv, D, qkv, 2 * D, probs, grad_mixed, pack, pack, D, pack, 2 * D, spaces)


def rows_product(kept, at, pairs):
    total = None
    for mine, grad in zip(kept, pairs):
        term = matmul(mine[at : at + D // 2, :], grad)
        total = term if total is None else total + term
    return total


def ffn_out_grad_kernel(n, scalars, kept, got, grad, other, *rest):
    *outs, stage, sems = rest
    fetch(kept, grad, got, other)
    blocks = Blocks(scalars, outs, stage, sems)
    rows, half = D // 8, D // 2
    grads = (grad[...], other[...])
    for b in range(4):
        picked = [
            jnp.concatenate([x[(1 + z) * half + b * rows : (1 + z) * half + (b + 1) * rows, :] for z in range(4)])
            for x in (kept, got)
        ]
        blocks.put(b, matmul(picked[0], grads[0]) + matmul(picked[1], grads[1]))
    blocks.finish()


def ffn_in_grad_kernel(n, scalars, kept, got, grad, other, *rest):
    *outs, stage, sems = rest
    fetch(kept, got, grad, other)
    blocks = Blocks(scalars, outs, stage, sems)
    for b in range(4):
        at = slice(b * D, (b + 1) * D)
        grad.ready(b)
        other.ready(b)
        blocks.put(b, rows_product((kept, got), 0, (grad.inner[:, at], other.inner[:, at])))
    blocks.finish()


def cross_grads_kernel(n, scalars, kept, got, pack, other, *rest):
    *outs, stage, sems = rest
    fetch(kept, got, pack, other)
    blocks = Blocks(scalars, outs, stage, sems)
    half = D // 2
    rows = kept.shape[1]
    views = [cross_views(p.inner, rows) for p in (pack, other)]
    ready_part(0, pack, other)
    blocks.put(0, rows_product((kept, got), 0, [v[1][...] for v in views]))
    blocks.put(1, rows_product((kept, got), half, [v[0][...] for v in views]))
    for b in range(2):
        ready_part(1 + b, pack, other)
        at = slice(b * D, (b + 1) * D)
        value = rows_product((kept, got), 2 * half, [v[2][:rows, at] for v in views])
        value += rows_product((kept, got), 3 * half, [v[2][rows:, at] for v in views])
        blocks.put(2 + b, value)
    blocks.finish()


def self_grads_kernel(n, scalars, kept, got, pack, other, *rest):
    *outs, stage, sems = rest
    fetch(kept, got, pack, other)
    blocks = Blocks(scalars, outs, stage, sems)
    for b in range(4):
        at = slice(b * D, (b + 1) * D)
        part = D // 2 if b == 3 else 0
        ready_part(b, pack, other)
        blocks.put(b, rows_product((kept, got), part, (pack.inner[:, at], other.inner[:, at])))
    blocks.finish()


def combine_kernel(slots, scalars, *rest):
    count = sum(len(terms) for terms in slots)
    refs, (out, stage, out_stage, sems, out_sems) = rest[:count], rest[count:]
    copies = []
    for terms in slots:
        for index in terms:
            at = len(copies)
            source = refs[at] if index is None else refs[at].at[index]
            copies.append(pltpu.make_async_copy(source, stage.at[at], sems.at[at]))
    for copy in copies:
        copy.start()
    sent, at = [], 0
    for i, terms in enumerate(slots):
        total = None
        for _ in terms:
            copies[at].wait()
            term = stage[at].astype(jnp.float32)
            total = term if total is None else total + term
            at += 1
        out_stage[i] = low(total)
        target = out if len(slots) == 1 else out.at[:, i]
        sent.append(pltpu.make_async_copy(out_stage.at[i], target, out_sems.at[i]))
        sent[-1].start()
    for copy in sent:
        copy.wait()


def combine(name, scalars, slots):
    slots = [[term if isinstance(term, tuple) else (term, None) for term in terms] for terms in slots]
    flat = [term for terms in slots for term in terms]
    part = flat[0][0].shape[-2:]
    shape = (4,) + ((len(slots),) if len(slots) > 1 else ()) + part
    return pl.pallas_call(
        functools.partial(combine_kernel, [[index for _, index in terms] for terms in slots]),
        out_shape=jax.ShapeDtypeStruct(shape, jnp.bfloat16),
        in_specs=[pl.BlockSpec(memory_space=pltpu.SMEM)]
        + [pl.BlockSpec(memory_space=pltpu.HBM)] * len(flat),
        out_specs=pl.BlockSpec(memory_space=pltpu.HBM),
        scratch_shapes=[
            pltpu.VMEM((len(flat), 4) + part, jnp.bfloat16),
            pltpu.VMEM((len(slots), 4) + part, jnp.bfloat16),
            pltpu.SemaphoreType.DMA((len(flat),)),
            pltpu.SemaphoreType.DMA((len(slots),)),
        ],
        compiler_params=pltpu.CompilerParams(vmem_limit_bytes=63 << 20),
        cost_estimate=pl.CostEstimate(flops=1 << 28, bytes_accessed=1 << 18, transcendentals=0),
        name=name,
    )(scalars, *[array for array, _ in flat])


def plain_grads_kernel(n, scalars, left, right, out, sems):
    fetch(left, right)
    out[...] = low(matmul_left_t(left[...], right[...]))


def pick_kernel(counts, scalars, *rest):
    inputs, outs = rest[:7], rest[7 : 7 + len(counts)]
    stage, sems, out_sems = rest[7 + len(counts) :]
    rows = inputs[0].shape[0]
    qkv, sout, cq, ckv, cout, f_in, f_out = inputs

    def columns(ref):
        return [ref.at[:, pl.ds(b * D, D)] for b in range(ref.shape[1] // D)]

    groups = {
        1: columns(qkv) + [sout],
        2: [cq, cout] + columns(ckv),
        3: columns(f_in),
        4: [f_out.at[pl.ds(b * rows, rows)] for b in range(4)],
    }
    used = 0
    loads = []
    for group, many in counts:
        for i in range(many):
            for b in range(4):
                copy = pltpu.make_async_copy(groups[group][b], stage.at[used], sems.at[used])
                pl.when(scalars[0] == (b ^ 3 if i else b))(copy.start)
            loads.append(copy)
            used += 1
    sent = []
    used = 0
    for (group, many), out in zip(counts, outs):
        for i in range(many):
            loads[used].wait()
            for z in range(4):
                target = out.at[z, i] if many > 1 else out.at[z]
                copy = pltpu.make_async_copy(stage.at[used], target, out_sems.at[used * 4 + z])
                copy.start()
                sent.append(copy)
            used += 1
    for copy in sent:
        copy.wait()


def pick(scalars, shards, counts):
    rows = shards[0].shape[0]
    total = sum(many for _, many in counts)
    shapes = [((4,) if many == 1 else (4, many)) + (rows, D) for _, many in counts]
    return pl.pallas_call(
        functools.partial(pick_kernel, counts),
        out_shape=[jax.ShapeDtypeStruct(shape, jnp.bfloat16) for shape in shapes],
        in_specs=[pl.BlockSpec(memory_space=pltpu.SMEM)]
        + [pl.BlockSpec(memory_space=pltpu.HBM)] * len(shards),
        out_specs=[pl.BlockSpec(memory_space=pltpu.HBM)] * len(counts),
        scratch_shapes=[
            pltpu.VMEM((total, rows, D), jnp.bfloat16),
            pltpu.SemaphoreType.DMA((total,)),
            pltpu.SemaphoreType.DMA((total * 4,)),
        ],
        compiler_params=pltpu.CompilerParams(vmem_limit_bytes=63 << 20),
        cost_estimate=pl.CostEstimate(flops=2 << 26, bytes_accessed=2 << 16, transcendentals=0),
        name="pick",
    )(scalars, *shards)


def plain_grads_kernel(n, scalars, left, right, out, sems):
    out[...] = low(matmul_left_t(left[...], right[...]))


def memory_back_kernel(n, scalars, pack, *rest):
    refs, (memory_grad, scratch, sems) = rest[: n[0]], rest[n[0] :]
    group = Group(scalars, refs, scratch, sems, True, (2, 3))
    fetch(pack, group)
    group.wait_block(2)
    product = matmul_right_t(pack[:, :D], group.block(2))
    group.wait_block(3)
    memory_grad[...] = product + matmul_right_t(pack[:, D : 2 * D], group.block(3))


def token_back_kernel(n, scalars, grad_qkv, tokens, grad_first, gains, *rest):
    refs, (token_grad, grad_gain, scratch, sems) = rest[: n[0]], rest[n[0] :]
    group = Group(scalars, refs, scratch, sems, True, (0, 1, 2))
    fetch(grad_qkv, group, tokens, grad_first)
    group.wait_block(0)
    upstream = matmul_right_t(grad_qkv[:, :D], group.block(0))
    for b in range(1, 3):
        group.wait_block(b)
        upstream += matmul_right_t(grad_qkv[:, b * D : (b + 1) * D], group.block(b))
    part, grad_gain[...] = norm_grad(tokens[...].astype(jnp.float32), gains[0:1], upstream)
    token_grad[...] = grad_first[...] + part


def nbytes(shape, kind):
    total = jnp.dtype(kind).itemsize
    for size in shape:
        total *= size
    return total


class Moved:
    def __init__(self, outer, inner, sems, first, windows, is_input):
        self.inner, self.is_input = inner, is_input
        self.copies, self.flying, self.done = [], set(), set()
        for i, window in enumerate(windows):
            pair = (outer, inner)
            if window is not None:
                at = (pl.ds(window[0], window[1]), pl.ds(window[2], window[3]))
                pair = (outer.at[at], inner.at[at])
            self.copies.append(pltpu.make_async_copy(*(pair if is_input else pair[::-1]), sems.at[first + i]))

    def start(self, part=None):
        for i, copy in enumerate(self.copies):
            if part in (None, i) and i not in self.flying:
                copy.start()
                self.flying.add(i)

    def ready(self, part=None):
        if self.is_input:
            self.start()
            for i, copy in enumerate(self.copies):
                if part in (None, i) and i not in self.done:
                    copy.wait()
                    self.done.add(i)
        return self.inner

    def finish(self):
        self.start()
        for i, copy in enumerate(self.copies):
            if i not in self.done:
                copy.wait()

    @property
    def shape(self):
        return self.inner.shape

    @property
    def at(self):
        return self.ready().at

    def __getitem__(self, index):
        return self.ready()[index]

    def __setitem__(self, index, value):
        self.inner[index] = value


def fetch(*things):
    for thing in things:
        if isinstance(thing, (Moved, Group)):
            thing.start()


def send(*arrays):
    for array in arrays:
        if isinstance(array, Moved):
            array.start()


def send_part(part, *arrays):
    for array in arrays:
        if isinstance(array, Moved):
            array.start(part)


def inner_of(array):
    return array.inner if isinstance(array, Moved) else array


def ready(*arrays):
    for array in arrays:
        if isinstance(array, Moved):
            array.ready()


def ready_part(part, *arrays):
    for array in arrays:
        array.ready(part)


def column_blocks(shape):
    return [(0, shape[0], b * D, D) for b in range(shape[1] // D)]


def tiled(shape):
    return shape[-1] % 128 == 0 and shape[-2] % 16 == 0


def run(kernel, name, micros, scalars, arrays, groups, outs, scratch=(), direct=False, cut=None):
    n = tuple(len(group) for group in groups)
    outs, scratch = list(outs), list(scratch)
    windows = [pair[1] if isinstance(pair, tuple) else [None] for pair in arrays]
    arrays = [pair[0] if isinstance(pair, tuple) else pair for pair in arrays]
    ins = [(a.shape, a.dtype) for a in arrays]
    flat = [part for group in groups for part in group]
    moved = [pair for pair in (ins if direct else ins + outs) if tiled(pair[0])]
    rows = D // 8
    shape = (4, 2, 4, rows, D) if name in ("ffn_out", "ffn_back") else (4, 4, 2, rows, D)
    spaces = scratch + [(shape, jnp.bfloat16)] * len(groups)

    def body(scalar_ref, *refs):
        refs = list(refs)
        inputs, pieces = refs[: len(ins)], refs[len(ins) : len(ins) + len(flat)]
        results = refs[len(ins) + len(flat) :][: len(outs)]
        rest = refs[len(ins) + len(flat) + len(outs) :]
        copies, rest = rest[: len(moved)], rest[len(moved) :]
        if moved:
            sems, rest = rest[0], rest[1:]
        used, first = 0, 0
        for side, pairs in ((inputs, ins), (results, [] if direct else outs)):
            for i, (shape, _) in enumerate(pairs):
                if tiled(shape):
                    parts = windows[i] if side is inputs else (cut or {}).get(i, [None])
                    side[i] = Moved(side[i], copies[used], sems, first, parts, side is inputs)
                    used, first = used + 1, first + len(parts)
        kernel(n, scalar_ref, *inputs, *pieces, *results, *rest)
        for array in inputs + results:
            if isinstance(array, Moved):
                array.finish()

    def spec(shape):
        return pl.BlockSpec(memory_space=pltpu.HBM if tiled(shape) else pltpu.VMEM)

    return pl.pallas_call(
        body,
        out_shape=[jax.ShapeDtypeStruct(shape, kind) for shape, kind in outs],
        in_specs=[pl.BlockSpec(memory_space=pltpu.SMEM)]
        + [spec(shape) for shape, _ in ins]
        + [pl.BlockSpec(memory_space=pltpu.HBM)] * len(flat),
        out_specs=[spec(shape) for shape, _ in outs],
        scratch_shapes=[pltpu.VMEM(shape, kind) for shape, kind in moved]
        + ([pltpu.SemaphoreType.DMA((len(outs) * 4 + sum(map(len, windows)),))] if moved else [])
        + [pltpu.VMEM(shape, kind) for shape, kind in spaces]
        + [pltpu.SemaphoreType.DMA((32,)) for _ in (groups or [None])],
        compiler_params=pltpu.CompilerParams(vmem_limit_bytes=63 << 20),
        cost_estimate=pl.CostEstimate(
            flops=int(micros * 2e8), bytes_accessed=int(micros * 2e5), transcendentals=0
        ),
        name=name,
    )(scalars, *arrays, *flat)


def moves(step):
    pairs = []
    for y in range(2):
        for x in range(2):
            for z in range(4):
                for c in range(2):
                    ty, tx, tz, tc = step(y, x, z, c)
                    pairs.append((((y * 2 + x) * 4 + z) * 2 + c, ((ty * 2 + tx) * 4 + tz) * 2 + tc))
    return pairs


def swap_x(values):
    return lax.ppermute(values, BOTH, moves(lambda y, x, z, c: (y, 1 - x, z, c)))


def swap_y(values):
    return lax.ppermute(values, BOTH, moves(lambda y, x, z, c: (1 - y, x, z, c)))


def swap_core(values):
    return lax.ppermute(values, BOTH, moves(lambda y, x, z, c: (y, x, z, 1 - c)))


def turn_z(values, by):
    return lax.ppermute(values, BOTH, moves(lambda y, x, z, c: (y, x, (z + by) % 4, c)))


def after(value, *marks):
    return lax.optimization_barrier((value,) + marks)[0]


def first_swap(values):
    return lax.ppermute(
        values, BOTH, moves(lambda y, x, z, c: (y, 1 - x, z, c) if c == 0 else (1 - y, x, z, c))
    )


def second_swap(values):
    return lax.ppermute(
        values, BOTH, moves(lambda y, x, z, c: (1 - y, x, z, c) if c == 0 else (y, 1 - x, z, c))
    )


LINES = [[z * 2 + c for z in range(4)] for c in range(2)]


def spread_z(values):
    return lax.all_to_all(
        values, "fsdp", split_axis=0, concat_axis=0, tiled=True, axis_index_groups=LINES
    )


class Layer:
    def __init__(self, scalars, tokens, memory, cotangent, staged):
        self.scalars, self.tokens, self.memory, self.cotangent = scalars, tokens, memory, cotangent
        self.staged = staged
        self.t, self.m = tokens.shape[0], memory.shape[0]

    def hold(self, *marks):
        self.scalars = after(self.scalars, *marks)

    def adapters(self, generated):
        block, start = D * ADAPT, 3 * D
        self.gains = 1.0 + 0.25 * generated[:start].astype(jnp.float32).reshape(3, D)
        self.down_1 = generated[start : start + block].reshape(D, ADAPT)
        self.up_1 = generated[start + block : start + 2 * block].reshape(ADAPT, D)
        self.down_2 = generated[start + 2 * block : start + 3 * block].reshape(D, ADAPT)
        self.up_2 = generated[start + 3 * block : start + 4 * block].reshape(ADAPT, D)

    def rows(self, width=D, kind=jnp.bfloat16):
        return ((self.t, width), kind)

    def wide(self, width=D):
        return self.rows(width, jnp.float32)

    def halves(self, count):
        return [((count * (D // 2), self.t), jnp.bfloat16)] * 2

    def self_forward(self, w1):
        local = [self.rows(), self.rows()]
        outs = run(
            self_forward_kernel,
            "self_forward",
            11,
            self.scalars,
            [self.tokens, self.gains, self.down_1, self.up_1],
            [w1],
            [
                self.rows(3 * D),
                ((HEADS, self.t, self.t), jnp.bfloat16),
                self.rows(),
                self.wide(ADAPT),
                self.wide(),
                self.rows(),
            ]
            + (self.halves(2) if self.staged else local),
            scratch=(local if self.staged else []) + attend_spaces(self.t, self.t),
        )
        self.qkv, self.probs_1, self.branch_1, self.inner_1, self.first, self.normed_2 = outs[:6]
        self.saved_1 = outs[6:]

    def cross_forward(self, w2):
        local = [self.rows()]
        outs = run(
            cross_forward_kernel,
            "cross_forward",
            15,
            self.scalars,
            [self.normed_2, self.first, self.memory, self.gains],
            [w2],
            [
                self.rows(),
                ((self.m, 2 * D), jnp.bfloat16),
                ((HEADS, self.m, self.t), jnp.bfloat16),
                self.wide(),
                self.rows(),
            ]
            + (self.halves(4) if self.staged else local),
            scratch=(local if self.staged else []) + attend_spaces(self.m, self.t),
        )
        self.queries, self.memory_kv, self.probs_2, self.second, self.normed_3 = outs[:5]
        self.saved_2 = outs[5:]

    def ffn_in(self, w3):
        outs = run(
            ffn_in_kernel,
            "ffn_in",
            6,
            self.scalars,
            [self.normed_3],
            [w3],
            [self.rows(4 * D), self.rows(4 * D)] + (self.halves(5) if self.staged else []),
            cut={i: column_blocks((self.t, 4 * D)) for i in range(2)},
        )
        self.slope, self.hidden = outs[:2]
        self.saved_3 = outs[2:]

    def adapter_outs(self):
        return [((D, ADAPT), jnp.float32), ((ADAPT, D), jnp.float32)]

    def ffn_out(self, w4):
        self.mixed_out, self.grad_branch, self.grad_down_2, self.grad_up_2 = run(
            ffn_out_kernel,
            "ffn_out",
            8,
            self.scalars,
            [self.hidden, self.second, self.cotangent, self.down_2, self.up_2],
            [w4],
            [self.rows(), self.rows()] + self.adapter_outs(),
        )

    def ffn_back(self, w4):
        (self.grad_pre,) = run(
            ffn_back_kernel,
            "ffn_back",
            8,
            self.scalars,
            [self.grad_branch, self.slope],
            [w4],
            [self.rows(4 * D)],
        )

    def cross_back(self, w3, w2):
        self.grad_second, self.grad_gain_3, self.cross_pack = run(
            cross_back_kernel,
            "cross_back",
            15,
            self.scalars,
            [
                self.grad_pre,
                self.cotangent,
                self.second,
                self.gains,
                self.queries,
                self.memory_kv,
                self.probs_2,
            ],
            [w3, w2],
            [self.wide(), ((1, D), jnp.float32), ((self.m, 3 * D), jnp.bfloat16)],
            scratch=[self.rows()] + attend_spaces(self.m, self.t),
        )

    def self_back(self, w1, w2):
        self.grad_first, self.grad_gain_2, self.grad_down_1, self.grad_up_1, self.self_pack = run(
            self_back_kernel,
            "self_back",
            0.5,
            self.scalars,
            [
                (self.cross_pack, [(self.t, self.t, 2 * D, D)]),
                self.grad_second,
                self.first,
                self.gains,
                self.branch_1,
                self.inner_1,
                self.down_1,
                self.up_1,
                self.qkv,
                self.probs_1,
            ],
            [w1, w2],
            [self.wide(), ((1, D), jnp.float32)] + self.adapter_outs() + [self.rows(4 * D)],
            scratch=[self.rows()] + attend_spaces(self.t, self.t),
        )

    def token_back(self, w1):
        self.token_grad, self.grad_gain_1 = run(
            token_back_kernel,
            "token_back",
            5,
            self.scalars,
            [(self.self_pack, [(0, self.t, 0, 3 * D)]), self.tokens, self.grad_first, self.gains],
            [w1],
            [self.wide(), ((1, D), jnp.float32)],
        )

    def memory_back(self, w2):
        (self.memory_grad,) = run(
            memory_back_kernel,
            "memory_back",
            0.3,
            self.scalars,
            [(self.cross_pack, [(0, self.m, 0, 2 * D)])],
            [w2],
            [((self.m, D), jnp.float32)],
        )

    def block_grads(self, kernel, name, kept, got, grad, other, windows=None, rows=None):
        stage = ((4, 4, D // 8, D), jnp.bfloat16)
        part = ((2, 4, D // 8, D), jnp.bfloat16)
        if rows:
            kept, got = (kept, [rows + (0, self.t)]), (got, [rows + (0, self.t)])
        if windows:
            grad, other = (grad, windows), (other, windows)
        return run(
            kernel, name, 5, self.scalars, [kept, got, grad, other], [], [part, part], [stage], direct=True
        )

    def plain_grads(self, left, right):
        (out,) = run(
            plain_grads_kernel,
            "plain_grads",
            5,
            self.scalars,
            [left, right],
            [],
            [((left.shape[1], right.shape[1]), jnp.bfloat16)],
        )
        return out

    def grad_generated(self):
        return low(
            jnp.concatenate(
                [
                    0.25 * self.grad_gain_1,
                    0.25 * self.grad_gain_2,
                    0.25 * self.grad_gain_3,
                    self.grad_down_1.reshape(ADAPT, D),
                    self.grad_up_1,
                    self.grad_down_2.reshape(ADAPT, D),
                    self.grad_up_2,
                ]
            )
        ).reshape(-1)


def staged_layer(layer, where, task_ids, hidden_all, hyper_gen, shards):
    q, z, c = where[0], where[1], where[2]

    own_1, own_2, own_3, own_4 = pick(where, shards, [(1, 1), (2, 1), (3, 2), (4, 2)])
    column_1 = spread_z(own_1)
    ids = jnp.stack([task_ids, swap_core(task_ids)])
    ids_ahead = [ids] + [turn_z(ids, 4 - k) for k in (1, 2, 3)]
    gen_shard = low(matmul(hidden_all, hyper_gen))
    column_1 = after(column_1, *ids_ahead)
    near_x_1, near_y_1 = swap_x(column_1), swap_y(column_1)

    column_2 = spread_z(after(own_2, column_1))

    def pick_near(near_x, near_y, *marks):
        return jnp.where(c == 0, after(near_x, *marks), after(near_y, *marks))

    leaving_1 = pick_near(near_x_1, near_y_1)
    far_1 = second_swap(leaving_1)

    def rows_of(tasks):
        select = low(tasks[:, 0:1] == jnp.arange(TASKS, dtype=jnp.int32)[None, :])
        return after(low(matmul(select, gen_shard)), near_x_1, near_y_1, leaving_1, column_2)

    asked = [rows_of(tasks) for tasks in ids_ahead]
    turned = [turn_z(asked[k], k) for k in (1, 2, 3)]
    got = jnp.stack([asked[0]] + turned, axis=1)
    pieces = jnp.concatenate([got[0], swap_core(got[1])])
    slots = jnp.arange(8, dtype=jnp.int32)
    source = ((slots % 2) ^ c) * 4 + (z - slots // 2 + 4) % 4
    unturn = low(source[:, None] == slots[None, :])
    layer.adapters(low(matmul(unturn, pieces)).reshape(-1))

    w1 = [column_1, near_x_1, near_y_1, far_1]
    w1 += [swap_core(after(part, near_x_1)) for part in w1]

    def split(pair, *marks):
        return after(pair, *marks)[:, 0], pair[:, 1]

    def with_other(parts, *marks):
        return parts + [swap_core(after(part, *marks)) for part in parts]

    near_2 = [swap_x(column_2), swap_y(column_2)]
    pair_3 = spread_z(after(own_3, *turned))
    layer.hold(column_2)
    layer.self_forward(w1)
    leaving_2 = pick_near(*near_2, layer.normed_2)
    far_2 = second_swap(leaving_2)
    got_1 = swap_core(after(layer.saved_1[1], leaving_2))
    column_3, far_3 = split(pair_3, leaving_2)
    w2 = [column_2] + near_2 + [far_2]
    w2 += [swap_core(after(part, leaving_2)) for part in w2[:3]] + [swap_core(after(far_2, column_3))]
    near_3 = [swap_x(column_3), swap_y(column_3)]
    pair_4 = spread_z(after(own_4, column_3))
    layer.hold(got_1, column_3)
    layer.cross_forward(w2)
    layer.hold(layer.normed_3)
    w3 = with_other([column_3] + near_3 + [far_3], layer.normed_3, *near_3)
    got_2 = swap_core(after(layer.saved_2[1], *near_3))
    column_4, far_4 = split(pair_4, *near_3)
    layer.hold(got_2, column_4)
    layer.ffn_in(w3)
    near_4 = [swap_x(column_4), swap_y(column_4)]
    got_3 = swap_core(layer.saved_3[1])
    near = [swap_core(after(part, layer.hidden)) for part in near_4]
    w4 = [column_4] + near_4 + [far_4, swap_core(column_4)] + near + [swap_core(far_4)]
    layer.hold(got_3)
    layer.ffn_out(w4)

    def first_way(sums, *marks):
        home, away = sums
        return home, first_swap(after(away, *marks))

    def leaving(*sums):
        return combine("leaving", layer.scalars, [[(home, 1), (got, 1)] for home, got in sums])

    def staying(*sums):
        return combine("staying", layer.scalars, [[(home, 0), (got, 0), part] for home, got, part in sums])

    def grads(kernel, name, kept, got, grad, other):
        windows = column_blocks(grad.shape) if grad.shape[1] > D else None
        if kernel is cross_grads_kernel:
            windows = [windows[2]] + windows[:2]
        half = D // 2
        rows = {ffn_in_grad_kernel: (0, half), ffn_out_grad_kernel: (half, 4 * half)}.get(kernel)
        return layer.block_grads(kernel, name, kept, got, grad, other, windows, rows)

    other = swap_core(layer.grad_branch)
    layer.hold(other)
    layer.ffn_back(w4)
    other_pre = swap_core(layer.grad_pre)
    layer.hold(layer.grad_pre)
    g4 = grads(
        ffn_out_grad_kernel, "ffn_out_grad", layer.saved_3[0], got_3, layer.grad_branch, other
    )
    layer.hold(g4[0])
    g3 = grads(
        ffn_in_grad_kernel, "ffn_in_grad", layer.saved_3[0], got_3, layer.grad_pre, other_pre
    )
    s4, s3 = first_way(g4, g3[0]), first_way(g3)
    layer.hold(g3[0])
    layer.cross_back(w3, w2)
    layer.hold(layer.cross_pack)
    layer.self_back(w1, w2)
    other = swap_core(after(layer.cross_pack, layer.self_pack))
    layer.hold(layer.self_pack)
    t43 = leaving(s4, s3)
    q43 = second_swap(t43)
    other_self = swap_core(after(layer.self_pack, t43))
    layer.hold(t43)
    g2 = grads(
        cross_grads_kernel, "cross_grads", layer.saved_2[0], got_2, layer.cross_pack, other
    )
    s2 = first_way(g2)
    layer.hold(g2[0])
    g1 = grads(
        self_grads_kernel, "self_grads", layer.saved_1[0], got_1, layer.self_pack, other_self
    )
    s1 = first_way(g1)
    layer.hold(g1[0])
    layer.token_back(w1)
    layer.hold(layer.token_grad)
    u43 = staying(s4 + ((q43, (slice(None), 0)),), s3 + ((q43, (slice(None), 1)),))
    sent_43 = spread_z(u43)
    layer.hold(u43)
    t2 = leaving(s2)
    q2 = second_swap(t2)
    layer.hold(t2)
    layer.memory_back(w2)
    layer.hold(layer.memory_grad)
    t1 = leaving(s1)
    q1 = second_swap(t1)
    layer.hold(t1)
    u21 = staying(s2 + (q2,), s1 + (q1,))
    sent_21 = spread_z(after(u21, sent_43))
    own_4, own_3 = jnp.sum(after(sent_43, u21).astype(jnp.float32), axis=0)

    pieces = after(layer.grad_generated().reshape(4, 2, -1), u21, sent_43)
    mine = lax.dynamic_index_in_dim(pieces, c, 1, keepdims=False)
    theirs = lax.dynamic_index_in_dim(pieces, 1 - c, 1, keepdims=False)
    both = jnp.stack([mine, swap_core(theirs)], axis=1)
    both = lax.dynamic_slice_in_dim(jnp.concatenate([both, both]), z, 4, 0)
    terms = jnp.concatenate([both[0]] + [turn_z(both[k], k) for k in (1, 2, 3)])
    ids = jnp.concatenate([ids_ahead[(4 - k) % 4] for k in range(4)])[:, 0]
    select = low(jnp.arange(TASKS, dtype=jnp.int32)[:, None] == ids[None, :])
    task_grad = low(matmul(select, terms))
    task_grad = add_low(task_grad, swap_x(task_grad))
    task_grad = task_grad.astype(jnp.float32) + swap_y(task_grad).astype(jnp.float32)

    def sum_owners(part):
        part = part + swap_core(part)
        got = [part] + [turn_z(part, k) for k in (1, 2, 3)]
        return (got[0] + got[2]) + (got[1] + got[3])

    def share(owns):
        own = low(jnp.stack(owns))
        pair = jnp.stack([own, first_swap(own)])
        quad = jnp.concatenate([pair, second_swap(pair)])
        slots = [jnp.where(c == 0, q ^ b, ((q ^ b) % 2) * 2 + (q ^ b) // 2) for b in range(4)]
        return [
            [lax.dynamic_index_in_dim(quad, at, 0, keepdims=False)[i].astype(jnp.float32) for at in slots]
            for i in range(len(owns))
        ]

    own_2, own_1 = jnp.sum(sent_21.astype(jnp.float32), axis=0)
    g3, g4 = share([own_3, own_4])
    g2, g1 = share([own_2, own_1])
    summed = (
        jnp.concatenate(g1[:3], axis=1),
        g1[3],
        g2[0],
        jnp.concatenate(g2[2:], axis=1),
        g2[1],
        jnp.concatenate(g3, axis=1),
        jnp.concatenate(g4, axis=0),
    )
    return summed, task_grad, sum_owners


def plain_layer(layer, task_ids, hidden_all, hyper_gen, groups):
    owners = lax.axis_size("fsdp")

    def whole(shard):
        return lax.all_gather(shard, "fsdp", axis=0, tiled=True)

    w1, w2, w3 = (
        [jnp.concatenate([whole(block) for block in blocks]).reshape(4, 4, 2, D // 8, D)] for blocks in groups[:3]
    )
    w4 = [whole(jnp.concatenate(groups[3])).reshape(4, 2, 4, D // 8, D)]
    select = low(task_ids[:, None] == jnp.arange(TASKS, dtype=jnp.int32)[None, :])
    gen_shard = low(matmul(hidden_all, hyper_gen))
    gen_tasks = lax.all_gather(gen_shard, "fsdp", axis=1, tiled=True)
    layer.adapters(low(matmul(select, gen_tasks)[0]))
    layer.self_forward(w1)
    layer.cross_forward(w2)
    layer.ffn_in(w3)
    layer.ffn_out(w4)
    layer.ffn_back(w4)
    layer.cross_back(w3, w2)
    layer.self_back(w1, w2)
    layer.token_back(w1)
    layer.memory_back(w2)

    def owned(left, right):
        part = low(lax.psum_scatter(layer.plain_grads(left, right), "fsdp", scatter_dimension=0, tiled=True))
        return lax.psum(part, "dp").astype(jnp.float32)

    t = layer.t
    pack = layer.cross_pack
    summed = (
        owned(layer.saved_1[0], layer.self_pack[:, : 3 * D]),
        owned(layer.saved_1[1], layer.self_pack[:, 3 * D :]),
        owned(layer.normed_2, pack[t : 2 * t, 2 * D :]),
        owned(layer.memory, pack[:, : 2 * D]),
        owned(layer.saved_2[0], pack[:t, 2 * D :]),
        owned(layer.normed_3, layer.grad_pre),
        owned(layer.hidden, layer.grad_branch),
    )
    pieces = layer.grad_generated().reshape(owners, 1, -1)
    select = low(jnp.arange(TASKS, dtype=jnp.int32)[:, None] == task_ids[None, :])
    terms = low(select[None].astype(jnp.float32) * pieces.astype(jnp.float32))
    terms = lax.all_to_all(terms, "fsdp", split_axis=0, concat_axis=0, tiled=True)
    task_grad = low(jnp.sum(terms.astype(jnp.float32), axis=0))
    task_grad = lax.psum(task_grad, "dp").astype(jnp.float32)
    return summed, task_grad, lambda part: lax.psum(part, "fsdp")


def hyper_tail(task_grad, pre_all, hidden_all, task_table, hyper_in, hyper_gen, sum_owners):
    grad_hyper_gen = jnp.dot(
        hidden_all.astype(jnp.float32).T, task_grad, precision=lax.Precision.HIGHEST
    )
    grad_hidden = jnp.dot(
        task_grad, hyper_gen.astype(jnp.float32).T, precision=lax.Precision.HIGHEST
    )
    grad_pre_all = gelu_slope(pre_all) * sum_owners(grad_hidden)
    grad_table = jnp.dot(grad_pre_all, hyper_in.T, precision=lax.Precision.HIGHEST)
    grad_first = jnp.dot(task_table.T, grad_pre_all, precision=lax.Precision.HIGHEST)
    return grad_table, grad_first, grad_hyper_gen


def shards(
    tokens,
    memory,
    target_lengths,
    memory_lengths,
    task_ids,
    cotangent,
    self_qkv,
    self_out,
    cross_q,
    cross_kv,
    cross_out,
    ffn_in,
    ffn_out,
    task_table,
    hyper_in,
    hyper_gen,
):
    staged = lax.axis_size("fsdp") == 8 and lax.axis_size("dp") == 4
    pre_all = jnp.dot(task_table, hyper_in, precision=lax.Precision.HIGHEST)
    hidden_all = low(jax.nn.gelu(pre_all))

    def columns(shard):
        return [shard[:, b * D : (b + 1) * D] for b in range(shard.shape[1] // D)]

    q = lax.axis_index("dp").astype(jnp.int32)
    f = lax.axis_index("fsdp").astype(jnp.int32)
    where = jnp.stack([q, f // 2, f % 2])
    scalars = jnp.concatenate([where, target_lengths, memory_lengths])
    layer = Layer(scalars, tokens, memory, cotangent, staged)
    if staged:
        summed, task_grad, sum_owners = staged_layer(
            layer,
            where,
            task_ids,
            hidden_all,
            hyper_gen,
            (self_qkv, self_out, cross_q, cross_kv, cross_out, ffn_in, ffn_out),
        )
    else:
        rows = self_qkv.shape[0]
        groups = (
            columns(self_qkv) + [self_out],
            [cross_q, cross_out] + columns(cross_kv),
            columns(ffn_in),
            [ffn_out[b * rows : (b + 1) * rows] for b in range(4)],
        )
        summed, task_grad, sum_owners = plain_layer(layer, task_ids, hidden_all, hyper_gen, groups)
    grad_table, grad_first, grad_hyper_gen = hyper_tail(
        task_grad, pre_all, hidden_all, task_table, hyper_in, hyper_gen, sum_owners
    )
    return (
        (layer.mixed_out, layer.token_grad, layer.memory_grad)
        + summed
        + (grad_table, grad_first, grad_hyper_gen)
    )


def solution(mesh):
    by_both = P(("dp", "fsdp"), None)
    by_rows = P("fsdp", None)
    return jax.shard_map(
        shards,
        mesh=mesh,
        in_specs=(by_both, by_both)
        + (P(("dp", "fsdp")),) * 3
        + (by_both,)
        + (by_rows,) * 7
        + (P(), P(), P(None, "fsdp")),
        out_specs=(by_both,) * 3 + (by_rows,) * 7 + (P(), P(), P(None, "fsdp")),
        check_vma=False,
    )
```

```python
import functools

import jax
import jax.numpy as jnp
from jax import lax
from jax.experimental import pallas as pl
from jax.experimental.pallas import tpu as pltpu
from jax.sharding import PartitionSpec as P

D = 768
HEADS = 12
HEAD = 64
ADAPT = 24
TASKS = 8
BOTH = ("dp", "fsdp")


def matmul(left, right):
    return jnp.dot(left, right, preferred_element_type=jnp.float32)


def matmul_left_t(left, right):
    return lax.dot_general(
        left, right, (((0,), (0,)), ((), ())), preferred_element_type=jnp.float32
    )


def matmul_right_t(left, right):
    return lax.dot_general(
        left, right, (((1,), (1,)), ((), ())), preferred_element_type=jnp.float32
    )


def low(values):
    return values.astype(jnp.bfloat16)


def add_low(left, right):
    return low(left.astype(jnp.float32) + right.astype(jnp.float32))


def rms_factor(values):
    return lax.rsqrt(jnp.mean(values * values, axis=-1, keepdims=True) + 1e-06)


def norm_grad(values, gains, upstream):
    factor = rms_factor(values)
    scaled = upstream * gains
    mean = jnp.mean(values * scaled, axis=-1, keepdims=True)
    part = factor * scaled - values * (factor * factor * factor * mean)
    return part, jnp.sum(upstream * values * factor, axis=0, keepdims=True)


GELU_A = 0.7978845608
GELU_B = 0.044715


def gelu(values):
    inside = GELU_A * (values + GELU_B * values * values * values)
    return 0.5 * values * (1.0 + jnp.tanh(inside))


def gelu_both(values):
    square = values * values
    curve = jnp.tanh(GELU_A * (values + GELU_B * square * values))
    inner = GELU_A * (1.0 + 3.0 * GELU_B * square)
    half = 0.5 * (1.0 + curve)
    return values * half, half + 0.5 * values * (1.0 - curve * curve) * inner


def gelu_slope(values):
    square = values * values
    curve = jnp.tanh(GELU_A * (values + GELU_B * square * values))
    inner = GELU_A * (1.0 + 3.0 * GELU_B * square)
    return 0.5 * (1.0 + curve) + 0.5 * values * (1.0 - curve * curve) * inner


class Group:
    def __init__(self, scalars, refs, scratch, sems, by_block, blocks=(0, 1, 2, 3)):
        self.scalars, self.refs, self.scratch, self.sems = scalars, refs, scratch, sems
        self.by_block, self.blocks = by_block, blocks
        self.staged = len(refs) > 1
        self.waited = False

    def _each(self, act, part=None):
        if not self.staged:
            act(pltpu.make_async_copy(self.refs[0], self.scratch, self.sems.at[0]))
            return
        c = self.scalars[2]
        for place in range(4):
            block = self.which(place)

            def parts(place=place, block=block):
                for side in range(2):
                    source = self.refs[side * 4 + place]
                    if self.by_block and part in (None, place):
                        target = self.scratch.at[place, :, c ^ side]
                        act(pltpu.make_async_copy(source, target, self.sems.at[place * 2 + side]))
                    if not self.by_block:
                        for half in range(2):
                            if part in (None, half):
                                at = pl.ds(half * 2, 2)
                                act(
                                    pltpu.make_async_copy(
                                        source.at[at],
                                        self.scratch.at[at, c ^ side, block],
                                        self.sems.at[(place * 2 + side) * 2 + half],
                                    )
                                )

            if len(self.blocks) == 4:
                parts()
            else:
                wanted = block == self.blocks[0]
                for other in self.blocks[1:]:
                    wanted = wanted | (block == other)
                pl.when(wanted)(parts)

    def start(self):
        self._each(lambda copy: copy.start())

    def wait(self, part=None):
        if self.staged:
            self._each(lambda copy: copy.wait(), part)
        elif not self.waited:
            self._each(lambda copy: copy.wait())
            self.waited = True

    def wait_block(self, index):
        if not self.staged:
            self.wait()
            return
        place, c = self.which(index), self.scalars[2]
        for side in range(2):
            target = self.scratch.at[place, :, c ^ side]
            pltpu.make_async_copy(self.refs[0], target, self.sems.at[place * 2 + side]).wait()

    def place(self, place):
        return self.scratch[place].reshape(D, D)

    def which(self, place):
        return self.scalars[0] ^ place if self.staged else place

    def block(self, index):
        return self.scratch[self.which(index)].reshape(D, D)

    def quarter(self, z):
        return self.scratch[z].reshape(D, D)


def columns_at(block):
    return pl.ds(pl.multiple_of(block * D, D), D)


def part_rows(scalars, value, keep, send, at):
    flat = value.T
    rows = flat.shape[0] // 8
    for parity in range(2):
        here = scalars[2] == parity

        @pl.when(here)
        def _():
            for z in range(4):
                piece = flat[(z * 2 + parity) * rows : (z * 2 + parity + 1) * rows]
                keep[at + z * rows : at + (z + 1) * rows, :] = piece

        @pl.when(jnp.logical_not(here))
        def _():
            for z in range(4):
                piece = flat[(z * 2 + parity) * rows : (z * 2 + parity + 1) * rows]
                send[at + z * rows : at + (z + 1) * rows, :] = piece


class Blocks:
    def __init__(self, scalars, outs, stage, sems):
        self.scalars, self.outs, self.stage, self.sems = scalars, outs, stage, sems
        self.sent = []

    def put(self, block, value):
        rows = value.shape[0] // 4
        value = low(value)
        for z in range(4):
            self.stage[block, z] = value[z * rows : (z + 1) * rows]
        r, c = self.scalars[0] ^ block, self.scalars[2]
        first = jnp.where(c == 0, r % 2, r // 2)
        second = jnp.where(c == 0, r // 2, r % 2)
        for way, out in enumerate(self.outs):
            copy = pltpu.make_async_copy(self.stage.at[block], out.at[second], self.sems.at[block * 2 + way])
            pl.when(first == way)(copy.start)
            self.sent.append((first == way, copy))

    def finish(self):
        for here, copy in self.sent:
            pl.when(here)(copy.wait)


def head_lanes(rows, head):
    lane = lax.broadcasted_iota(jnp.int32, (rows, 128), 1)
    return lane < HEAD if head == 0 else lane >= HEAD


def pick_head(values, head):
    return jnp.where(head_lanes(values.shape[0], head), values, jnp.zeros_like(values))


def pair_at(pair, base=0):
    if isinstance(pair, int):
        return slice(base + pair * 128, base + pair * 128 + 128)
    return pl.ds(pl.multiple_of(base + pair * 128, 128), 128)


def work_on_pairs(first, middle, last, spaces):
    wide, low_spaces = spaces[:2], spaces[2:]
    pairs = HEADS // 2
    first(0, wide[0])
    if wide[0].shape[1] > 256:
        for pair in range(pairs):
            i = pair % 2
            if pair + 1 < pairs:
                first(pair + 1, wide[1 - i])
            middle(pair, wide[i], low_spaces[i])
            if pair:
                last(pair - 1, low_spaces[1 - i])
    else:

        @pl.loop(0, pairs // 2)
        def _(turn):
            for i in range(2):
                pair = turn * 2 + i
                first(jnp.minimum(pair + 1, pairs - 1), wide[1 - i])
                middle(pair, wide[i], low_spaces[i])
                last(jnp.maximum(pair - 1, 0), low_spaces[1 - i])

    last(pairs - 1, low_spaces[1])


def attend_spaces(keys, queries):
    shape = (2, keys, queries)
    return [(shape, jnp.float32)] * 2 + [(shape, jnp.bfloat16)] * 2


def attend_pairs(q_ref, k_ref, k_at, v_ref, v_at, bias, probs, mixed, spaces):
    ready(q_ref, k_ref, v_ref)
    q_ref, k_ref, v_ref, probs = (inner_of(ref) for ref in (q_ref, k_ref, v_ref, probs))

    def scores_of(pair, wide):
        keys = k_ref[:, pair_at(pair, k_at)]
        for head in range(2):
            wide[head] = matmul_right_t(pick_head(keys, head), q_ref[:, pair_at(pair)])

    def weights_of(pair, wide, space):
        for head in range(2):
            scores = wide[head] + bias
            weights = jnp.exp(scores - jnp.max(scores, axis=0, keepdims=True))
            weights = low(weights * (1.0 / jnp.sum(weights, axis=0, keepdims=True)))
            space[head] = weights
            probs[pair * 2 + head] = weights

    def mix(pair, space):
        values = v_ref[:, pair_at(pair, v_at)].T
        halves = [matmul(values[head * HEAD : (head + 1) * HEAD], space[head]) for head in range(2)]
        mixed[:, pair_at(pair)] = low(jnp.concatenate(halves, axis=0).T)

    work_on_pairs(scores_of, weights_of, mix, spaces)


def attend_pairs_back(
    q_ref, k_ref, k_at, v_ref, v_at, probs, grad_mixed, grad_q, grad_k, gk_at, grad_v, gv_at, spaces
):
    ready(q_ref, k_ref, v_ref, probs)
    q_ref, k_ref, v_ref, probs = (inner_of(ref) for ref in (q_ref, k_ref, v_ref, probs))
    grad_q, grad_k, grad_v = (inner_of(ref) for ref in (grad_q, grad_k, grad_v))

    def grad_weights(pair, wide):
        values = v_ref[:, pair_at(pair, v_at)]
        for head in range(2):
            wide[head] = matmul_right_t(pick_head(values, head), grad_mixed[:, pair_at(pair)])

    def grad_scores(pair, wide, space):
        for head in range(2):
            weights = probs[pair * 2 + head].astype(jnp.float32)
            grads = wide[head]
            total = jnp.sum(grads * weights, axis=0, keepdims=True)
            space[head] = low(weights * (grads - total))

    def products(pair, space):
        queries = q_ref[:, pair_at(pair)]
        keys = k_ref[:, pair_at(pair, k_at)]
        grads = grad_mixed[:, pair_at(pair)]
        keys_t = keys.T
        part_v = [matmul(probs[pair * 2 + head], grads) for head in range(2)]
        part_k = [matmul(space[head], queries) for head in range(2)]
        halves = [matmul(keys_t[head * HEAD : (head + 1) * HEAD], space[head]) for head in range(2)]
        first = head_lanes(keys.shape[0], 0)
        grad_q[:, pair_at(pair)] = low(jnp.concatenate(halves, axis=0).T * HEAD ** (-0.5))
        grad_k[:, pair_at(pair, gk_at)] = low(jnp.where(first, part_k[0], part_k[1]))
        grad_v[:, pair_at(pair, gv_at)] = low(jnp.where(first, part_v[0], part_v[1]))

    work_on_pairs(grad_weights, grad_scores, products, spaces)


def adapter_forward(branch, down, upward):
    inner = matmul(branch, down) * D ** (-0.5)
    active = low(gelu(inner))
    return branch.astype(jnp.float32) + matmul(active, upward) * ADAPT ** (-0.5), inner, active


def adapter_backward(branch, down, upward, inner, active, grad_out):
    grad_low = low(grad_out)
    grad_up = matmul_left_t(active, grad_low) * ADAPT ** (-0.5)
    grad_active = matmul_right_t(grad_low, upward) * ADAPT ** (-0.5)
    grad_inner = low(gelu_slope(inner) * grad_active)
    grad_down = matmul_left_t(branch, grad_inner) * D ** (-0.5)
    grad_branch = low(grad_out + matmul_right_t(grad_inner, down) * D ** (-0.5))
    return grad_branch, grad_down, grad_up


def self_forward_kernel(n, scalars, tokens, gains, down, up, *rest):
    refs, (qkv, probs, branch, inner_out, first_out, normed_cross, *saved, scratch, sems) = rest[: n[0]], rest[n[0] :]
    *halves, normed, mixed = saved[:-4]
    group = Group(scalars, refs, scratch, sems, True)
    fetch(tokens, group)
    inputs = tokens[...].astype(jnp.float32)
    normed[...] = low(inputs * rms_factor(inputs) * gains[0:1])
    rows = inputs.shape[0]
    key = lax.broadcasted_iota(jnp.int32, (rows, rows), 0)
    query = lax.broadcasted_iota(jnp.int32, (rows, rows), 1)
    bias = jnp.where((key <= query) & (key < scalars[3]), 0.0, -1e30)
    if halves:
        part_rows(scalars, normed[...], *halves, 0)
    for b in range(3):
        group.wait_block(b)
        product = matmul(normed[...], group.block(b))
        qkv[:, b * D : (b + 1) * D] = low(product) * (HEAD ** (-0.5) if b == 0 else 1.0)
    send(qkv)
    attend_pairs(qkv, qkv, D, qkv, 2 * D, bias, probs, mixed, saved[-4:])
    send(probs)
    group.wait_block(3)
    branch[...] = low(matmul(mixed[...], group.block(3)))
    adapted, inner, _ = adapter_forward(branch[...], down[...], up[...])
    inner_out[...] = inner
    first = inputs + adapted
    first_out[...] = first
    normed_cross[...] = low(first * rms_factor(first) * gains[1:2])
    send(branch, first_out, normed_cross)
    if halves:
        part_rows(scalars, mixed[...], *halves, D // 2)


def cross_forward_kernel(n, scalars, normed, first, memory, gains, *rest):
    refs, (queries, memory_kv, probs, second_out, normed_ffn, *saved, scratch, sems) = rest[: n[0]], rest[n[0] :]
    *halves, mixed = saved[:-4]
    group = Group(scalars, refs, scratch, sems, True)
    fetch(memory, normed, group, first)
    slot = lax.broadcasted_iota(jnp.int32, (memory.shape[0], 1), 0)
    bias = jnp.where(slot < scalars[4], 0.0, -1e30)
    if halves:
        part_rows(scalars, normed[...], *halves, 0)
        half = memory.shape[0] // 2
        for i in range(2):
            part_rows(scalars, memory[i * half : (i + 1) * half, :], *halves, (2 + i) * (D // 2))
    group.wait()
    queries[...] = low(matmul(normed[...], group.block(0))) * HEAD ** (-0.5)
    for b in range(2):
        memory_kv[:, b * D : (b + 1) * D] = low(matmul(memory[...], group.block(2 + b)))
    send(queries, memory_kv)
    attend_pairs(queries, memory_kv, 0, memory_kv, D, bias, probs, mixed, saved[-4:])
    send(probs)
    second = first[...] + matmul(mixed[...], group.block(1))
    second_out[...] = second
    normed_ffn[...] = low(second * rms_factor(second) * gains[2:3])
    send(second_out, normed_ffn)
    if halves:
        part_rows(scalars, mixed[...], *halves, D // 2)


def ffn_in_kernel(n, scalars, normed, *rest):
    refs, (slope, hidden, *halves, scratch, sems) = rest[: n[0]], rest[n[0] :]
    group = Group(scalars, refs, scratch, sems, True)
    fetch(normed, group)
    if halves:
        part_rows(scalars, normed[...], *halves, 0)
    ahead = None
    for b in range(5):
        product = ahead
        if b < 4:
            group.wait_block(b)
            ahead = matmul(normed[...], group.block(b))
        if b:
            at = slice((b - 1) * D, b * D)
            hidden_b, slope_b = gelu_both(product)
            hidden_b = low(hidden_b)
            slope[:, at] = low(slope_b)
            hidden[:, at] = hidden_b
            send_part(b - 1, slope, hidden)
            if halves:
                flat, half = hidden_b.T, D // 2
                to = slice(b * half, (b + 1) * half)
                even = scalars[2] == 0
                halves[0][to, :] = jnp.where(even, flat[:half], flat[half:])
                halves[1][to, :] = jnp.where(even, flat[half:], flat[:half])


def ffn_out_kernel(n, scalars, hidden, second, cotangent, down, up, *rest):
    refs, (mixed_out, grad_branch, grad_down, grad_up, scratch, sems) = rest[: n[0]], rest[n[0] :]
    group = Group(scalars, refs, scratch, sems, False)
    fetch(hidden, group, second, cotangent)
    rows = hidden.shape[0]
    valid = lax.broadcasted_iota(jnp.int32, (rows, 1), 0) < scalars[3]
    product = None
    for z in range(4):
        if z % 2 == 0:
            group.wait(z // 2)
        term = matmul(hidden[:, z * D : (z + 1) * D], group.quarter(z))
        product = term if product is None else product + term
    branch = low(product)
    adapted, inner, active = adapter_forward(branch, down[...], up[...])
    mixed_out[...] = low(jnp.where(valid, second[...] + adapted, 0.0))
    send(mixed_out)
    grad_result = jnp.where(valid, cotangent[...].astype(jnp.float32), 0.0)
    grad_branch[...], grad_down[...], grad_up[...] = adapter_backward(
        branch, down[...], up[...], inner, active, grad_result
    )


def ffn_back_kernel(n, scalars, grad_branch, slope, *rest):
    refs, (grad_pre, scratch, sems) = rest[: n[0]], rest[n[0] :]
    group = Group(scalars, refs, scratch, sems, False)
    fetch(grad_branch, group, slope)
    for z in range(4):
        if z % 2 == 0:
            group.wait(z // 2)
        at = slice(z * D, (z + 1) * D)
        grad_hidden = matmul_right_t(grad_branch[...], group.quarter(z))
        grad_pre[:, at] = low(slope[:, at].astype(jnp.float32) * grad_hidden)


def cross_views(pack, rows):
    side = pack.at[:, 2 * D :]
    return side.at[:rows], side.at[rows : 2 * rows], pack.at[:, : 2 * D]


def cross_back_kernel(n, scalars, grad_pre, cotangent, second, gains, queries, memory_kv, probs, *rest):
    refs, cross_refs = rest[: n[0]], rest[n[0] : n[0] + n[1]]
    (grad_second_out, grad_gain, pack, grad_mixed, *spaces, scratch, cross_scratch, sems, cross_sems) = rest[n[0] + n[1] :]
    group = Group(scalars, refs, scratch, sems, True)
    cross = Group(scalars, cross_refs, cross_scratch, cross_sems, True, (1,))
    fetch(grad_pre, group)
    rows = second.shape[0]
    valid = lax.broadcasted_iota(jnp.int32, (rows, 1), 0) < scalars[3]
    upstream = None
    for r in range(4):
        group.wait(r)
        if r == 0:
            fetch(second, cotangent, cross)
        if r == 2:
            fetch(queries, memory_kv, probs)
        term = matmul_right_t(grad_pre[:, columns_at(group.which(r))], group.place(r))
        upstream = term if upstream is None else upstream + term
    grad_result = jnp.where(valid, cotangent[...].astype(jnp.float32), 0.0)
    part, grad_gain[...] = norm_grad(second[...], gains[2:3], upstream)
    grad_second = grad_result + part
    grad_second_out[...] = grad_second
    send(grad_second_out)
    grad_cross, grad_q, _ = cross_views(pack, rows)
    grad_cross[...] = low(grad_second)
    cross.wait()
    grad_mixed[...] = low(matmul_right_t(grad_cross[...], cross.block(1)))
    attend_pairs_back(queries, memory_kv, 0, memory_kv, D, probs, grad_mixed, grad_q, pack, 0, pack, D, spaces)


def self_back_kernel(n, scalars, cross_pack, grad_second, first, gains, branch, inner, down, up, qkv, probs, *rest):
    refs, cross_refs = rest[: n[0]], rest[n[0] : n[0] + n[1]]
    (grad_first_out, grad_gain, grad_down, grad_up, pack, grad_mixed, *spaces, scratch, cross_scratch, sems, cross_sems) = rest[n[0] + n[1] :]
    cross = Group(scalars, cross_refs, cross_scratch, cross_sems, True, (0,))
    group = Group(scalars, refs, scratch, sems, True, (3,))
    fetch(cross_pack, cross, first, grad_second, branch, group, qkv, probs)
    _, grad_q, _ = cross_views(cross_pack, first.shape[0])
    cross.wait()
    upstream = matmul_right_t(grad_q[...], cross.block(0))
    part, grad_gain[...] = norm_grad(first[...], gains[1:2], upstream)
    grad_first = grad_second[...] + part
    grad_first_out[...] = grad_first
    send(grad_first_out)
    active = low(gelu(inner[...]))
    grad_branch, grad_down[...], grad_up[...] = adapter_backward(
        branch[...], down[...], up[...], inner[...], active, grad_first
    )
    pack[:, 3 * D :] = grad_branch
    group.wait()
    grad_mixed[...] = low(matmul_right_t(grad_branch, group.block(3)))
    attend_pairs_back(qkv, qkv, D, qkv, 2 * D, probs, grad_mixed, pack, pack, D, pack, 2 * D, spaces)


def rows_product(kept, at, pairs):
    total = None
    for mine, grad in zip(kept, pairs):
        term = matmul(mine[at : at + D // 2, :], grad)
        total = term if total is None else total + term
    return total


def ffn_out_grad_kernel(n, scalars, kept, got, grad, other, *rest):
    *outs, stage, sems = rest
    fetch(kept, grad, got, other)
    blocks = Blocks(scalars, outs, stage, sems)
    rows, half = D // 8, D // 2
    grads = (grad[...], other[...])
    for b in range(4):
        picked = [
            jnp.concatenate([x[(1 + z) * half + b * rows : (1 + z) * half + (b + 1) * rows, :] for z in range(4)])
            for x in (kept, got)
        ]
        blocks.put(b, matmul(picked[0], grads[0]) + matmul(picked[1], grads[1]))
    blocks.finish()


def ffn_in_grad_kernel(n, scalars, kept, got, grad, other, *rest):
    *outs, stage, sems = rest
    fetch(kept, got, grad, other)
    blocks = Blocks(scalars, outs, stage, sems)
    for b in range(4):
        at = slice(b * D, (b + 1) * D)
        grad.ready(b)
        other.ready(b)
        blocks.put(b, rows_product((kept, got), 0, (grad.inner[:, at], other.inner[:, at])))
    blocks.finish()


def cross_grads_kernel(n, scalars, kept, got, pack, other, *rest):
    *outs, stage, sems = rest
    fetch(kept, got, pack, other)
    blocks = Blocks(scalars, outs, stage, sems)
    half = D // 2
    rows = kept.shape[1]
    views = [cross_views(p.inner, rows) for p in (pack, other)]
    ready_part(0, pack, other)
    blocks.put(0, rows_product((kept, got), 0, [v[1][...] for v in views]))
    blocks.put(1, rows_product((kept, got), half, [v[0][...] for v in views]))
    for b in range(2):
        ready_part(1 + b, pack, other)
        at = slice(b * D, (b + 1) * D)
        value = rows_product((kept, got), 2 * half, [v[2][:rows, at] for v in views])
        value += rows_product((kept, got), 3 * half, [v[2][rows:, at] for v in views])
        blocks.put(2 + b, value)
    blocks.finish()


def self_grads_kernel(n, scalars, kept, got, pack, other, *rest):
    *outs, stage, sems = rest
    fetch(kept, got, pack, other)
    blocks = Blocks(scalars, outs, stage, sems)
    for b in range(4):
        at = slice(b * D, (b + 1) * D)
        part = D // 2 if b == 3 else 0
        ready_part(b, pack, other)
        blocks.put(b, rows_product((kept, got), part, (pack.inner[:, at], other.inner[:, at])))
    blocks.finish()


def combine_kernel(slots, scalars, *rest):
    count = sum(len(terms) for terms in slots)
    refs, (out, stage, out_stage, sems, out_sems) = rest[:count], rest[count:]
    copies = []
    for terms in slots:
        for index in terms:
            at = len(copies)
            source = refs[at] if index is None else refs[at].at[index]
            copies.append(pltpu.make_async_copy(source, stage.at[at], sems.at[at]))
    for copy in copies:
        copy.start()
    sent, at = [], 0
    for i, terms in enumerate(slots):
        total = None
        for _ in terms:
            copies[at].wait()
            term = stage[at].astype(jnp.float32)
            total = term if total is None else total + term
            at += 1
        out_stage[i] = low(total)
        target = out if len(slots) == 1 else out.at[:, i]
        sent.append(pltpu.make_async_copy(out_stage.at[i], target, out_sems.at[i]))
        sent[-1].start()
    for copy in sent:
        copy.wait()


def combine(name, scalars, slots):
    slots = [[term if isinstance(term, tuple) else (term, None) for term in terms] for terms in slots]
    flat = [term for terms in slots for term in terms]
    part = flat[0][0].shape[-2:]
    shape = (4,) + ((len(slots),) if len(slots) > 1 else ()) + part
    return pl.pallas_call(
        functools.partial(combine_kernel, [[index for _, index in terms] for terms in slots]),
        out_shape=jax.ShapeDtypeStruct(shape, jnp.bfloat16),
        in_specs=[pl.BlockSpec(memory_space=pltpu.SMEM)]
        + [pl.BlockSpec(memory_space=pltpu.HBM)] * len(flat),
        out_specs=pl.BlockSpec(memory_space=pltpu.HBM),
        scratch_shapes=[
            pltpu.VMEM((len(flat), 4) + part, jnp.bfloat16),
            pltpu.VMEM((len(slots), 4) + part, jnp.bfloat16),
            pltpu.SemaphoreType.DMA((len(flat),)),
            pltpu.SemaphoreType.DMA((len(slots),)),
        ],
        compiler_params=pltpu.CompilerParams(vmem_limit_bytes=63 << 20),
        cost_estimate=pl.CostEstimate(flops=1 << 28, bytes_accessed=1 << 18, transcendentals=0),
        name=name,
    )(scalars, *[array for array, _ in flat])


def plain_grads_kernel(n, scalars, left, right, out, sems):
    fetch(left, right)
    out[...] = low(matmul_left_t(left[...], right[...]))


def pick_kernel(counts, scalars, *rest):
    inputs, outs = rest[:7], rest[7 : 7 + len(counts)]
    stage, sems, out_sems = rest[7 + len(counts) :]
    rows = inputs[0].shape[0]
    qkv, sout, cq, ckv, cout, f_in, f_out = inputs

    def columns(ref):
        return [ref.at[:, pl.ds(b * D, D)] for b in range(ref.shape[1] // D)]

    groups = {
        1: columns(qkv) + [sout],
        2: [cq, cout] + columns(ckv),
        3: columns(f_in),
        4: [f_out.at[pl.ds(b * rows, rows)] for b in range(4)],
    }
    used = 0
    loads = []
    for group, many in counts:
        for i in range(many):
            for b in range(4):
                copy = pltpu.make_async_copy(groups[group][b], stage.at[used], sems.at[used])
                pl.when(scalars[0] == (b ^ 3 if i else b))(copy.start)
            loads.append(copy)
            used += 1
    sent = []
    used = 0
    for (group, many), out in zip(counts, outs):
        for i in range(many):
            loads[used].wait()
            for z in range(4):
                target = out.at[z, i] if many > 1 else out.at[z]
                copy = pltpu.make_async_copy(stage.at[used], target, out_sems.at[used * 4 + z])
                copy.start()
                sent.append(copy)
            used += 1
    for copy in sent:
        copy.wait()


def pick(scalars, shards, counts):
    rows = shards[0].shape[0]
    total = sum(many for _, many in counts)
    shapes = [((4,) if many == 1 else (4, many)) + (rows, D) for _, many in counts]
    return pl.pallas_call(
        functools.partial(pick_kernel, counts),
        out_shape=[jax.ShapeDtypeStruct(shape, jnp.bfloat16) for shape in shapes],
        in_specs=[pl.BlockSpec(memory_space=pltpu.SMEM)]
        + [pl.BlockSpec(memory_space=pltpu.HBM)] * len(shards),
        out_specs=[pl.BlockSpec(memory_space=pltpu.HBM)] * len(counts),
        scratch_shapes=[
            pltpu.VMEM((total, rows, D), jnp.bfloat16),
            pltpu.SemaphoreType.DMA((total,)),
            pltpu.SemaphoreType.DMA((total * 4,)),
        ],
        compiler_params=pltpu.CompilerParams(vmem_limit_bytes=63 << 20),
        cost_estimate=pl.CostEstimate(flops=2 << 26, bytes_accessed=2 << 16, transcendentals=0),
        name="pick",
    )(scalars, *shards)


def plain_grads_kernel(n, scalars, left, right, out, sems):
    out[...] = low(matmul_left_t(left[...], right[...]))


def memory_back_kernel(n, scalars, pack, *rest):
    refs, (memory_grad, scratch, sems) = rest[: n[0]], rest[n[0] :]
    group = Group(scalars, refs, scratch, sems, True, (2, 3))
    fetch(pack, group)
    group.wait_block(2)
    product = matmul_right_t(pack[:, :D], group.block(2))
    group.wait_block(3)
    memory_grad[...] = product + matmul_right_t(pack[:, D : 2 * D], group.block(3))


def token_back_kernel(n, scalars, grad_qkv, tokens, grad_first, gains, *rest):
    refs, (token_grad, grad_gain, scratch, sems) = rest[: n[0]], rest[n[0] :]
    group = Group(scalars, refs, scratch, sems, True, (0, 1, 2))
    fetch(grad_qkv, group, tokens, grad_first)
    group.wait_block(0)
    upstream = matmul_right_t(grad_qkv[:, :D], group.block(0))
    for b in range(1, 3):
        group.wait_block(b)
        upstream += matmul_right_t(grad_qkv[:, b * D : (b + 1) * D], group.block(b))
    part, grad_gain[...] = norm_grad(tokens[...].astype(jnp.float32), gains[0:1], upstream)
    token_grad[...] = grad_first[...] + part


def nbytes(shape, kind):
    total = jnp.dtype(kind).itemsize
    for size in shape:
        total *= size
    return total


class Moved:
    def __init__(self, outer, inner, sems, first, windows, is_input):
        self.inner, self.is_input = inner, is_input
        self.copies, self.flying, self.done = [], set(), set()
        for i, window in enumerate(windows):
            pair = (outer, inner)
            if window is not None:
                at = (pl.ds(window[0], window[1]), pl.ds(window[2], window[3]))
                pair = (outer.at[at], inner.at[at])
            self.copies.append(pltpu.make_async_copy(*(pair if is_input else pair[::-1]), sems.at[first + i]))

    def start(self, part=None):
        for i, copy in enumerate(self.copies):
            if part in (None, i) and i not in self.flying:
                copy.start()
                self.flying.add(i)

    def ready(self, part=None):
        if self.is_input:
            self.start()
            for i, copy in enumerate(self.copies):
                if part in (None, i) and i not in self.done:
                    copy.wait()
                    self.done.add(i)
        return self.inner

    def finish(self):
        self.start()
        for i, copy in enumerate(self.copies):
            if i not in self.done:
                copy.wait()

    @property
    def shape(self):
        return self.inner.shape

    @property
    def at(self):
        return self.ready().at

    def __getitem__(self, index):
        return self.ready()[index]

    def __setitem__(self, index, value):
        self.inner[index] = value


def fetch(*things):
    for thing in things:
        if isinstance(thing, (Moved, Group)):
            thing.start()


def send(*arrays):
    for array in arrays:
        if isinstance(array, Moved):
            array.start()


def send_part(part, *arrays):
    for array in arrays:
        if isinstance(array, Moved):
            array.start(part)


def inner_of(array):
    return array.inner if isinstance(array, Moved) else array


def ready(*arrays):
    for array in arrays:
        if isinstance(array, Moved):
            array.ready()


def ready_part(part, *arrays):
    for array in arrays:
        array.ready(part)


def column_blocks(shape):
    return [(0, shape[0], b * D, D) for b in range(shape[1] // D)]


def tiled(shape):
    return shape[-1] % 128 == 0 and shape[-2] % 16 == 0


def run(kernel, name, micros, scalars, arrays, groups, outs, scratch=(), direct=False, cut=None):
    n = tuple(len(group) for group in groups)
    outs, scratch = list(outs), list(scratch)
    windows = [pair[1] if isinstance(pair, tuple) else [None] for pair in arrays]
    arrays = [pair[0] if isinstance(pair, tuple) else pair for pair in arrays]
    ins = [(a.shape, a.dtype) for a in arrays]
    flat = [part for group in groups for part in group]
    moved = [pair for pair in (ins if direct else ins + outs) if tiled(pair[0])]
    rows = D // 8
    shape = (4, 2, 4, rows, D) if name in ("ffn_out", "ffn_back") else (4, 4, 2, rows, D)
    spaces = scratch + [(shape, jnp.bfloat16)] * len(groups)

    def body(scalar_ref, *refs):
        refs = list(refs)
        inputs, pieces = refs[: len(ins)], refs[len(ins) : len(ins) + len(flat)]
        results = refs[len(ins) + len(flat) :][: len(outs)]
        rest = refs[len(ins) + len(flat) + len(outs) :]
        copies, rest = rest[: len(moved)], rest[len(moved) :]
        if moved:
            sems, rest = rest[0], rest[1:]
        used, first = 0, 0
        for side, pairs in ((inputs, ins), (results, [] if direct else outs)):
            for i, (shape, _) in enumerate(pairs):
                if tiled(shape):
                    parts = windows[i] if side is inputs else (cut or {}).get(i, [None])
                    side[i] = Moved(side[i], copies[used], sems, first, parts, side is inputs)
                    used, first = used + 1, first + len(parts)
        kernel(n, scalar_ref, *inputs, *pieces, *results, *rest)
        for array in inputs + results:
            if isinstance(array, Moved):
                array.finish()

    def spec(shape):
        return pl.BlockSpec(memory_space=pltpu.HBM if tiled(shape) else pltpu.VMEM)

    return pl.pallas_call(
        body,
        out_shape=[jax.ShapeDtypeStruct(shape, kind) for shape, kind in outs],
        in_specs=[pl.BlockSpec(memory_space=pltpu.SMEM)]
        + [spec(shape) for shape, _ in ins]
        + [pl.BlockSpec(memory_space=pltpu.HBM)] * len(flat),
        out_specs=[spec(shape) for shape, _ in outs],
        scratch_shapes=[pltpu.VMEM(shape, kind) for shape, kind in moved]
        + ([pltpu.SemaphoreType.DMA((len(outs) * 4 + sum(map(len, windows)),))] if moved else [])
        + [pltpu.VMEM(shape, kind) for shape, kind in spaces]
        + [pltpu.SemaphoreType.DMA((32,)) for _ in (groups or [None])],
        compiler_params=pltpu.CompilerParams(vmem_limit_bytes=63 << 20),
        cost_estimate=pl.CostEstimate(
            flops=int(micros * 2e8), bytes_accessed=int(micros * 2e5), transcendentals=0
        ),
        name=name,
    )(scalars, *arrays, *flat)


def moves(step):
    pairs = []
    for y in range(2):
        for x in range(2):
            for z in range(4):
                for c in range(2):
                    ty, tx, tz, tc = step(y, x, z, c)
                    pairs.append((((y * 2 + x) * 4 + z) * 2 + c, ((ty * 2 + tx) * 4 + tz) * 2 + tc))
    return pairs


def swap_x(values):
    return lax.ppermute(values, BOTH, moves(lambda y, x, z, c: (y, 1 - x, z, c)))


def swap_y(values):
    return lax.ppermute(values, BOTH, moves(lambda y, x, z, c: (1 - y, x, z, c)))


def swap_core(values):
    return lax.ppermute(values, BOTH, moves(lambda y, x, z, c: (y, x, z, 1 - c)))


def turn_z(values, by):
    return lax.ppermute(values, BOTH, moves(lambda y, x, z, c: (y, x, (z + by) % 4, c)))


def after(value, *marks):
    return lax.optimization_barrier((value,) + marks)[0]


def first_swap(values):
    return lax.ppermute(
        values, BOTH, moves(lambda y, x, z, c: (y, 1 - x, z, c) if c == 0 else (1 - y, x, z, c))
    )


def second_swap(values):
    return lax.ppermute(
        values, BOTH, moves(lambda y, x, z, c: (1 - y, x, z, c) if c == 0 else (y, 1 - x, z, c))
    )


LINES = [[z * 2 + c for z in range(4)] for c in range(2)]


def spread_z(values):
    return lax.all_to_all(
        values, "fsdp", split_axis=0, concat_axis=0, tiled=True, axis_index_groups=LINES
    )


class Layer:
    def __init__(self, scalars, tokens, memory, cotangent, staged):
        self.scalars, self.tokens, self.memory, self.cotangent = scalars, tokens, memory, cotangent
        self.staged = staged
        self.t, self.m = tokens.shape[0], memory.shape[0]

    def hold(self, *marks):
        self.scalars = after(self.scalars, *marks)

    def adapters(self, generated):
        block, start = D * ADAPT, 3 * D
        self.gains = 1.0 + 0.25 * generated[:start].astype(jnp.float32).reshape(3, D)
        self.down_1 = generated[start : start + block].reshape(D, ADAPT)
        self.up_1 = generated[start + block : start + 2 * block].reshape(ADAPT, D)
        self.down_2 = generated[start + 2 * block : start + 3 * block].reshape(D, ADAPT)
        self.up_2 = generated[start + 3 * block : start + 4 * block].reshape(ADAPT, D)

    def rows(self, width=D, kind=jnp.bfloat16):
        return ((self.t, width), kind)

    def wide(self, width=D):
        return self.rows(width, jnp.float32)

    def halves(self, count):
        return [((count * (D // 2), self.t), jnp.bfloat16)] * 2

    def self_forward(self, w1):
        local = [self.rows(), self.rows()]
        outs = run(
            self_forward_kernel,
            "self_forward",
            11,
            self.scalars,
            [self.tokens, self.gains, self.down_1, self.up_1],
            [w1],
            [
                self.rows(3 * D),
                ((HEADS, self.t, self.t), jnp.bfloat16),
                self.rows(),
                self.wide(ADAPT),
                self.wide(),
                self.rows(),
            ]
            + (self.halves(2) if self.staged else local),
            scratch=(local if self.staged else []) + attend_spaces(self.t, self.t),
        )
        self.qkv, self.probs_1, self.branch_1, self.inner_1, self.first, self.normed_2 = outs[:6]
        self.saved_1 = outs[6:]

    def cross_forward(self, w2):
        local = [self.rows()]
        outs = run(
            cross_forward_kernel,
            "cross_forward",
            15,
            self.scalars,
            [self.normed_2, self.first, self.memory, self.gains],
            [w2],
            [
                self.rows(),
                ((self.m, 2 * D), jnp.bfloat16),
                ((HEADS, self.m, self.t), jnp.bfloat16),
                self.wide(),
                self.rows(),
            ]
            + (self.halves(4) if self.staged else local),
            scratch=(local if self.staged else []) + attend_spaces(self.m, self.t),
        )
        self.queries, self.memory_kv, self.probs_2, self.second, self.normed_3 = outs[:5]
        self.saved_2 = outs[5:]

    def ffn_in(self, w3):
        outs = run(
            ffn_in_kernel,
            "ffn_in",
            6,
            self.scalars,
            [self.normed_3],
            [w3],
            [self.rows(4 * D), self.rows(4 * D)] + (self.halves(5) if self.staged else []),
            cut={i: column_blocks((self.t, 4 * D)) for i in range(2)},
        )
        self.slope, self.hidden = outs[:2]
        self.saved_3 = outs[2:]

    def adapter_outs(self):
        return [((D, ADAPT), jnp.float32), ((ADAPT, D), jnp.float32)]

    def ffn_out(self, w4):
        self.mixed_out, self.grad_branch, self.grad_down_2, self.grad_up_2 = run(
            ffn_out_kernel,
            "ffn_out",
            8,
            self.scalars,
            [self.hidden, self.second, self.cotangent, self.down_2, self.up_2],
            [w4],
            [self.rows(), self.rows()] + self.adapter_outs(),
        )

    def ffn_back(self, w4):
        (self.grad_pre,) = run(
            ffn_back_kernel,
            "ffn_back",
            8,
            self.scalars,
            [self.grad_branch, self.slope],
            [w4],
            [self.rows(4 * D)],
        )

    def cross_back(self, w3, w2):
        self.grad_second, self.grad_gain_3, self.cross_pack = run(
            cross_back_kernel,
            "cross_back",
            15,
            self.scalars,
            [
                self.grad_pre,
                self.cotangent,
                self.second,
                self.gains,
                self.queries,
                self.memory_kv,
                self.probs_2,
            ],
            [w3, w2],
            [self.wide(), ((1, D), jnp.float32), ((self.m, 3 * D), jnp.bfloat16)],
            scratch=[self.rows()] + attend_spaces(self.m, self.t),
        )

    def self_back(self, w1, w2):
        self.grad_first, self.grad_gain_2, self.grad_down_1, self.grad_up_1, self.self_pack = run(
            self_back_kernel,
            "self_back",
            0.5,
            self.scalars,
            [
                (self.cross_pack, [(self.t, self.t, 2 * D, D)]),
                self.grad_second,
                self.first,
                self.gains,
                self.branch_1,
                self.inner_1,
                self.down_1,
                self.up_1,
                self.qkv,
                self.probs_1,
            ],
            [w1, w2],
            [self.wide(), ((1, D), jnp.float32)] + self.adapter_outs() + [self.rows(4 * D)],
            scratch=[self.rows()] + attend_spaces(self.t, self.t),
        )

    def token_back(self, w1):
        self.token_grad, self.grad_gain_1 = run(
            token_back_kernel,
            "token_back",
            5,
            self.scalars,
            [(self.self_pack, [(0, self.t, 0, 3 * D)]), self.tokens, self.grad_first, self.gains],
            [w1],
            [self.wide(), ((1, D), jnp.float32)],
        )

    def memory_back(self, w2):
        (self.memory_grad,) = run(
            memory_back_kernel,
            "memory_back",
            0.3,
            self.scalars,
            [(self.cross_pack, [(0, self.m, 0, 2 * D)])],
            [w2],
            [((self.m, D), jnp.float32)],
        )

    def block_grads(self, kernel, name, kept, got, grad, other, windows=None, rows=None):
        stage = ((4, 4, D // 8, D), jnp.bfloat16)
        part = ((2, 4, D // 8, D), jnp.bfloat16)
        if rows:
            kept, got = (kept, [rows + (0, self.t)]), (got, [rows + (0, self.t)])
        if windows:
            grad, other = (grad, windows), (other, windows)
        return run(
            kernel, name, 5, self.scalars, [kept, got, grad, other], [], [part, part], [stage], direct=True
        )

    def plain_grads(self, left, right):
        (out,) = run(
            plain_grads_kernel,
            "plain_grads",
            5,
            self.scalars,
            [left, right],
            [],
            [((left.shape[1], right.shape[1]), jnp.bfloat16)],
        )
        return out

    def grad_generated(self):
        return low(
            jnp.concatenate(
                [
                    0.25 * self.grad_gain_1,
                    0.25 * self.grad_gain_2,
                    0.25 * self.grad_gain_3,
                    self.grad_down_1.reshape(ADAPT, D),
                    self.grad_up_1,
                    self.grad_down_2.reshape(ADAPT, D),
                    self.grad_up_2,
                ]
            )
        ).reshape(-1)


def staged_layer(layer, where, task_ids, hidden_all, hyper_gen, shards):
    q, z, c = where[0], where[1], where[2]

    own_1, own_2, own_3, own_4 = pick(where, shards, [(1, 1), (2, 1), (3, 2), (4, 2)])
    column_1 = spread_z(own_1)
    ids = jnp.stack([task_ids, swap_core(task_ids)])
    ids_ahead = [ids] + [turn_z(ids, 4 - k) for k in (1, 2, 3)]
    gen_shard = low(matmul(hidden_all, hyper_gen))
    column_1 = after(column_1, *ids_ahead)
    near_x_1, near_y_1 = swap_x(column_1), swap_y(column_1)

    column_2 = spread_z(after(own_2, column_1))

    def pick_near(near_x, near_y, *marks):
        return jnp.where(c == 0, after(near_x, *marks), after(near_y, *marks))

    leaving_1 = pick_near(near_x_1, near_y_1)
    far_1 = second_swap(leaving_1)

    def rows_of(tasks):
        select = low(tasks[:, 0:1] == jnp.arange(TASKS, dtype=jnp.int32)[None, :])
        return after(low(matmul(select, gen_shard)), near_x_1, near_y_1, leaving_1, column_2)

    asked = [rows_of(tasks) for tasks in ids_ahead]
    turned = [turn_z(asked[k], k) for k in (1, 2, 3)]
    got = jnp.stack([asked[0]] + turned, axis=1)
    pieces = jnp.concatenate([got[0], swap_core(got[1])])
    slots = jnp.arange(8, dtype=jnp.int32)
    source = ((slots % 2) ^ c) * 4 + (z - slots // 2 + 4) % 4
    unturn = low(source[:, None] == slots[None, :])
    layer.adapters(low(matmul(unturn, pieces)).reshape(-1))

    w1 = [column_1, near_x_1, near_y_1, far_1]
    w1 += [swap_core(after(part, near_x_1)) for part in w1]

    def split(pair, *marks):
        return after(pair, *marks)[:, 0], pair[:, 1]

    def with_other(parts, *marks):
        return parts + [swap_core(after(part, *marks)) for part in parts]

    near_2 = [swap_x(column_2), swap_y(column_2)]
    pair_3 = spread_z(after(own_3, *turned))
    layer.hold(column_2)
    layer.self_forward(w1)
    leaving_2 = pick_near(*near_2, layer.normed_2)
    far_2 = second_swap(leaving_2)
    got_1 = swap_core(after(layer.saved_1[1], leaving_2))
    column_3, far_3 = split(pair_3, leaving_2)
    w2 = [column_2] + near_2 + [far_2]
    w2 += [swap_core(after(part, leaving_2)) for part in w2[:3]] + [swap_core(after(far_2, column_3))]
    near_3 = [swap_x(column_3), swap_y(column_3)]
    pair_4 = spread_z(after(own_4, column_3))
    layer.hold(got_1, column_3)
    layer.cross_forward(w2)
    layer.hold(layer.normed_3)
    w3 = with_other([column_3] + near_3 + [far_3], layer.normed_3, *near_3)
    got_2 = swap_core(after(layer.saved_2[1], *near_3))
    column_4, far_4 = split(pair_4, *near_3)
    layer.hold(got_2, column_4)
    layer.ffn_in(w3)
    near_4 = [swap_x(column_4), swap_y(column_4)]
    got_3 = swap_core(layer.saved_3[1])
    near = [swap_core(after(part, layer.hidden)) for part in near_4]
    w4 = [column_4] + near_4 + [far_4, swap_core(column_4)] + near + [swap_core(far_4)]
    layer.hold(got_3)
    layer.ffn_out(w4)

    def first_way(sums, *marks):
        home, away = sums
        return home, first_swap(after(away, *marks))

    def leaving(*sums):
        return combine("leaving", layer.scalars, [[(home, 1), (got, 1)] for home, got in sums])

    def staying(*sums):
        return combine("staying", layer.scalars, [[(home, 0), (got, 0), part] for home, got, part in sums])

    def grads(kernel, name, kept, got, grad, other):
        windows = column_blocks(grad.shape) if grad.shape[1] > D else None
        if kernel is cross_grads_kernel:
            windows = [windows[2]] + windows[:2]
        half = D // 2
        rows = {ffn_in_grad_kernel: (0, half), ffn_out_grad_kernel: (half, 4 * half)}.get(kernel)
        return layer.block_grads(kernel, name, kept, got, grad, other, windows, rows)

    other = swap_core(layer.grad_branch)
    layer.ffn_back(w4)
    other_pre = swap_core(after(layer.grad_pre, other))
    layer.hold(layer.grad_pre)
    g4 = grads(
        ffn_out_grad_kernel, "ffn_out_grad", layer.saved_3[0], got_3, layer.grad_branch, other
    )
    layer.hold(g4[0])
    g3 = grads(
        ffn_in_grad_kernel, "ffn_in_grad", layer.saved_3[0], got_3, layer.grad_pre, other_pre
    )
    s4, s3 = first_way(g4, g3[0]), first_way(g3)
    layer.hold(g3[0])
    layer.cross_back(w3, w2)
    layer.hold(layer.cross_pack)
    layer.self_back(w1, w2)
    other = swap_core(after(layer.cross_pack, layer.self_pack))
    layer.hold(layer.self_pack)
    t43 = leaving(s4, s3)
    q43 = second_swap(t43)
    other_self = swap_core(after(layer.self_pack, t43))
    layer.hold(t43)
    g2 = grads(
        cross_grads_kernel, "cross_grads", layer.saved_2[0], got_2, layer.cross_pack, other
    )
    s2 = first_way(g2)
    layer.hold(g2[0])
    g1 = grads(
        self_grads_kernel, "self_grads", layer.saved_1[0], got_1, layer.self_pack, other_self
    )
    s1 = first_way(g1)
    layer.hold(g1[0])
    layer.token_back(w1)
    layer.hold(layer.token_grad)
    u43 = staying(s4 + ((q43, (slice(None), 0)),), s3 + ((q43, (slice(None), 1)),))
    sent_43 = spread_z(u43)
    layer.hold(u43)
    t2 = leaving(s2)
    q2 = second_swap(t2)
    layer.hold(t2)
    layer.memory_back(w2)
    layer.hold(layer.memory_grad)
    t1 = leaving(s1)
    q1 = second_swap(t1)
    layer.hold(t1)
    u21 = staying(s2 + (q2,), s1 + (q1,))
    sent_21 = spread_z(after(u21, sent_43))
    own_4, own_3 = jnp.sum(after(sent_43, u21).astype(jnp.float32), axis=0)

    pieces = after(layer.grad_generated().reshape(4, 2, -1), u21, sent_43)
    mine = lax.dynamic_index_in_dim(pieces, c, 1, keepdims=False)
    theirs = lax.dynamic_index_in_dim(pieces, 1 - c, 1, keepdims=False)
    both = jnp.stack([mine, swap_core(theirs)], axis=1)
    both = lax.dynamic_slice_in_dim(jnp.concatenate([both, both]), z, 4, 0)
    terms = jnp.concatenate([both[0]] + [turn_z(both[k], k) for k in (1, 2, 3)])
    ids = jnp.concatenate([ids_ahead[(4 - k) % 4] for k in range(4)])[:, 0]
    select = low(jnp.arange(TASKS, dtype=jnp.int32)[:, None] == ids[None, :])
    task_grad = low(matmul(select, terms))
    task_grad = add_low(task_grad, swap_x(task_grad))
    task_grad = task_grad.astype(jnp.float32) + swap_y(task_grad).astype(jnp.float32)

    def sum_owners(part):
        part = part + swap_core(part)
        got = [part] + [turn_z(part, k) for k in (1, 2, 3)]
        return (got[0] + got[2]) + (got[1] + got[3])

    def share(owns):
        own = low(jnp.stack(owns))
        pair = jnp.stack([own, first_swap(own)])
        quad = jnp.concatenate([pair, second_swap(pair)])
        slots = [jnp.where(c == 0, q ^ b, ((q ^ b) % 2) * 2 + (q ^ b) // 2) for b in range(4)]
        return [
            [lax.dynamic_index_in_dim(quad, at, 0, keepdims=False)[i].astype(jnp.float32) for at in slots]
            for i in range(len(owns))
        ]

    own_2, own_1 = jnp.sum(sent_21.astype(jnp.float32), axis=0)
    g3, g4 = share([own_3, own_4])
    g2, g1 = share([own_2, own_1])
    summed = (
        jnp.concatenate(g1[:3], axis=1),
        g1[3],
        g2[0],
        jnp.concatenate(g2[2:], axis=1),
        g2[1],
        jnp.concatenate(g3, axis=1),
        jnp.concatenate(g4, axis=0),
    )
    return summed, task_grad, sum_owners


def plain_layer(layer, task_ids, hidden_all, hyper_gen, groups):
    owners = lax.axis_size("fsdp")

    def whole(shard):
        return lax.all_gather(shard, "fsdp", axis=0, tiled=True)

    w1, w2, w3 = (
        [jnp.concatenate([whole(block) for block in blocks]).reshape(4, 4, 2, D // 8, D)] for blocks in groups[:3]
    )
    w4 = [whole(jnp.concatenate(groups[3])).reshape(4, 2, 4, D // 8, D)]
    select = low(task_ids[:, None] == jnp.arange(TASKS, dtype=jnp.int32)[None, :])
    gen_shard = low(matmul(hidden_all, hyper_gen))
    gen_tasks = lax.all_gather(gen_shard, "fsdp", axis=1, tiled=True)
    layer.adapters(low(matmul(select, gen_tasks)[0]))
    layer.self_forward(w1)
    layer.cross_forward(w2)
    layer.ffn_in(w3)
    layer.ffn_out(w4)
    layer.ffn_back(w4)
    layer.cross_back(w3, w2)
    layer.self_back(w1, w2)
    layer.token_back(w1)
    layer.memory_back(w2)

    def owned(left, right):
        part = low(lax.psum_scatter(layer.plain_grads(left, right), "fsdp", scatter_dimension=0, tiled=True))
        return lax.psum(part, "dp").astype(jnp.float32)

    t = layer.t
    pack = layer.cross_pack
    summed = (
        owned(layer.saved_1[0], layer.self_pack[:, : 3 * D]),
        owned(layer.saved_1[1], layer.self_pack[:, 3 * D :]),
        owned(layer.normed_2, pack[t : 2 * t, 2 * D :]),
        owned(layer.memory, pack[:, : 2 * D]),
        owned(layer.saved_2[0], pack[:t, 2 * D :]),
        owned(layer.normed_3, layer.grad_pre),
        owned(layer.hidden, layer.grad_branch),
    )
    pieces = layer.grad_generated().reshape(owners, 1, -1)
    select = low(jnp.arange(TASKS, dtype=jnp.int32)[:, None] == task_ids[None, :])
    terms = low(select[None].astype(jnp.float32) * pieces.astype(jnp.float32))
    terms = lax.all_to_all(terms, "fsdp", split_axis=0, concat_axis=0, tiled=True)
    task_grad = low(jnp.sum(terms.astype(jnp.float32), axis=0))
    task_grad = lax.psum(task_grad, "dp").astype(jnp.float32)
    return summed, task_grad, lambda part: lax.psum(part, "fsdp")


def hyper_tail(task_grad, pre_all, hidden_all, task_table, hyper_in, hyper_gen, sum_owners):
    grad_hyper_gen = jnp.dot(
        hidden_all.astype(jnp.float32).T, task_grad, precision=lax.Precision.HIGHEST
    )
    grad_hidden = jnp.dot(
        task_grad, hyper_gen.astype(jnp.float32).T, precision=lax.Precision.HIGHEST
    )
    grad_pre_all = gelu_slope(pre_all) * sum_owners(grad_hidden)
    grad_table = jnp.dot(grad_pre_all, hyper_in.T, precision=lax.Precision.HIGHEST)
    grad_first = jnp.dot(task_table.T, grad_pre_all, precision=lax.Precision.HIGHEST)
    return grad_table, grad_first, grad_hyper_gen


def shards(
    tokens,
    memory,
    target_lengths,
    memory_lengths,
    task_ids,
    cotangent,
    self_qkv,
    self_out,
    cross_q,
    cross_kv,
    cross_out,
    ffn_in,
    ffn_out,
    task_table,
    hyper_in,
    hyper_gen,
):
    staged = lax.axis_size("fsdp") == 8 and lax.axis_size("dp") == 4
    pre_all = jnp.dot(task_table, hyper_in, precision=lax.Precision.HIGHEST)
    hidden_all = low(jax.nn.gelu(pre_all))

    def columns(shard):
        return [shard[:, b * D : (b + 1) * D] for b in range(shard.shape[1] // D)]

    q = lax.axis_index("dp").astype(jnp.int32)
    f = lax.axis_index("fsdp").astype(jnp.int32)
    where = jnp.stack([q, f // 2, f % 2])
    scalars = jnp.concatenate([where, target_lengths, memory_lengths])
    layer = Layer(scalars, tokens, memory, cotangent, staged)
    if staged:
        summed, task_grad, sum_owners = staged_layer(
            layer,
            where,
            task_ids,
            hidden_all,
            hyper_gen,
            (self_qkv, self_out, cross_q, cross_kv, cross_out, ffn_in, ffn_out),
        )
    else:
        rows = self_qkv.shape[0]
        groups = (
            columns(self_qkv) + [self_out],
            [cross_q, cross_out] + columns(cross_kv),
            columns(ffn_in),
            [ffn_out[b * rows : (b + 1) * rows] for b in range(4)],
        )
        summed, task_grad, sum_owners = plain_layer(layer, task_ids, hidden_all, hyper_gen, groups)
    grad_table, grad_first, grad_hyper_gen = hyper_tail(
        task_grad, pre_all, hidden_all, task_table, hyper_in, hyper_gen, sum_owners
    )
    return (
        (layer.mixed_out, layer.token_grad, layer.memory_grad)
        + summed
        + (grad_table, grad_first, grad_hyper_gen)
    )


def solution(mesh):
    by_both = P(("dp", "fsdp"), None)
    by_rows = P("fsdp", None)
    return jax.shard_map(
        shards,
        mesh=mesh,
        in_specs=(by_both, by_both)
        + (P(("dp", "fsdp")),) * 3
        + (by_both,)
        + (by_rows,) * 7
        + (P(), P(), P(None, "fsdp")),
        out_specs=(by_both,) * 3 + (by_rows,) * 7 + (P(), P(), P(None, "fsdp")),
        check_vma=False,
    )
```
